512 devices in a mesh: grp: 32 (over x, z), vocab: 16 (over y, core).
Axes of the slice: x: 4, y: 8, z: 8, core: 2. Of those that a mesh axis runs over, the one named last changes fastest.
Arguments:
- teacher_rows: bfloat16 [64, 8, 4096], P('grp', None, 'vocab'), may hold values from -160 to 160
- student_rows: bfloat16 [32, 8, 5120], P('grp', None, 'vocab'), may hold values from -160 to 160
- teacher_head: bfloat16 [4096, 131072], P(None, ('grp', 'vocab')), may hold values from -0.25 to 0.25
- student_head: bfloat16 [5120, 131072], P(None, ('grp', 'vocab')), may hold values from -0.25 to 0.25
- lengths: int32 [64], replicated, may hold values from 1 to 7, as said below
- owner: int32 [64], replicated, may hold values from 0 to 31, as said below
Outputs:
- divergence: float32 [32, 8], P('grp')
- grad_student: bfloat16 [32, 8, 5120], P('grp', None, 'vocab')
The draws below stay inside these ranges and needn't reach their ends.
Inputs may be any that keep to these rules, and one draw needn't show every extreme that they name: All 2 sequences of one teacher group share one owner, and each student group owns the sequences of exactly one teacher group. The lengths of the 2 sequences of one teacher group sum to at most 8, and to exactly 8 for some group.
All inputs are finite; a program needn't handle non-finite values.
Results may differ from the reference program's by a relative error of at most 0.018.
Values may be sent and summed in bfloat16 or wider, within the bound.
No kernel may reach another device: no remote copies, remote signals or barrier semaphores. Data moves between devices by JAX's collectives and lax.ppermute only.
A program may use at most 64 MiB of HBM per device.

```python
import jax
import jax.numpy as jnp
from jax import lax

DT = 4096
DS = 5120
VOC_DEV = 256
LMAX = 8
ROWS = 256
VOCAB = 131072
PAD = 8
SEQ_TEA = 2
SEQS = 64
N_GRP = 32
N_VOCAB = 16


def plan_groups(key):
    count = N_GRP
    seq_count = SEQ_TEA
    base_key = jax.random.fold_in(key, 7001)
    perm_key, level_key, star_key, unit_key = jax.random.split(base_key, 4)
    teacher_owner = jax.random.permutation(perm_key, count).astype(jnp.int32)
    owners = jnp.repeat(teacher_owner, seq_count)
    levels = jax.random.randint(level_key, (count,), 0, 65)
    totals = seq_count + (PAD - seq_count) * levels * levels // 4096
    starred = jax.random.randint(star_key, (), 0, count)
    marked_flag = jnp.arange(count) == starred
    totals = jnp.where(marked_flag, PAD, totals)
    extra = totals - seq_count
    unit_rows = LMAX - 1
    width = seq_count * unit_rows
    column_span = jnp.arange(width)
    score_values = jax.random.randint(unit_key, (count, width), 0, 1 << 16) * width + column_span[None, :]
    extra_reward = jnp.where(marked_flag[:, None] & (column_span[None, :] < unit_rows), 1 << 30, 0)
    score_values = score_values - extra_reward
    ranked = jnp.argsort(jnp.argsort(score_values, axis=1), axis=1)
    chosen = (ranked < extra[:, None]).astype(jnp.int32)
    seq_len = 1 + jnp.sum(chosen.reshape(count, seq_count, unit_rows), axis=2)
    return (owners.astype(jnp.int32), seq_len.reshape(-1).astype(jnp.int32))


def draw_lengths(key, part):
    return plan_groups(key)[1]


def draw_owner(key, part):
    return plan_groups(key)[0]


def hidden_values(key, shape):
    value_key = jax.random.fold_in(key, 0)
    values = jax.random.truncated_normal(value_key, -4.0, 4.0, shape, jnp.float32)
    return values


def draw_teacher_rows(key, part):
    return hidden_values(jax.random.fold_in(key, 311), (SEQS, LMAX, DT)).astype(jnp.bfloat16)


def draw_student_rows(key, part):
    return hidden_values(jax.random.fold_in(key, 523), (N_GRP, PAD, DS)).astype(jnp.bfloat16)


def block_scale(rng, extent, cuts, low, top_value):
    factor_of, own = 1.0, jax.random.fold_in(rng, 6)
    for position, blocks in cuts:
        draws = jnp.exp(jax.random.uniform(jax.random.fold_in(own, position), (blocks,), jnp.float32, low / len(cuts), top_value / len(cuts)))
        factor_of = factor_of * jnp.repeat(draws, extent[position] // blocks).reshape([-1 if axis == position else 1 for axis in range(len(extent))])
    return factor_of


def scatter_about(own_key, shape, scale, reach, cuts=(), kind=jnp.bfloat16):
    loudness = block_scale(own_key, shape, cuts, -0.22, 0.18) if cuts else 1.0
    values = jax.random.normal(own_key, shape, jnp.float32) * scale * loudness
    return jnp.minimum(jnp.maximum(values, -reach), reach).astype(kind)


def setup_inputs(seed: int = 0) -> dict:
    keys = jax.random.split(jax.random.key(seed), 7)
    return {
        "teacher_rows": draw_teacher_rows(jax.random.fold_in(keys[6], 71), 0),
        "student_rows": draw_student_rows(jax.random.fold_in(keys[6], 71), 0),
        "teacher_head": scatter_about(keys[2], (DT, VOCAB), (DT // 9) ** -0.5, 0.25, ((1, 512),)),
        "student_head": scatter_about(keys[3], (DS, VOCAB), (DS // 9) ** -0.5, 0.25, ((1, 512),)),
        "lengths": draw_lengths(jax.random.fold_in(keys[6], 71), 0),
        "owner": draw_owner(jax.random.fold_in(keys[6], 71), 0),
    }


def routing_tables(lengths, owner, groups, seq_count, positions, pad_rows):
    slot_count = seq_count * positions
    group_ids = jnp.arange(groups, dtype=jnp.int32)
    length_table = lengths.reshape(groups, seq_count)
    owner_table = owner.reshape(groups, seq_count)[:, 0]
    teacher_of = jnp.sum((owner_table[None, :] == group_ids[:, None]).astype(jnp.int32) * group_ids[None, :], axis=1).astype(jnp.int32)
    position_ids = jnp.arange(positions, dtype=jnp.int32)
    live_slots = (position_ids[None, None, :] < length_table[:, :, None]).reshape(groups, slot_count)
    ranked = jnp.cumsum(live_slots.astype(jnp.int32), axis=1) - 1
    target = jnp.where(live_slots, ranked, pad_rows).astype(jnp.int32)
    matches = target[:, None, :] == jnp.arange(pad_rows, dtype=jnp.int32)[None, :, None]
    source = jnp.sum(matches.astype(jnp.int32) * jnp.arange(slot_count, dtype=jnp.int32)[None, None, :], axis=2).astype(jnp.int32)
    totals = jnp.sum(length_table, axis=1).astype(jnp.int32)
    owned_total = jnp.take(totals, teacher_of, axis=0)
    student_live = jnp.arange(pad_rows, dtype=jnp.int32)[None, :] < owned_total[:, None]
    return teacher_of, source, student_live


def log_softmax_rows(logits):
    highest = jnp.max(logits, axis=-1, keepdims=True)
    shifted = logits - highest
    return shifted - jnp.log(jnp.sum(jnp.exp(shifted), axis=-1, keepdims=True))


def reference(teacher_rows, student_rows, teacher_head, student_head, lengths, owner):
    groups = N_GRP
    slot_count = SEQ_TEA * LMAX
    teacher_of, source, student_live = routing_tables(lengths, owner, groups, SEQ_TEA, LMAX, PAD)
    row_position = (teacher_of[:, None] * slot_count + jnp.take(source, teacher_of, axis=0)).reshape(ROWS).astype(jnp.int32)
    arrived = jnp.take(teacher_rows.reshape(groups * slot_count, DT), row_position, axis=0)
    student_block = student_rows.reshape(ROWS, DS)
    teacher_logits = jnp.dot(arrived, teacher_head, preferred_element_type=jnp.float32)
    student_logits = jnp.dot(student_block, student_head, preferred_element_type=jnp.float32)
    log_p = log_softmax_rows(teacher_logits)
    log_q = log_softmax_rows(student_logits)
    student_prob = jnp.exp(log_q)
    log_ratio = log_q - log_p
    weight = student_live.reshape(ROWS).astype(jnp.float32)
    kl_rows = jnp.sum(student_prob * log_ratio, axis=-1) * weight
    grad_logits = (weight[:, None] * student_prob * (log_ratio - kl_rows[:, None])).astype(jnp.bfloat16)

    def add_block(shard, running):
        offset = (shard * VOC_DEV).astype(jnp.int32)
        grad_block = lax.dynamic_slice_in_dim(grad_logits, offset, VOC_DEV, 1)
        head_block = lax.dynamic_slice_in_dim(student_head, offset, VOC_DEV, 1)
        partial_value = jnp.dot(grad_block, head_block.T, preferred_element_type=jnp.float32)
        rounded = lax.optimization_barrier(partial_value.astype(jnp.bfloat16))
        return running + rounded.astype(jnp.float32)

    summed = lax.fori_loop(0, N_GRP * N_VOCAB, add_block, jnp.zeros((ROWS, DS), jnp.float32))
    divergence = kl_rows.reshape(groups, PAD)
    grad_student = summed.astype(jnp.bfloat16).reshape(groups, PAD, DS)
    return divergence, grad_student
```

```python
import functools

import jax
import jax.numpy as jnp
from jax import lax
from jax.experimental import pallas as pl
from jax.experimental.pallas import tpu as pltpu
from jax.sharding import Mesh
from jax.sharding import PartitionSpec as P

GRP = ("x", "z")
VOCAB = ("y", "c")
OWNER = ("x", "z", "c")
CAPACITIES = (256,)
F32 = jnp.float32
BF16 = jnp.bfloat16
VMEM = pl.BlockSpec(memory_space=pltpu.VMEM)
SMEM = pl.BlockSpec(memory_space=pltpu.SMEM)
PARAMS = pltpu.CompilerParams(vmem_limit_bytes=48 * 1024 * 1024)


def iota(shape, dim):
    return lax.broadcasted_iota(jnp.int32, shape, dim)


def exchange(pieces, axes):
    return lax.all_to_all(pieces, axes, 0, 0, tiled=True)


def arrange_kernel(group_ref, lengths_ref, teacher_ref, student_ref, out_ref):
    count, pad, _ = out_ref.shape
    width = teacher_ref.shape[2]
    first = lengths_ref[2 * group_ref[0]]
    upper = teacher_ref[0].astype(F32)
    lower = pltpu.roll(teacher_ref[1].astype(F32), first, 0)
    chosen = jnp.where(iota(upper.shape, 0) < first, upper, lower).astype(BF16)
    for k in range(count):
        out_ref[k, :, :width] = chosen
        out_ref[k, :, width:] = student_ref[0]


def arrange(group, lengths, teacher_rows, student_rows, count):
    pad = student_rows.shape[1]
    width = teacher_rows.shape[2] + student_rows.shape[2]
    return pl.pallas_call(
        arrange_kernel,
        out_shape=jax.ShapeDtypeStruct((count, pad, width), BF16),
        in_specs=[SMEM, SMEM, VMEM, VMEM],
        out_specs=VMEM,
    )(group, lengths, teacher_rows, student_rows)


def logits_kernel(teacher_width, rows_ref, teacher_ref, student_ref, t_ref, s_ref):
    @pl.when(pl.program_id(0) == 0)
    def _():
        t_ref[...] = jnp.zeros_like(t_ref)
        s_ref[...] = jnp.zeros_like(s_ref)

    student_width = rows_ref.shape[2] - teacher_width
    t, s = t_ref[...], s_ref[...]
    for k in range(rows_ref.shape[0]):
        t += jnp.dot(
            rows_ref[k, :, :teacher_width],
            teacher_ref[k * teacher_width : (k + 1) * teacher_width, :],
            preferred_element_type=F32,
        )
        s += jnp.dot(
            rows_ref[k, :, teacher_width:],
            student_ref[k * student_width : (k + 1) * student_width, :],
            preferred_element_type=F32,
        )
    t_ref[...] = t
    s_ref[...] = s


def logits(rows, teacher_head, student_head, teacher_width):
    count, slots, width = rows.shape
    steps = 4
    vocab = teacher_head.shape[1]
    return pl.pallas_call(
        functools.partial(logits_kernel, teacher_width),
        grid=(steps,),
        out_shape=[jax.ShapeDtypeStruct((slots, vocab), F32)] * 2,
        in_specs=[
            pl.BlockSpec((count // steps, slots, width), lambda i: (i, 0, 0)),
            pl.BlockSpec((teacher_head.shape[0] // steps, vocab), lambda i: (i, 0)),
            pl.BlockSpec((student_head.shape[0] // steps, vocab), lambda i: (i, 0)),
        ],
        out_specs=[pl.BlockSpec((slots, vocab), lambda i: (0, 0))] * 2,
        compiler_params=PARAMS,
    )(rows, teacher_head, student_head)


def local_kernel(t_ref, s_ref, t_place_ref, s_place_ref, logit_ref, gap_ref, stat_ref):
    lanes = logit_ref.shape[0]
    place = iota((lanes, t_ref.shape[0]), 0)

    def packed(place_ref, ref):
        pick = (place == place_ref[...]).astype(F32)
        return jnp.dot(
            pick, ref[...], preferred_element_type=F32, precision=lax.Precision.HIGHEST
        )

    t = packed(t_place_ref, t_ref)
    s = packed(s_place_ref, s_ref)
    gap = s - t
    t_top = jnp.max(t, axis=1, keepdims=True)
    t_lse = t_top + jnp.log(jnp.sum(jnp.exp(t - t_top), axis=1, keepdims=True))
    s_top = jnp.max(s, axis=1, keepdims=True)
    e = jnp.exp(s - s_top)
    total = jnp.sum(e, axis=1, keepdims=True)
    weighted = jnp.sum(e * gap, axis=1, keepdims=True)
    logit_ref[...] = s
    gap_ref[...] = gap
    lane = iota((lanes, 128), 1)
    table = jnp.where(
        lane == 0,
        s_top,
        jnp.where(lane == 1, total, jnp.where(lane == 2, weighted, t_lse)),
    )
    table = table.T[:4]
    for k in range(stat_ref.shape[0]):
        stat_ref[k] = table


def local(t, s, t_place, s_place, lanes, count):
    return pl.pallas_call(
        local_kernel,
        out_shape=[
            jax.ShapeDtypeStruct((lanes, t.shape[1]), F32),
            jax.ShapeDtypeStruct((lanes, t.shape[1]), F32),
            jax.ShapeDtypeStruct((count, 4, lanes), F32),
        ],
        in_specs=[VMEM] * 4,
        out_specs=[VMEM] * 3,
        compiler_params=PARAMS,
    )(t, s, t_place, s_place)


def merged(stat_ref):
    top = stat_ref[:, 0, :]
    high = jnp.max(top, axis=0, keepdims=True)
    scale = jnp.exp(top - high)
    total = jnp.sum(scale * stat_ref[:, 1, :], axis=0, keepdims=True)
    weighted = jnp.sum(scale * stat_ref[:, 2, :], axis=0, keepdims=True)
    t_lse = stat_ref[:, 3, :]
    t_high = jnp.max(t_lse, axis=0, keepdims=True)
    t_lse = t_high + jnp.log(jnp.sum(jnp.exp(t_lse - t_high), axis=0, keepdims=True))
    return high, total, weighted, t_lse


def merge_kernel(stat_ref, out_ref):
    high, total, weighted, t_lse = merged(stat_ref)
    table = jnp.concatenate([high, total, weighted, t_lse], axis=0)
    for k in range(out_ref.shape[0]):
        out_ref[k] = table


def merge(stat, count):
    return pl.pallas_call(
        merge_kernel,
        out_shape=jax.ShapeDtypeStruct((count, *stat.shape[1:]), F32),
        in_specs=[VMEM],
        out_specs=VMEM,
    )(stat)


def gradient_kernel(
    core_ref, stat_ref, logit_ref, gap_ref, head_ref, keep_ref, send_ref, kl_ref, g_ref
):
    @pl.when(pl.program_id(0) == 0)
    def _():
        high, total, weighted, t_lse = merged(stat_ref)
        lanes = high.shape[1]
        mean = weighted / total
        kl_ref[...] = mean - (high + jnp.log(total)) + t_lse
        row = iota((128, lanes), 0)
        table = jnp.where(row == 0, high, jnp.where(row == 1, 1.0 / total, mean)).T
        q = jnp.exp(logit_ref[...] - table[:, 0:1]) * table[:, 1:2]
        g = q * (gap_ref[...] - table[:, 2:3])
        g_ref[...] = g[: g_ref.shape[0]].astype(BF16)

    width = keep_ref.shape[2]
    half = keep_ref.shape[1]
    low = core_ref[0] == 0
    for k in range(keep_ref.shape[0]):
        part = lax.dot_general(
            g_ref[...],
            head_ref[k * width : (k + 1) * width, :],
            (((1,), (1,)), ((), ())),
            preferred_element_type=F32,
        ).astype(BF16)
        keep_ref[k] = jnp.where(low, part[:half], part[half:])
        send_ref[k] = jnp.where(low, part[half:], part[:half])


def gradient(core, stat, logit, gap, head, rows, count):
    steps = 4
    width = head.shape[0] // count
    part = jax.ShapeDtypeStruct((count, rows // 2, width), BF16)
    block = pl.BlockSpec((count // steps, rows // 2, width), lambda i: (i, 0, 0))
    whole = lambda a: pl.BlockSpec(a.shape, lambda i: (0,) * a.ndim)
    return pl.pallas_call(
        gradient_kernel,
        grid=(steps,),
        out_shape=[part, part, jax.ShapeDtypeStruct((1, logit.shape[0]), F32)],
        in_specs=[
            SMEM,
            whole(stat),
            whole(logit),
            whole(gap),
            pl.BlockSpec((head.shape[0] // steps, head.shape[1]), lambda i: (i, 0)),
        ],
        out_specs=[block, block, pl.BlockSpec((1, logit.shape[0]), lambda i: (0, 0))],
        scratch_shapes=[pltpu.VMEM((rows, head.shape[1]), BF16)],
        compiler_params=PARAMS,
    )(core, stat, logit, gap, head)


def spread_kernel(core_ref, part_ref, place_ref, out_ref):
    count, pad, width = out_ref.shape
    rows = part_ref.shape[1]
    total = part_ref[0].astype(F32)
    for k in range(1, part_ref.shape[0]):
        total += part_ref[k].astype(F32)
    total = total.astype(BF16)
    slots = place_ref.shape[0]
    target = iota((slots, rows), 1) + core_ref[0] * rows
    pick = (place_ref[...] == target).astype(F32).astype(BF16)
    for c in range(2):
        found = jnp.dot(
            pick, total[:, c * width : (c + 1) * width], preferred_element_type=F32
        )
        found = found.astype(BF16).reshape(count // 2, pad, width)
        for k in range(count // 2):
            out_ref[2 * k + c] = found[k]


def spread(core, parts, place, pad):
    slots = place.shape[0]
    return pl.pallas_call(
        spread_kernel,
        out_shape=jax.ShapeDtypeStruct(
            (2 * slots // pad, pad, parts.shape[2] // 2), BF16
        ),
        in_specs=[SMEM, VMEM, VMEM],
        out_specs=VMEM,
        compiler_params=PARAMS,
    )(core, parts, place)


def tail(rows, pad, operands):
    core, t, s, t_place, s_place, s_column, student_head = operands
    lanes = -(-rows // 128) * 128
    ring = lax.axis_size("y")
    logit, gap, stat = local(t, s, t_place, s_place, lanes, lax.axis_size(VOCAB))
    stat = merge(exchange(stat, VOCAB), lax.axis_size(GRP))
    stat = exchange(stat, GRP)
    keep, send, kl = gradient(core, stat, logit, gap, student_head, rows, ring)
    came = lax.ppermute(send, "c", ((0, 1), (1, 0)))
    both = (keep.astype(F32) + came.astype(F32)).astype(BF16)
    pieces = spread(core, exchange(both, "y"), s_column, pad)
    pieces = exchange(pieces, OWNER)
    grad = jnp.sum(pieces.astype(F32), axis=0).astype(BF16)
    kl = jnp.pad(kl[0], (0, t.shape[0] + pad - lanes))
    return kl, grad


def routing(lengths, owner, groups, pad):
    totals = jnp.sum(lengths.reshape(groups, -1), axis=1)
    owners = owner.reshape(groups, -1)[:, 0]
    ids = jnp.arange(groups, dtype=jnp.int32)
    step = jnp.arange(pad, dtype=jnp.int32)
    t_start = jnp.sum(jnp.where(owners[None, :] < owners[:, None], totals[None, :], 0), axis=1)
    s_start = jnp.sum(jnp.where(owners[None, :] < ids[:, None], totals[None, :], 0), axis=1)
    s_total = jnp.sum(jnp.where(owners[None, :] == ids[:, None], totals[None, :], 0), axis=1)

    def places(start, total):
        return jnp.where(step[None, :] < total[:, None], start[:, None] + step[None, :], -1)

    return places(t_start, totals), places(s_start, s_total), jnp.sum(totals)


def per_device(teacher_rows, student_rows, teacher_head, student_head, lengths, owner):
    groups = lax.axis_size(GRP)
    pad = student_rows.shape[1]
    group = lax.axis_index(GRP).astype(jnp.int32)
    core = lax.axis_index("c").astype(jnp.int32).reshape(1)
    teacher_width = teacher_rows.shape[2]
    mine = arrange(group.reshape(1), lengths, teacher_rows, student_rows, groups)
    rows = exchange(mine, GRP).reshape(groups * pad, mine.shape[2])
    rows = lax.all_gather(rows, VOCAB)
    t_place, s_place, live = routing(lengths, owner, groups, pad)
    t, s = logits(rows, teacher_head, student_head, teacher_width)
    operands = (
        core,
        t,
        s,
        t_place.reshape(1, -1),
        s_place.reshape(1, -1),
        s_place.reshape(-1, 1),
        student_head,
    )
    branches = [functools.partial(tail, c, pad) for c in CAPACITIES]
    which = sum((live > c).astype(jnp.int32) for c in CAPACITIES[:-1])
    kl, grad = lax.switch(which, branches, operands) if len(branches) > 1 else branches[0](operands)
    own = lax.dynamic_index_in_dim(s_place, group, 0, keepdims=False)
    found = lax.dynamic_slice_in_dim(kl, jnp.maximum(own[0], 0), pad, 0)
    divergence = jnp.where(own >= 0, found, 0.0)
    return divergence.reshape(1, pad), grad.reshape(1, pad, grad.shape[1])


def solution(mesh):
    torus = Mesh(mesh.devices.reshape(4, 8, 8, 2), ("x", "z", "y", "c"))
    return jax.shard_map(
        per_device,
        mesh=torus,
        in_specs=(
            P(GRP, None, VOCAB),
            P(GRP, None, VOCAB),
            P(None, (*GRP, *VOCAB)),
            P(None, (*GRP, *VOCAB)),
            P(),
            P(),
        ),
        out_specs=(P(GRP, None), P(GRP, None, VOCAB)),
        check_vma=False,
    )
```

```python
import functools

import jax
import jax.numpy as jnp
from jax import lax
from jax.experimental import pallas as pl
from jax.experimental.pallas import tpu as pltpu
from jax.sharding import Mesh
from jax.sharding import PartitionSpec as P

GRP = ("x", "z")
VOCAB = ("y", "c")
OWNER = ("x", "z", "c")
CAPACITIES = (128, 160, 256)
F32 = jnp.float32
BF16 = jnp.bfloat16
VMEM = pl.BlockSpec(memory_space=pltpu.VMEM)
SMEM = pl.BlockSpec(memory_space=pltpu.SMEM)
PARAMS = pltpu.CompilerParams(vmem_limit_bytes=20 * 1024 * 1024)


def iota(shape, dim):
    return lax.broadcasted_iota(jnp.int32, shape, dim)


def exchange(pieces, axes):
    return lax.all_to_all(pieces, axes, 0, 0, tiled=True)


def arrange_kernel(group_ref, lengths_ref, teacher_ref, student_ref, out_ref):
    count, pad, _ = out_ref.shape
    width = teacher_ref.shape[2]
    rest = out_ref.shape[2] - width - student_ref.shape[2]
    first = lengths_ref[2 * group_ref[0]]
    upper = teacher_ref[0].astype(F32)
    lower = pltpu.roll(teacher_ref[1].astype(F32), first, 0)
    chosen = jnp.where(iota(upper.shape, 0) < first, upper, lower).astype(BF16)
    for k in range(count):
        out_ref[k, :, :width] = chosen
        out_ref[k, :, width : width + student_ref.shape[2]] = student_ref[0]
        if rest:
            out_ref[k, :, -rest:] = jnp.zeros((pad, rest), BF16)


def arrange(group, lengths, teacher_rows, student_rows, count):
    pad = student_rows.shape[1]
    width = -(-(teacher_rows.shape[2] + student_rows.shape[2]) // 128) * 128
    return pl.pallas_call(
        arrange_kernel,
        out_shape=jax.ShapeDtypeStruct((count, pad, width), BF16),
        in_specs=[SMEM, SMEM, VMEM, VMEM],
        out_specs=VMEM,
    )(group, lengths, teacher_rows, student_rows)


def stage_kernel(teacher_ref, student_ref, t_out_ref, s_out_ref, sems):
    copies = [
        pltpu.make_async_copy(teacher_ref, t_out_ref, sems.at[0]),
        pltpu.make_async_copy(student_ref, s_out_ref, sems.at[1]),
    ]
    for copy in copies:
        copy.start()
    for copy in copies:
        copy.wait()


def stage(teacher_head, student_head):
    size = 2 * (teacher_head.size + student_head.size)
    return pl.pallas_call(
        stage_kernel,
        out_shape=[
            jax.ShapeDtypeStruct(teacher_head.shape, BF16),
            jax.ShapeDtypeStruct(student_head.shape, BF16),
        ],
        in_specs=[pl.BlockSpec(memory_space=pl.ANY)] * 2,
        out_specs=[VMEM] * 2,
        scratch_shapes=[pltpu.SemaphoreType.DMA((2,))],
        compiler_params=PARAMS,
        cost_estimate=pl.CostEstimate(flops=0, bytes_accessed=2 * size, transcendentals=0),
    )(teacher_head, student_head)


def logits_step(teacher_width, steps, rows_ref, teacher_ref, student_ref, t_ref, s_ref):
    @pl.when(pl.program_id(0) == 0)
    def _():
        t_ref[...] = jnp.zeros_like(t_ref)
        s_ref[...] = jnp.zeros_like(s_ref)

    pieces = range(rows_ref.shape[0])
    student_width = student_ref.shape[0] // (steps * len(pieces))
    whole = student_width // 128 * 128
    end = teacher_width + whole
    stop = teacher_width + student_width
    step = pl.program_id(0)
    deep = len(pieces) * teacher_width
    first = pl.multiple_of(step * deep, deep)
    t_ref[...] += jnp.dot(
        jnp.concatenate([rows_ref[k, :, :teacher_width] for k in pieces], axis=1),
        teacher_ref[pl.ds(first, deep), :],
        preferred_element_type=F32,
    )
    base = step * len(pieces) * student_width

    def heads(k, start, count):
        return student_ref[pl.ds(pl.multiple_of(base + k * student_width + start, 64), count), :]

    s_ref[...] += jnp.dot(
        jnp.concatenate(
            [rows_ref[k, :, teacher_width:end] for k in pieces]
            + [rows_ref[k, :, end:stop] for k in pieces],
            axis=1,
        ),
        jnp.concatenate(
            [heads(k, 0, whole) for k in pieces]
            + [heads(k, whole, student_width - whole) for k in pieces],
            axis=0,
        ),
        preferred_element_type=F32,
    )


def logits(rows, teacher_head, student_head, teacher_width):
    count, slots, width = rows.shape
    steps = 4
    vocab = teacher_head.shape[1]
    return pl.pallas_call(
        functools.partial(logits_step, teacher_width, steps),
        grid=(steps,),
        out_shape=[jax.ShapeDtypeStruct((slots, vocab), F32)] * 2,
        in_specs=[
            pl.BlockSpec((count // steps, slots, width), lambda i: (i, 0, 0)),
            VMEM,
            VMEM,
        ],
        out_specs=[pl.BlockSpec((slots, vocab), lambda i: (0, 0))] * 2,
        compiler_params=pltpu.CompilerParams(vmem_limit_bytes=50 * 1024 * 1024),
    )(rows, teacher_head, student_head)


def local_kernel(t_ref, s_ref, t_place_ref, s_place_ref, logit_ref, gap_ref, stat_ref):
    lanes = logit_ref.shape[0]
    place = iota((lanes, t_ref.shape[0]), 0)

    def packed(place_ref, ref):
        pick = (place == place_ref[...]).astype(F32)
        return jnp.dot(
            pick, ref[...], preferred_element_type=F32, precision=lax.Precision.HIGHEST
        )

    t = packed(t_place_ref, t_ref)
    s = packed(s_place_ref, s_ref)
    gap = s - t
    t_top = jnp.max(t, axis=1, keepdims=True)
    t_lse = t_top + jnp.log(jnp.sum(jnp.exp(t - t_top), axis=1, keepdims=True))
    s_top = jnp.max(s, axis=1, keepdims=True)
    e = jnp.exp(s - s_top)
    total = jnp.sum(e, axis=1, keepdims=True)
    weighted = jnp.sum(e * gap, axis=1, keepdims=True)
    logit_ref[...] = s
    gap_ref[...] = gap
    lane = iota((lanes, 128), 1)
    table = jnp.where(
        lane == 0,
        s_top,
        jnp.where(lane == 1, total, jnp.where(lane == 2, weighted, t_lse)),
    )
    table = table.T[:4]
    for k in range(stat_ref.shape[0]):
        stat_ref[k] = table


def local(t, s, t_place, s_place, lanes, count):
    return pl.pallas_call(
        local_kernel,
        out_shape=[
            jax.ShapeDtypeStruct((lanes, t.shape[1]), F32),
            jax.ShapeDtypeStruct((lanes, t.shape[1]), F32),
            jax.ShapeDtypeStruct((count, 4, lanes), F32),
        ],
        in_specs=[VMEM] * 4,
        out_specs=[VMEM] * 3,
        compiler_params=PARAMS,
    )(t, s, t_place, s_place)


def merged(stat_ref):
    top = stat_ref[:, 0, :]
    high = jnp.max(top, axis=0, keepdims=True)
    scale = jnp.exp(top - high)
    total = jnp.sum(scale * stat_ref[:, 1, :], axis=0, keepdims=True)
    weighted = jnp.sum(scale * stat_ref[:, 2, :], axis=0, keepdims=True)
    t_lse = stat_ref[:, 3, :]
    t_high = jnp.max(t_lse, axis=0, keepdims=True)
    t_lse = t_high + jnp.log(jnp.sum(jnp.exp(t_lse - t_high), axis=0, keepdims=True))
    return high, total, weighted, t_lse


def merge_kernel(stat_ref, out_ref):
    high, total, weighted, t_lse = merged(stat_ref)
    table = jnp.concatenate([high, total, weighted, t_lse], axis=0)
    for k in range(out_ref.shape[0]):
        out_ref[k] = table


def merge(stat, count):
    return pl.pallas_call(
        merge_kernel,
        out_shape=jax.ShapeDtypeStruct((count, *stat.shape[1:]), F32),
        in_specs=[VMEM],
        out_specs=VMEM,
    )(stat)


def gradient_kernel(
    info_ref, stat_ref, logit_ref, gap_ref, head_ref, keep_ref, send_ref, kl_ref, g_ref
):
    @pl.when(pl.program_id(0) == 0)
    def _():
        high, total, weighted, t_lse = merged(stat_ref)
        lanes = high.shape[1]
        mean = weighted / total
        kl = jnp.broadcast_to(mean - (high + jnp.log(total)) + t_lse, (8, lanes))
        kl = pltpu.roll(kl, lax.rem(lanes - info_ref[2], lanes), 1)[:1, :128]
        kl_ref[...] = jnp.where(iota((1, 128), 1) < info_ref[3], kl, 0.0)
        row = iota((128, lanes), 0)
        table = jnp.where(row == 0, high, jnp.where(row == 1, 1.0 / total, mean)).T
        q = jnp.exp(logit_ref[...] - table[:, 0:1]) * table[:, 1:2]
        g = q * (gap_ref[...] - table[:, 2:3])
        g_ref[...] = g[: g_ref.shape[0]].astype(BF16)

    width = keep_ref.shape[2]
    half = keep_ref.shape[1]
    low = info_ref[1] == 0
    for k in range(keep_ref.shape[0]):
        part = lax.dot_general(
            g_ref[...],
            head_ref[k * width : (k + 1) * width, :],
            (((1,), (1,)), ((), ())),
            preferred_element_type=F32,
        ).astype(BF16)
        keep_ref[k] = jnp.where(low, part[:half], part[half:])
        send_ref[k] = jnp.where(low, part[half:], part[:half])


def gradient(info, stat, logit, gap, head, rows, count):
    steps = 4
    width = head.shape[0] // count
    part = jax.ShapeDtypeStruct((count, rows // 2, width), BF16)
    block = pl.BlockSpec((count // steps, rows // 2, width), lambda i: (i, 0, 0))
    whole = lambda a: pl.BlockSpec(a.shape, lambda i: (0,) * a.ndim)
    return pl.pallas_call(
        gradient_kernel,
        grid=(steps,),
        out_shape=[part, part, jax.ShapeDtypeStruct((1, 128), F32)],
        in_specs=[
            SMEM,
            whole(stat),
            whole(logit),
            whole(gap),
            pl.BlockSpec((head.shape[0] // steps, head.shape[1]), lambda i: (i, 0)),
        ],
        out_specs=[block, block, pl.BlockSpec((1, 128), lambda i: (0, 0))],
        scratch_shapes=[pltpu.VMEM((rows, head.shape[1]), BF16)],
        compiler_params=PARAMS,
    )(info, stat, logit, gap, head)


def spread_kernel(info_ref, part_ref, place_ref, out_ref):
    count, pad, width = out_ref.shape
    rows = part_ref.shape[1]
    total = part_ref[0].astype(F32)
    for k in range(1, part_ref.shape[0]):
        total += part_ref[k].astype(F32)
    total = total.astype(BF16)
    slots = place_ref.shape[0]
    target = iota((slots, rows), 1) + info_ref[1] * rows
    pick = (place_ref[:, :rows] == target).astype(F32).astype(BF16)
    for c in range(2):
        found = jnp.dot(
            pick, total[:, c * width : (c + 1) * width], preferred_element_type=F32
        )
        found = found.astype(BF16).reshape(count // 2, pad, width)
        for k in range(count // 2):
            out_ref[2 * k + c] = found[k]


def spread(info, parts, place, pad):
    slots = place.shape[0]
    return pl.pallas_call(
        spread_kernel,
        out_shape=jax.ShapeDtypeStruct(
            (2 * slots // pad, pad, parts.shape[2] // 2), BF16
        ),
        in_specs=[SMEM, VMEM, VMEM],
        out_specs=VMEM,
        compiler_params=PARAMS,
    )(info, parts, place)


def tail(rows, pad, operands):
    info, t, s, t_place, s_place, s_column, student_head = operands
    lanes = -(-rows // 128) * 128
    ring = lax.axis_size("y")
    logit, gap, stat = local(t, s, t_place, s_place, lanes, lax.axis_size(VOCAB))
    stat = merge(exchange(stat, VOCAB), lax.axis_size(GRP))
    stat = exchange(stat, GRP)
    keep, send, kl = gradient(info, stat, logit, gap, student_head, rows, ring)
    came = lax.ppermute(send, "c", ((0, 1), (1, 0)))
    both = (keep.astype(F32) + came.astype(F32)).astype(BF16)
    pieces = spread(info, exchange(both, "y"), s_column, pad)
    pieces = exchange(pieces, OWNER)
    grad = jnp.sum(pieces.astype(F32), axis=0).astype(BF16)
    return kl, grad


def routing_kernel(
    groups, pad, group_ref, core_ref, lengths_ref, owner_ref, t_ref, s_ref, column_ref, info_ref, start_ref
):
    share = lengths_ref.shape[0] // groups

    def total(g):
        return sum(lengths_ref[share * g + k] for k in range(share))

    def owned(j, found):
        g, count = found
        return lax.fori_loop(
            0,
            groups,
            lambda i, f: (
                jnp.where(owner_ref[share * i] == j, i, f[0]),
                jnp.where(owner_ref[share * i] == j, total(i), f[1]),
            ),
            (g, count),
        )

    lane = iota(t_ref.shape, 1)
    column = iota(column_ref.shape, 0)
    zero = jnp.int32(0)

    def place(j, carry):
        t, s, wide, start = carry
        g, count = owned(j, (zero, zero))
        s_step = lane - j * pad
        t_step = lane - g * pad
        down = column - j * pad
        t = jnp.where((t_step >= 0) & (t_step < count), start + t_step, t)
        s = jnp.where((s_step >= 0) & (s_step < count), start + s_step, s)
        wide = jnp.where((down >= 0) & (down < count), start + down, wide)
        start_ref[j] = start
        start_ref[groups + j] = count
        return t, s, wide, start + count

    none = jnp.full(t_ref.shape, -1, jnp.int32)
    t, s, wide, live = lax.fori_loop(
        0, groups, place, (none, none, jnp.full(column_ref.shape, -1, jnp.int32), zero)
    )
    t_ref[...] = t
    s_ref[...] = s
    column_ref[...] = wide
    which = zero
    for c in CAPACITIES[:-1]:
        which += (live > c).astype(jnp.int32)
    info_ref[0] = which
    info_ref[1] = core_ref[0]
    info_ref[2] = start_ref[group_ref[0]]
    info_ref[3] = start_ref[groups + group_ref[0]]


def routing(group, core, lengths, owner, groups, pad):
    slots = groups * pad
    return pl.pallas_call(
        functools.partial(routing_kernel, groups, pad),
        out_shape=[
            jax.ShapeDtypeStruct((1, slots), jnp.int32),
            jax.ShapeDtypeStruct((1, slots), jnp.int32),
            jax.ShapeDtypeStruct((slots, 128), jnp.int32),
            jax.ShapeDtypeStruct((4,), jnp.int32),
        ],
        in_specs=[SMEM] * 4,
        out_specs=[VMEM] * 3 + [SMEM],
        scratch_shapes=[pltpu.SMEM((2 * groups,), jnp.int32)],
        cost_estimate=pl.CostEstimate(flops=10**8, bytes_accessed=10**6, transcendentals=0),
    )(group, core, lengths, owner)


def per_device(teacher_rows, student_rows, teacher_head, student_head, lengths, owner):
    groups = lax.axis_size(GRP)
    pad = student_rows.shape[1]
    group = lax.axis_index(GRP).astype(jnp.int32).reshape(1)
    core = lax.axis_index("c").astype(jnp.int32).reshape(1)
    mine = arrange(group, lengths, teacher_rows, student_rows, groups)
    rows = exchange(mine, GRP).reshape(groups * pad, mine.shape[2])
    rows = lax.all_gather(rows, VOCAB, axis=0, tiled=True)
    rows = rows.reshape(-1, groups * pad, mine.shape[2])
    t_place, s_place, s_column, info = routing(group, core, lengths, owner, groups, pad)
    t_head, s_head = stage(teacher_head, student_head)
    t, s = logits(rows, t_head, s_head, teacher_rows.shape[2])
    operands = (info, t, s, t_place, s_place, s_column, student_head)
    branches = [functools.partial(tail, c, pad) for c in CAPACITIES]
    kl, grad = lax.switch(info[0], branches, operands)
    return kl[:, :pad], grad.reshape(1, pad, grad.shape[1])


def solution(mesh):
    torus = Mesh(mesh.devices.reshape(4, 8, 8, 2), ("x", "z", "y", "c"))
    return jax.shard_map(
        per_device,
        mesh=torus,
        in_specs=(
            P(GRP, None, VOCAB),
            P(GRP, None, VOCAB),
            P(None, (*GRP, *VOCAB)),
            P(None, (*GRP, *VOCAB)),
            P(),
            P(),
        ),
        out_specs=(P(GRP, None), P(GRP, None, VOCAB)),
        check_vma=False,
    )
```

```python
import functools

import jax
import jax.numpy as jnp
from jax import lax
from jax.experimental import pallas as pl
from jax.experimental.pallas import tpu as pltpu
from jax.sharding import Mesh
from jax.sharding import PartitionSpec as P

GRP = ("x", "z")
VOCAB = ("y", "c")
CAPACITIES = (128, 256)
F32 = jnp.float32
BF16 = jnp.bfloat16
VMEM = pl.BlockSpec(memory_space=pltpu.VMEM)
SMEM = pl.BlockSpec(memory_space=pltpu.SMEM)
PARAMS = pltpu.CompilerParams(vmem_limit_bytes=20 * 1024 * 1024)


def iota(shape, dim):
    return lax.broadcasted_iota(jnp.int32, shape, dim)


def exchange(pieces, axes):
    return lax.all_to_all(pieces, axes, 0, 0, tiled=True)


def arrange_kernel(group_ref, lengths_ref, teacher_ref, student_ref, out_ref):
    count, pad, _ = out_ref.shape
    width = teacher_ref.shape[2]
    rest = out_ref.shape[2] - width - student_ref.shape[2]
    first = lengths_ref[2 * group_ref[0]]
    upper = teacher_ref[0].astype(F32)
    lower = pltpu.roll(teacher_ref[1].astype(F32), first, 0)
    chosen = jnp.where(iota(upper.shape, 0) < first, upper, lower).astype(BF16)
    for k in range(count):
        out_ref[k, :, :width] = chosen
        out_ref[k, :, width : width + student_ref.shape[2]] = student_ref[0]
        if rest:
            out_ref[k, :, -rest:] = jnp.zeros((pad, rest), BF16)


def arrange(group, lengths, teacher_rows, student_rows, count):
    pad = student_rows.shape[1]
    width = -(-(teacher_rows.shape[2] + student_rows.shape[2]) // 128) * 128
    return pl.pallas_call(
        arrange_kernel,
        out_shape=jax.ShapeDtypeStruct((count, pad, width), BF16),
        in_specs=[SMEM, SMEM, VMEM, VMEM],
        out_specs=VMEM,
    )(group, lengths, teacher_rows, student_rows)


def stage_kernel(teacher_ref, student_ref, t_out_ref, s_out_ref, sems):
    copies = [
        pltpu.make_async_copy(teacher_ref, t_out_ref, sems.at[0]),
        pltpu.make_async_copy(student_ref, s_out_ref, sems.at[1]),
    ]
    for copy in copies:
        copy.start()
    for copy in copies:
        copy.wait()


def stage(teacher_head, student_head):
    size = 2 * (teacher_head.size + student_head.size)
    return pl.pallas_call(
        stage_kernel,
        out_shape=[
            jax.ShapeDtypeStruct(teacher_head.shape, BF16),
            jax.ShapeDtypeStruct(student_head.shape, BF16),
        ],
        in_specs=[pl.BlockSpec(memory_space=pl.ANY)] * 2,
        out_specs=[VMEM] * 2,
        scratch_shapes=[pltpu.SemaphoreType.DMA((2,))],
        compiler_params=PARAMS,
        cost_estimate=pl.CostEstimate(flops=0, bytes_accessed=2 * size, transcendentals=0),
    )(teacher_head, student_head)


def logits_step(teacher_width, steps, rows_ref, teacher_ref, student_ref, t_ref, s_ref):
    @pl.when(pl.program_id(0) == 0)
    def _():
        t_ref[...] = jnp.zeros_like(t_ref)
        s_ref[...] = jnp.zeros_like(s_ref)

    pieces = range(rows_ref.shape[0])
    student_width = student_ref.shape[0] // (steps * len(pieces))
    whole = student_width // 128 * 128
    end = teacher_width + whole
    stop = teacher_width + student_width
    step = pl.program_id(0)
    deep = len(pieces) * teacher_width
    first = pl.multiple_of(step * deep, deep)
    t_ref[...] += jnp.dot(
        jnp.concatenate([rows_ref[k, :, :teacher_width] for k in pieces], axis=1),
        teacher_ref[pl.ds(first, deep), :],
        preferred_element_type=F32,
    )
    base = step * len(pieces) * student_width

    def heads(k, start, count):
        return student_ref[pl.ds(pl.multiple_of(base + k * student_width + start, 64), count), :]

    s_ref[...] += jnp.dot(
        jnp.concatenate(
            [rows_ref[k, :, teacher_width:end] for k in pieces]
            + [rows_ref[k, :, end:stop] for k in pieces],
            axis=1,
        ),
        jnp.concatenate(
            [heads(k, 0, whole) for k in pieces]
            + [heads(k, whole, student_width - whole) for k in pieces],
            axis=0,
        ),
        preferred_element_type=F32,
    )

    @pl.when(step == steps - 1)
    def _():
        t_ref[...] = t_ref[...].T
        s_ref[...] = s_ref[...].T


def logits(rows, teacher_head, student_head, teacher_width):
    count, slots, width = rows.shape
    steps = 4
    vocab = teacher_head.shape[1]
    return pl.pallas_call(
        functools.partial(logits_step, teacher_width, steps),
        grid=(steps,),
        out_shape=[jax.ShapeDtypeStruct((slots, vocab), F32)] * 2,
        in_specs=[
            pl.BlockSpec((count // steps, slots, width), lambda i: (i, 0, 0)),
            VMEM,
            VMEM,
        ],
        out_specs=[pl.BlockSpec((slots, vocab), lambda i: (0, 0))] * 2,
        compiler_params=pltpu.CompilerParams(vmem_limit_bytes=50 * 1024 * 1024),
    )(rows, teacher_head, student_head)


def in_parts(stats, lanes):
    row = iota((16, lanes), 0)
    table = jnp.zeros((16, lanes), F32)
    for k, value in enumerate(stats):
        for part in range(3):
            rounded = value.astype(BF16).astype(F32)
            table = jnp.where(row == 3 * k + part, rounded, table)
            value = value - rounded
    return table


def from_parts(table, lanes):
    rows = [table[k : k + 1, :lanes] for k in range(9)]
    return [rows[k] + rows[k + 1] + rows[k + 2] for k in (0, 3, 6)]


def merged(stats):
    lse, mean, t_lse = zip(*stats)
    high = functools.reduce(jnp.maximum, lse)
    t_high = functools.reduce(jnp.maximum, t_lse)
    scale = [jnp.exp(v - high) for v in lse]
    total = sum(scale[1:], scale[0])
    scale = [v / total for v in scale]
    middle = sum((a * v for a, v in zip(scale[1:], mean[1:])), scale[0] * mean[0])
    t_total = sum((jnp.exp(v - t_high) for v in t_lse[1:]), jnp.exp(t_lse[0] - t_high))
    shift = [v - middle for v in mean]
    return scale, shift, [high + jnp.log(total), middle, t_high + jnp.log(t_total)]


def partial_kernel(
    info_ref, t_ref, s_ref, t_place_ref, s_place_ref, head_ref, keep_ref, send_ref, g_ref, stat_ref
):
    lanes = g_ref.shape[1] // 2

    @pl.when(pl.program_id(0) == 0)
    def _():
        def packed(place_ref, ref):
            slots = place_ref.shape[0]
            pick = (place_ref[:, :1] == iota((slots, lanes), 1)).astype(F32)
            return jnp.dot(
                ref[...], pick, preferred_element_type=F32, precision=lax.Precision.HIGHEST
            )

        t = packed(t_place_ref, t_ref)
        s = packed(s_place_ref, s_ref)
        gap = s - t
        t_top = jnp.max(t, axis=0, keepdims=True)
        t_lse = t_top + jnp.log(jnp.sum(jnp.exp(t - t_top), axis=0, keepdims=True))
        s_top = jnp.max(s, axis=0, keepdims=True)
        p = jnp.exp(s - s_top)
        total = jnp.sum(p, axis=0, keepdims=True)
        p = p / total
        mean = jnp.sum(p * gap, axis=0, keepdims=True)
        g_ref[:, :lanes] = (p * (gap - mean)).astype(BF16)
        g_ref[:, lanes:] = p.astype(BF16)
        table = in_parts([s_top + jnp.log(total), mean, t_lse], lanes)
        stat_ref[...] = jnp.concatenate([table, table], axis=1).astype(BF16)

    half = keep_ref.shape[1] - 16
    low = info_ref[1] == 0
    for k in range(keep_ref.shape[0]):
        part = jnp.dot(
            head_ref[2 * half * k : 2 * half * (k + 1), :],
            g_ref[...],
            preferred_element_type=F32,
        ).astype(BF16)
        keep_ref[k, :half] = jnp.where(low, part[:half], part[half:])
        send_ref[k, :half] = jnp.where(low, part[half:], part[:half])
        keep_ref[k, half:] = stat_ref[...]
        send_ref[k, half:] = stat_ref[...]


def partial(info, t, s, t_place, s_place, head, lanes, count):
    steps = 4
    half = head.shape[0] // count // 2
    part = jax.ShapeDtypeStruct((count, half + 16, 2 * lanes), BF16)
    block = pl.BlockSpec((count // steps, half + 16, 2 * lanes), lambda i: (i, 0, 0))
    whole = lambda a: pl.BlockSpec(a.shape, lambda i: (0,) * a.ndim)
    return pl.pallas_call(
        partial_kernel,
        grid=(steps,),
        out_shape=[part, part],
        in_specs=[
            SMEM,
            whole(t),
            whole(s),
            whole(t_place),
            whole(s_place),
            pl.BlockSpec((head.shape[0] // steps, head.shape[1]), lambda i: (i, 0)),
        ],
        out_specs=[block, block],
        scratch_shapes=[
            pltpu.VMEM((head.shape[1], 2 * lanes), BF16),
            pltpu.VMEM((16, 2 * lanes), BF16),
        ],
        compiler_params=PARAMS,
    )(info, t, s, t_place, s_place, head)


def pair_kernel(info_ref, keep_ref, came_ref, out_ref):
    lanes = out_ref.shape[2] // 2
    half = out_ref.shape[1] - 16
    low = info_ref[1] == 0
    kept = keep_ref[0, half:].astype(F32)
    come = came_ref[0, half:].astype(F32)
    first = jnp.where(low, kept, come)
    second = jnp.where(low, come, kept)
    scale, shift, stats = merged([from_parts(first, lanes), from_parts(second, lanes)])
    table = in_parts(stats, lanes)
    table = jnp.concatenate([table, table], axis=1).astype(BF16)
    own, other = (jnp.where(low, scale[0], scale[1]), jnp.where(low, scale[1], scale[0]))
    own_shift, other_shift = (
        own * jnp.where(low, shift[0], shift[1]),
        other * jnp.where(low, shift[1], shift[0]),
    )
    for k in range(out_ref.shape[0]):
        a = own * keep_ref[k, :half, :lanes].astype(F32)
        a += other * came_ref[k, :half, :lanes].astype(F32)
        b_own = keep_ref[k, :half, lanes:].astype(F32)
        b_other = came_ref[k, :half, lanes:].astype(F32)
        a += own_shift * b_own + other_shift * b_other
        out_ref[k, :half, :lanes] = a.astype(BF16)
        out_ref[k, :half, lanes:] = (own * b_own + other * b_other).astype(BF16)
        out_ref[k, half:] = table


def pair(info, keep, came):
    return pl.pallas_call(
        pair_kernel,
        out_shape=jax.ShapeDtypeStruct(keep.shape, BF16),
        in_specs=[SMEM, VMEM, VMEM],
        out_specs=VMEM,
        compiler_params=PARAMS,
    )(info, keep, came)


def spread_kernel(part_ref, place_ref, out_ref):
    lanes = part_ref.shape[2] // 2
    half = part_ref.shape[1] - 16
    count = part_ref.shape[0]
    groups, rows, width = out_ref.shape
    scale, shift, stats = merged(
        [from_parts(part_ref[k, half:].astype(F32), lanes) for k in range(count)]
    )
    a = jnp.zeros((half, lanes), F32)
    b = jnp.zeros((half, lanes), F32)
    for k in range(count):
        b_one = part_ref[k, :half, lanes:].astype(F32)
        a += scale[k] * part_ref[k, :half, :lanes].astype(F32) + (scale[k] * shift[k]) * b_one
        b += scale[k] * b_one
    rest = jnp.zeros((width - half - 16, lanes), F32)
    table = jnp.concatenate([in_parts(stats, lanes), rest], axis=0)
    slots = place_ref.shape[0]
    pick = (place_ref[:, :1] == iota((slots, lanes), 1)).astype(F32).astype(BF16)

    def found(value):
        value = jnp.concatenate([value, table], axis=0).astype(BF16)
        value = lax.dot_general(
            pick, value, (((1,), (1,)), ((), ())), preferred_element_type=F32
        )
        return value.reshape(groups, rows // 2, width)

    out_ref[...] = jnp.concatenate([found(a), found(b)], axis=1).astype(BF16)


def spread(parts, place, pad):
    groups = place.shape[0] // pad
    width = -(-parts.shape[1] // 128) * 128
    return pl.pallas_call(
        spread_kernel,
        out_shape=jax.ShapeDtypeStruct((groups, 2 * pad, width), BF16),
        in_specs=[VMEM, VMEM],
        out_specs=VMEM,
        compiler_params=PARAMS,
    )(parts, place)


def finish_kernel(info_ref, part_ref, grad_ref, kl_ref):
    _, pad, width = grad_ref.shape
    parts = [part_ref[k].astype(F32) for k in range(part_ref.shape[0])]
    stats = []
    for part in parts:
        column = [part[:pad, width + k : width + k + 1] for k in range(9)]
        stats.append([column[k] + column[k + 1] + column[k + 2] for k in (0, 3, 6)])
    scale, shift, (lse, mean, t_lse) = merged(stats)
    grad = jnp.zeros((pad, width), F32)
    for part, a, b in zip(parts, scale, shift):
        grad += a * (part[:pad, :width] + b * part[pad:, :width])
    grad_ref[0] = grad.astype(BF16)
    kl = jnp.where(iota((pad, 1), 0) < info_ref[3], mean - lse + t_lse, 0.0)
    square = iota((pad, pad), 0) == iota((pad, pad), 1)
    kl_ref[...] = jnp.sum(jnp.where(square, kl, 0.0), axis=0, keepdims=True)


def finish(info, parts, width):
    pad = parts.shape[1] // 2
    return pl.pallas_call(
        finish_kernel,
        out_shape=[
            jax.ShapeDtypeStruct((1, pad, width), BF16),
            jax.ShapeDtypeStruct((1, pad), F32),
        ],
        in_specs=[SMEM, VMEM],
        out_specs=[VMEM, VMEM],
    )(info, parts)


def tail(lanes, pad, operands):
    info, t, s, t_place, s_place, student_head = operands
    ring = lax.axis_size("y")
    keep, send = partial(info, t, s, t_place, s_place, student_head, lanes, ring)
    came = lax.ppermute(send, "c", ((0, 1), (1, 0)))
    both = pair(info, keep, came)
    return exchange(spread(exchange(both, "y"), s_place, pad), GRP)


def routing_kernel(
    groups, pad, group_ref, core_ref, lengths_ref, owner_ref, t_ref, s_ref, info_ref, start_ref
):
    share = lengths_ref.shape[0] // groups

    def total(g):
        return sum(lengths_ref[share * g + k] for k in range(share))

    def owned(j, found):
        g, count = found
        return lax.fori_loop(
            0,
            groups,
            lambda i, f: (
                jnp.where(owner_ref[share * i] == j, i, f[0]),
                jnp.where(owner_ref[share * i] == j, total(i), f[1]),
            ),
            (g, count),
        )

    slot = iota(t_ref.shape, 0)
    zero = jnp.int32(0)

    none = jnp.full(t_ref.shape, -1, jnp.int32)
    t_ref[...] = none
    s_ref[...] = none

    def place(j, start):
        g, count = owned(j, (zero, zero))
        for ref, first in ((t_ref, g * pad), (s_ref, j * pad)):
            step = slot - first
            ref[...] = jnp.where((step >= 0) & (step < count), start + step, ref[...])
        start_ref[j] = start
        start_ref[groups + j] = count
        return start + count

    live = lax.fori_loop(0, groups, place, zero)
    which = zero
    for c in CAPACITIES[:-1]:
        which += (live > c).astype(jnp.int32)
    info_ref[0] = which
    info_ref[1] = core_ref[0]
    info_ref[2] = start_ref[group_ref[0]]
    info_ref[3] = start_ref[groups + group_ref[0]]


def routing(group, core, lengths, owner, groups, pad):
    slots = groups * pad
    return pl.pallas_call(
        functools.partial(routing_kernel, groups, pad),
        out_shape=[
            jax.ShapeDtypeStruct((slots, 128), jnp.int32),
            jax.ShapeDtypeStruct((slots, 128), jnp.int32),
            jax.ShapeDtypeStruct((4,), jnp.int32),
        ],
        in_specs=[SMEM] * 4,
        out_specs=[VMEM] * 2 + [SMEM],
        scratch_shapes=[pltpu.SMEM((2 * groups,), jnp.int32)],
        cost_estimate=pl.CostEstimate(flops=10**8, bytes_accessed=10**6, transcendentals=0),
    )(group, core, lengths, owner)


def per_device(teacher_rows, student_rows, teacher_head, student_head, lengths, owner):
    groups = lax.axis_size(GRP)
    pad = student_rows.shape[1]
    group = lax.axis_index(GRP).astype(jnp.int32).reshape(1)
    core = lax.axis_index("c").astype(jnp.int32).reshape(1)
    mine = arrange(group, lengths, teacher_rows, student_rows, groups)
    rows = exchange(mine, GRP).reshape(groups * pad, mine.shape[2])
    rows = lax.all_gather(rows, VOCAB, axis=0, tiled=True)
    rows = rows.reshape(-1, groups * pad, mine.shape[2])
    t_place, s_place, info = routing(group, core, lengths, owner, groups, pad)
    t_head, s_head = stage(teacher_head, student_head)
    t, s = logits(rows, t_head, s_head, teacher_rows.shape[2])
    operands = (info, t, s, t_place, s_place, student_head)
    branches = [functools.partial(tail, c, pad) for c in CAPACITIES]
    parts = lax.switch(info[0], branches, operands)
    grad, divergence = finish(info, parts, student_rows.shape[2])
    return divergence, grad


def solution(mesh):
    torus = Mesh(mesh.devices.reshape(4, 8, 8, 2), ("x", "z", "y", "c"))
    return jax.shard_map(
        per_device,
        mesh=torus,
        in_specs=(
            P(GRP, None, VOCAB),
            P(GRP, None, VOCAB),
            P(None, (*GRP, *VOCAB)),
            P(None, (*GRP, *VOCAB)),
            P(),
            P(),
        ),
        out_specs=(P(GRP, None), P(GRP, None, VOCAB)),
        check_vma=False,
    )
```

```python
import functools

import jax
import jax.numpy as jnp
from jax import lax
from jax.experimental import pallas as pl
from jax.experimental.pallas import tpu as pltpu
from jax.sharding import Mesh
from jax.sharding import PartitionSpec as P

GRP = ("x", "z")
VOCAB = ("y", "c")
CAPACITIES = (128, 256)
F32 = jnp.float32
BF16 = jnp.bfloat16
VMEM = pl.BlockSpec(memory_space=pltpu.VMEM)
SMEM = pl.BlockSpec(memory_space=pltpu.SMEM)
PARAMS = pltpu.CompilerParams(vmem_limit_bytes=20 * 1024 * 1024)


def iota(shape, dim):
    return lax.broadcasted_iota(jnp.int32, shape, dim)


def exchange(pieces, axes):
    return lax.all_to_all(pieces, axes, 0, 0, tiled=True)


def arrange_kernel(
    place_ref, lengths_ref, owner_ref, meta_ref, teacher_ref, student_ref,
    out_ref, t_place_ref, s_place_ref, info_ref,
):
    count, pad, _ = out_ref.shape
    width = teacher_ref.shape[2]
    rest = out_ref.shape[2] - width - student_ref.shape[2]
    group = place_ref[0]
    share = lengths_ref.shape[0] // count
    first = lengths_ref[share * group]
    upper = teacher_ref[0].astype(F32)
    lower = pltpu.roll(teacher_ref[1].astype(F32), first, 0)
    chosen = jnp.where(iota(upper.shape, 0) < first, upper, lower).astype(BF16)
    for k in range(count):
        out_ref[k, :, :width] = chosen
        out_ref[k, :, width : width + student_ref.shape[2]] = student_ref[0]
        if rest:
            out_ref[k, :, -rest:] = jnp.zeros((pad, rest), BF16)

    live = jnp.int32(0)
    mine = jnp.int32(0)
    for k in range(lengths_ref.shape[0]):
        live += lengths_ref[k]
        mine += jnp.where(owner_ref[k] == group, lengths_ref[k], 0)
    which = jnp.int32(0)
    for c in CAPACITIES[:-1]:
        which += (live > c).astype(jnp.int32)
    info_ref[0] = which
    info_ref[1] = place_ref[1]
    info_ref[2] = mine

    slots = t_place_ref.shape[1]
    deep = meta_ref.shape[1]

    def column(k):
        one = jnp.broadcast_to(meta_ref[k : k + 1, :], (128, deep)).T
        return jnp.concatenate([one] * (slots // 128), axis=1)

    length, owner = column(0), column(1)
    seq = iota((deep, slots), 0)
    home = (iota((deep, slots), 1) // pad)
    zero = jnp.zeros((deep, slots), F32)

    def total(mask, value):
        return jnp.sum(jnp.where(mask, value, zero), axis=0, keepdims=True)

    home_f = home.astype(F32)
    step = (iota((1, slots), 1) % pad).astype(F32)
    t_count = total(seq // share == home, length)
    t_owner = total(seq == share * home, owner)
    t_start = total(owner < t_owner, length)
    s_count = total(owner == home_f, length)
    s_start = total(owner < home_f, length)
    t_place = jnp.where(step < t_count, t_start + step, -1.0)
    s_place = jnp.where(step < s_count, s_start + step, -1.0)
    t_place_ref[...] = t_place.astype(jnp.int32)
    s_place_ref[...] = s_place.astype(jnp.int32)


def arrange(place, lengths, owner, teacher_rows, student_rows, count):
    pad = student_rows.shape[1]
    width = -(-(teacher_rows.shape[2] + student_rows.shape[2]) // 128) * 128
    deep = -(-lengths.shape[0] // 128) * 128
    meta = jnp.stack([lengths, owner]).astype(F32)
    meta = jnp.pad(meta, ((0, 0), (0, deep - lengths.shape[0])))
    return pl.pallas_call(
        arrange_kernel,
        out_shape=[
            jax.ShapeDtypeStruct((count, pad, width), BF16),
            jax.ShapeDtypeStruct((1, count * pad), jnp.int32),
            jax.ShapeDtypeStruct((1, count * pad), jnp.int32),
            jax.ShapeDtypeStruct((3,), jnp.int32),
        ],
        in_specs=[SMEM, SMEM, SMEM, VMEM, VMEM, VMEM],
        out_specs=[VMEM, VMEM, VMEM, SMEM],
    )(place, lengths, owner, meta, teacher_rows, student_rows)


def pack_kernel(rows_ref, t_place_ref, s_place_ref, out_ref):
    count, half, _ = out_ref.shape
    slots = rows_ref.shape[0]
    width = out_ref.shape[2] // 2

    def packed(place_ref, first, stop):
        pick = (place_ref[...] == iota((2 * half, slots), 0)).astype(F32).astype(BF16)
        found = jnp.dot(pick, rows_ref[:, first:stop], preferred_element_type=F32)
        return found[:half], found[half:]

    t = packed(t_place_ref, 0, 256)
    s = packed(s_place_ref, 256, width)
    value = jnp.concatenate(
        [*t, s[0][:, :256], s[1][:, :256], s[0][:, 256:], s[1][:, 256:]], axis=1
    ).astype(BF16)
    for k in range(count):
        out_ref[k] = value


def pack(rows, t_place, s_place, lanes, width, count):
    return pl.pallas_call(
        pack_kernel,
        out_shape=jax.ShapeDtypeStruct((count, lanes // 2, 2 * width), BF16),
        in_specs=[VMEM] * 3,
        out_specs=VMEM,
        compiler_params=PARAMS,
    )(rows, t_place, s_place)


def stage_kernel(teacher_ref, student_ref, t_out_ref, s_out_ref, sems):
    copies = [
        pltpu.make_async_copy(teacher_ref, t_out_ref, sems.at[0]),
        pltpu.make_async_copy(student_ref, s_out_ref, sems.at[1]),
    ]
    for copy in copies:
        copy.start()
    for copy in copies:
        copy.wait()


def stage(teacher_head, student_head):
    size = 2 * (teacher_head.size + student_head.size)
    return pl.pallas_call(
        stage_kernel,
        out_shape=[
            jax.ShapeDtypeStruct(teacher_head.shape, BF16),
            jax.ShapeDtypeStruct(student_head.shape, BF16),
        ],
        in_specs=[pl.BlockSpec(memory_space=pl.ANY)] * 2,
        out_specs=[VMEM] * 2,
        scratch_shapes=[pltpu.SemaphoreType.DMA((2,))],
        compiler_params=PARAMS,
        cost_estimate=pl.CostEstimate(flops=0, bytes_accessed=2 * size, transcendentals=0),
    )(teacher_head, student_head)


def logits_step(teacher_width, steps, rows_ref, teacher_ref, student_ref, t_ref, s_ref):
    @pl.when(pl.program_id(0) == 0)
    def _():
        t_ref[...] = jnp.zeros_like(t_ref)
        s_ref[...] = jnp.zeros_like(s_ref)

    pieces = range(rows_ref.shape[0])
    student_width = student_ref.shape[0] // (steps * len(pieces))
    whole = student_width // 128 * 128
    end = teacher_width + whole
    stop = teacher_width + student_width
    step = pl.program_id(0)
    deep = len(pieces) * teacher_width
    first = pl.multiple_of(step * deep, deep)
    t_ref[...] += jnp.dot(
        jnp.concatenate([rows_ref[k, :, :teacher_width] for k in pieces], axis=1),
        teacher_ref[pl.ds(first, deep), :],
        preferred_element_type=F32,
    )
    base = step * len(pieces) * student_width

    def heads(k, start, count):
        return student_ref[pl.ds(pl.multiple_of(base + k * student_width + start, 64), count), :]

    s_ref[...] += jnp.dot(
        jnp.concatenate(
            [rows_ref[k, :, teacher_width:end] for k in pieces]
            + [rows_ref[k, :, end:stop] for k in pieces],
            axis=1,
        ),
        jnp.concatenate(
            [heads(k, 0, whole) for k in pieces]
            + [heads(k, whole, student_width - whole) for k in pieces],
            axis=0,
        ),
        preferred_element_type=F32,
    )

    @pl.when(step == steps - 1)
    def _():
        t_ref[...] = t_ref[...].T
        s_ref[...] = s_ref[...].T


def logits(rows, teacher_head, student_head, teacher_width):
    count, slots, width = rows.shape
    steps = 4
    vocab = teacher_head.shape[1]
    return pl.pallas_call(
        functools.partial(logits_step, teacher_width, steps),
        grid=(steps,),
        out_shape=[jax.ShapeDtypeStruct((slots, vocab), F32)] * 2,
        in_specs=[
            pl.BlockSpec((count // steps, slots, width), lambda i: (i, 0, 0)),
            VMEM,
            VMEM,
        ],
        out_specs=[pl.BlockSpec((slots, vocab), lambda i: (0, 0))] * 2,
        compiler_params=pltpu.CompilerParams(vmem_limit_bytes=50 * 1024 * 1024),
    )(rows, teacher_head, student_head)


def in_parts(stats, lanes):
    row = iota((16, lanes), 0)
    table = jnp.zeros((16, lanes), F32)
    for k, value in enumerate(stats):
        for part in range(3):
            rounded = value.astype(BF16).astype(F32)
            table = jnp.where(row == 3 * k + part, rounded, table)
            value = value - rounded
    return table


def from_parts(table, lanes):
    rows = [table[k : k + 1, :lanes] for k in range(9)]
    return [rows[k] + rows[k + 1] + rows[k + 2] for k in (0, 3, 6)]


def merged(stats):
    lse, mean, t_lse = zip(*stats)
    high = functools.reduce(jnp.maximum, lse)
    t_high = functools.reduce(jnp.maximum, t_lse)
    scale = [jnp.exp(v - high) for v in lse]
    total = sum(scale[1:], scale[0])
    scale = [v / total for v in scale]
    middle = sum((a * v for a, v in zip(scale[1:], mean[1:])), scale[0] * mean[0])
    t_total = sum((jnp.exp(v - t_high) for v in t_lse[1:]), jnp.exp(t_lse[0] - t_high))
    shift = [v - middle for v in mean]
    return scale, shift, [high + jnp.log(total), middle, t_high + jnp.log(t_total)]


def soften(t, s, g_ref, stat_ref):
    lanes = g_ref.shape[1] // 2
    gap = s - t
    t_top = jnp.max(t, axis=0, keepdims=True)
    t_lse = t_top + jnp.log(jnp.sum(jnp.exp(t - t_top), axis=0, keepdims=True))
    s_top = jnp.max(s, axis=0, keepdims=True)
    p = jnp.exp(s - s_top)
    total = jnp.sum(p, axis=0, keepdims=True)
    p = p / total
    mean = jnp.sum(p * gap, axis=0, keepdims=True)
    g_ref[:, :lanes] = (p * (gap - mean)).astype(BF16)
    g_ref[:, lanes:] = p.astype(BF16)
    table = in_parts([s_top + jnp.log(total), mean, t_lse], lanes)
    stat_ref[...] = jnp.concatenate([table, table], axis=1).astype(BF16)


def backward(low, head_ref, g_ref, stat_ref, keep_ref, send_ref):
    half = keep_ref.shape[1] - 16
    for k in range(keep_ref.shape[0]):
        part = jnp.dot(
            head_ref[2 * half * k : 2 * half * (k + 1), :],
            g_ref[...],
            preferred_element_type=F32,
        ).astype(BF16)
        keep_ref[k, :half] = jnp.where(low, part[:half], part[half:])
        send_ref[k, :half] = jnp.where(low, part[half:], part[:half])
        keep_ref[k, half:] = stat_ref[...]
        send_ref[k, half:] = stat_ref[...]


def partial_kernel(
    info_ref, t_ref, s_ref, t_place_ref, s_place_ref, head_ref, keep_ref, send_ref, g_ref, stat_ref
):
    lanes = g_ref.shape[1] // 2

    @pl.when(pl.program_id(0) == 0)
    def _():
        def packed(place_ref, ref):
            slots = place_ref.shape[1]
            pick = (place_ref[...] == iota((lanes, slots), 0)).astype(F32).T
            return jnp.dot(
                ref[...], pick, preferred_element_type=F32, precision=lax.Precision.HIGHEST
            )

        soften(packed(t_place_ref, t_ref), packed(s_place_ref, s_ref), g_ref, stat_ref)

    backward(info_ref[1] == 0, head_ref, g_ref, stat_ref, keep_ref, send_ref)


def whole_kernel(
    steps, info_ref, own_ref, other_ref, t_head_ref, s_head_ref, keep_ref, send_ref,
    t_ref, s_ref, g_ref, stat_ref,
):
    step = pl.program_id(0)
    low = info_ref[1] == 0

    @pl.when(step == 0)
    def _():
        t_ref[...] = jnp.zeros_like(t_ref)
        s_ref[...] = jnp.zeros_like(s_ref)

    @pl.when(step < steps)
    def _():
        pieces = []
        for k in range(own_ref.shape[0]):
            pieces.append(jnp.where(low, own_ref[k], other_ref[k]))
            pieces.append(jnp.where(low, other_ref[k], own_ref[k]))
        t_size = t_head_ref.shape[0] // len(pieces)
        s_size = s_head_ref.shape[0] // len(pieces)
        main = s_size // 128 * 128
        tail_size = s_size - main

        def rows(x, first, size):
            return jnp.concatenate([x[:, first : first + size], x[:, first + size : first + 2 * size]], axis=0)

        t_ref[...] += jnp.dot(
            jnp.concatenate([rows(x, 0, t_size) for x in pieces], axis=1),
            t_head_ref[...],
            preferred_element_type=F32,
        )
        first = 2 * t_size
        last = first + 2 * main
        count = len(pieces)
        s_ref[...] += jnp.dot(
            jnp.concatenate(
                [rows(x, first, main) for x in pieces] + [rows(x, last, tail_size) for x in pieces],
                axis=1,
            ),
            jnp.concatenate(
                [s_head_ref[k * s_size : k * s_size + main, :] for k in range(count)]
                + [s_head_ref[k * s_size + main : (k + 1) * s_size, :] for k in range(count)],
                axis=0,
            ),
            preferred_element_type=F32,
        )

    @pl.when(step == steps)
    def _():
        soften(t_ref[...].T, s_ref[...].T, g_ref, stat_ref)

    @pl.when(step >= steps)
    def _():
        backward(low, s_head_ref, g_ref, stat_ref, keep_ref, send_ref)


def whole(info, own, other, t_head, s_head):
    steps = 4
    count, half_rows, width = own.shape
    lanes = 2 * half_rows
    vocab = s_head.shape[1]
    half = s_head.shape[0] // count // 2
    part = jax.ShapeDtypeStruct((count, half + 16, 2 * lanes), BF16)
    block = pl.BlockSpec(
        (count // steps, half + 16, 2 * lanes), lambda i: (jnp.maximum(i - steps, 0), 0, 0)
    )
    rows = pl.BlockSpec(
        (count // steps, half_rows, width), lambda i: (jnp.minimum(i, steps - 1), 0, 0)
    )
    return pl.pallas_call(
        functools.partial(whole_kernel, steps),
        grid=(2 * steps,),
        out_shape=[part, part],
        in_specs=[
            SMEM,
            rows,
            rows,
            pl.BlockSpec((t_head.shape[0] // steps, vocab), lambda i: (jnp.minimum(i, steps - 1), 0)),
            pl.BlockSpec((s_head.shape[0] // steps, vocab), lambda i: (lax.rem(i, steps), 0)),
        ],
        out_specs=[block, block],
        scratch_shapes=[
            pltpu.VMEM((lanes, vocab), F32),
            pltpu.VMEM((lanes, vocab), F32),
            pltpu.VMEM((vocab, 2 * lanes), BF16),
            pltpu.VMEM((16, 2 * lanes), BF16),
        ],
        compiler_params=PARAMS,
    )(info, own, other, t_head, s_head)


def partial(info, t, s, t_place, s_place, head, lanes, count):
    steps = 4
    half = head.shape[0] // count // 2
    part = jax.ShapeDtypeStruct((count, half + 16, 2 * lanes), BF16)
    block = pl.BlockSpec((count // steps, half + 16, 2 * lanes), lambda i: (i, 0, 0))
    full = lambda a: pl.BlockSpec(a.shape, lambda i: (0,) * a.ndim)
    return pl.pallas_call(
        partial_kernel,
        grid=(steps,),
        out_shape=[part, part],
        in_specs=[
            SMEM,
            full(t),
            full(s),
            full(t_place),
            full(s_place),
            pl.BlockSpec((head.shape[0] // steps, head.shape[1]), lambda i: (i, 0)),
        ],
        out_specs=[block, block],
        scratch_shapes=[
            pltpu.VMEM((head.shape[1], 2 * lanes), BF16),
            pltpu.VMEM((16, 2 * lanes), BF16),
        ],
        compiler_params=PARAMS,
    )(info, t, s, t_place, s_place, head)


def pair_kernel(info_ref, keep_ref, came_ref, out_ref):
    lanes = out_ref.shape[2] // 2
    half = out_ref.shape[1] - 16
    low = info_ref[1] == 0
    kept = keep_ref[0, half:].astype(F32)
    come = came_ref[0, half:].astype(F32)
    first = jnp.where(low, kept, come)
    second = jnp.where(low, come, kept)
    scale, shift, stats = merged([from_parts(first, lanes), from_parts(second, lanes)])
    table = in_parts(stats, lanes)
    table = jnp.concatenate([table, table], axis=1).astype(BF16)
    own, other = (jnp.where(low, scale[0], scale[1]), jnp.where(low, scale[1], scale[0]))
    own_shift, other_shift = (
        own * jnp.where(low, shift[0], shift[1]),
        other * jnp.where(low, shift[1], shift[0]),
    )
    for k in range(out_ref.shape[0]):
        a = own * keep_ref[k, :half, :lanes].astype(F32)
        a += other * came_ref[k, :half, :lanes].astype(F32)
        b_own = keep_ref[k, :half, lanes:].astype(F32)
        b_other = came_ref[k, :half, lanes:].astype(F32)
        a += own_shift * b_own + other_shift * b_other
        out_ref[k, :half, :lanes] = a.astype(BF16)
        out_ref[k, :half, lanes:] = (own * b_own + other * b_other).astype(BF16)
        out_ref[k, half:] = table


def pair(info, keep, came):
    return pl.pallas_call(
        pair_kernel,
        out_shape=jax.ShapeDtypeStruct(keep.shape, BF16),
        in_specs=[SMEM, VMEM, VMEM],
        out_specs=VMEM,
        compiler_params=PARAMS,
    )(info, keep, came)


def spread_kernel(part_ref, place_ref, out_ref):
    lanes = part_ref.shape[2] // 2
    half = part_ref.shape[1] - 16
    count = part_ref.shape[0]
    groups, rows, width = out_ref.shape
    scale, shift, stats = merged(
        [from_parts(part_ref[k, half:].astype(F32), lanes) for k in range(count)]
    )
    a = jnp.zeros((half, lanes), F32)
    b = jnp.zeros((half, lanes), F32)
    for k in range(count):
        b_one = part_ref[k, :half, lanes:].astype(F32)
        a += scale[k] * part_ref[k, :half, :lanes].astype(F32) + (scale[k] * shift[k]) * b_one
        b += scale[k] * b_one
    rest = jnp.zeros((width - half - 16, lanes), F32)
    table = jnp.concatenate([in_parts(stats, lanes), rest], axis=0)
    slots = place_ref.shape[1]
    pick = (place_ref[...] == iota((lanes, slots), 0)).astype(F32).T.astype(BF16)

    def found(value):
        value = jnp.concatenate([value, table], axis=0).astype(BF16)
        value = lax.dot_general(
            pick, value, (((1,), (1,)), ((), ())), preferred_element_type=F32
        )
        return value.reshape(groups, rows // 2, width)

    out_ref[...] = jnp.concatenate([found(a), found(b)], axis=1).astype(BF16)


def spread(parts, place, pad):
    groups = place.shape[1] // pad
    width = -(-parts.shape[1] // 128) * 128
    return pl.pallas_call(
        spread_kernel,
        out_shape=jax.ShapeDtypeStruct((groups, 2 * pad, width), BF16),
        in_specs=[VMEM, VMEM],
        out_specs=VMEM,
        compiler_params=PARAMS,
    )(parts, place)


def finish_kernel(info_ref, part_ref, grad_ref, kl_ref):
    _, pad, width = grad_ref.shape
    parts = [part_ref[k].astype(F32) for k in range(part_ref.shape[0])]
    stats = []
    for part in parts:
        column = [part[:pad, width + k : width + k + 1] for k in range(9)]
        stats.append([column[k] + column[k + 1] + column[k + 2] for k in (0, 3, 6)])
    scale, shift, (lse, mean, t_lse) = merged(stats)
    grad = jnp.zeros((pad, width), F32)
    for part, a, b in zip(parts, scale, shift):
        grad += a * (part[:pad, :width] + b * part[pad:, :width])
    grad_ref[0] = grad.astype(BF16)
    kl = jnp.where(iota((pad, 1), 0) < info_ref[2], mean - lse + t_lse, 0.0)
    square = iota((pad, pad), 0) == iota((pad, pad), 1)
    kl_ref[...] = jnp.sum(jnp.where(square, kl, 0.0), axis=0, keepdims=True)


def finish(info, parts, width):
    pad = parts.shape[1] // 2
    return pl.pallas_call(
        finish_kernel,
        out_shape=[
            jax.ShapeDtypeStruct((1, pad, width), BF16),
            jax.ShapeDtypeStruct((1, pad), F32),
        ],
        in_specs=[SMEM, VMEM],
        out_specs=[VMEM, VMEM],
    )(info, parts)


def swap(value):
    return lax.ppermute(value, "c", ((0, 1), (1, 0)))


def reduce(info, keep, send, s_place, pad):
    both = pair(info, keep, swap(send))
    return exchange(spread(exchange(both, "y"), s_place, pad), GRP)


def some_rows(lanes, pad, width, operands):
    info, rows, t_place, s_place, teacher_head, student_head = operands
    ring = lax.axis_size("y")
    own = exchange(pack(rows, t_place, s_place, lanes, width, ring), "y")
    keep, send = whole(info, own, swap(own), teacher_head, student_head)
    return reduce(info, keep, send, s_place, pad)


def all_rows(lanes, pad, t_width, operands):
    info, rows, t_place, s_place, teacher_head, student_head = operands
    ring = lax.axis_size("y")
    full = lax.all_gather(rows, VOCAB, axis=0, tiled=True).reshape(-1, *rows.shape)
    t_head, s_head = stage(teacher_head, student_head)
    t, s = logits(full, t_head, s_head, t_width)
    keep, send = partial(info, t, s, t_place, s_place, student_head, lanes, ring)
    return reduce(info, keep, send, s_place, pad)


def per_device(teacher_rows, student_rows, teacher_head, student_head, lengths, owner):
    groups = lax.axis_size(GRP)
    pad = student_rows.shape[1]
    t_width, s_width = teacher_rows.shape[2], student_rows.shape[2]
    place = jnp.stack([lax.axis_index(GRP), lax.axis_index("c")]).astype(jnp.int32)
    mine, t_place, s_place, info = arrange(
        place, lengths, owner, teacher_rows, student_rows, groups
    )
    rows = exchange(mine, GRP).reshape(groups * pad, mine.shape[2])
    operands = (info, rows, t_place, s_place, teacher_head, student_head)
    few, every = CAPACITIES
    branches = [
        functools.partial(some_rows, few, pad, t_width + s_width),
        functools.partial(all_rows, every, pad, t_width),
    ]
    grad, divergence = finish(info, lax.switch(info[0], branches, operands), s_width)
    return divergence, grad


def solution(mesh):
    torus = Mesh(mesh.devices.reshape(4, 8, 8, 2), ("x", "z", "y", "c"))
    return jax.shard_map(
        per_device,
        mesh=torus,
        in_specs=(
            P(GRP, None, VOCAB),
            P(GRP, None, VOCAB),
            P(None, (*GRP, *VOCAB)),
            P(None, (*GRP, *VOCAB)),
            P(),
            P(),
        ),
        out_specs=(P(GRP, None), P(GRP, None, VOCAB)),
        check_vma=False,
    )
```

```python
import functools

import jax
import jax.numpy as jnp
from jax import lax
from jax.experimental import pallas as pl
from jax.experimental.pallas import tpu as pltpu
from jax.sharding import Mesh
from jax.sharding import PartitionSpec as P

GRP = ("x", "z")
VOCAB = ("y", "c")
CAPACITIES = (128, 256)
F32 = jnp.float32
BF16 = jnp.bfloat16
VMEM = pl.BlockSpec(memory_space=pltpu.VMEM)
SMEM = pl.BlockSpec(memory_space=pltpu.SMEM)
PARAMS = pltpu.CompilerParams(vmem_limit_bytes=20 * 1024 * 1024)


def iota(shape, dim):
    return lax.broadcasted_iota(jnp.int32, shape, dim)


def exchange(pieces, axes):
    return lax.all_to_all(pieces, axes, 0, 0, tiled=True)


def arrange_kernel(
    group_ref, core_ref, lengths_ref, owner_ref, length_row_ref, owner_row_ref, teacher_ref, student_ref,
    out_ref, t_place_ref, s_place_ref, info_ref,
):
    count, pad, _ = out_ref.shape
    width = teacher_ref.shape[2]
    rest = out_ref.shape[2] - width - student_ref.shape[2]
    group = group_ref[0]
    share = lengths_ref.shape[0] // count
    first = lengths_ref[share * group]
    upper = teacher_ref[0].astype(F32)
    lower = pltpu.roll(teacher_ref[1].astype(F32), first, 0)
    chosen = jnp.where(iota(upper.shape, 0) < first, upper, lower).astype(BF16)
    for k in range(count):
        out_ref[k, :, :width] = chosen
        out_ref[k, :, width : width + student_ref.shape[2]] = student_ref[0]
        if rest:
            out_ref[k, :, -rest:] = jnp.zeros((pad, rest), BF16)

    live = jnp.int32(0)
    mine = jnp.int32(0)
    for k in range(lengths_ref.shape[0]):
        live += lengths_ref[k]
        mine += jnp.where(owner_ref[k] == group, lengths_ref[k], 0)
    which = jnp.int32(0)
    for c in CAPACITIES[:-1]:
        which += (live > c).astype(jnp.int32)
    info_ref[0] = which
    info_ref[1] = core_ref[0]
    info_ref[2] = mine

    slots = t_place_ref.shape[1]
    deep = length_row_ref.shape[1]

    def column(ref):
        one = jnp.broadcast_to(ref[...].astype(F32), (deep, deep)).T
        return jnp.broadcast_to(one[:, :1], (deep, slots))

    length, owner = column(length_row_ref), column(owner_row_ref)
    seq = iota((deep, slots), 0)
    home = (iota((deep, slots), 1) // pad)
    zero = jnp.zeros((deep, slots), F32)

    def total(mask, value):
        return jnp.sum(jnp.where(mask, value, zero), axis=0, keepdims=True)

    home_f = home.astype(F32)
    step = (iota((1, slots), 1) % pad).astype(F32)
    t_count = total(seq // share == home, length)
    t_owner = total(seq == share * home, owner)
    t_start = total(owner < t_owner, length)
    s_count = total(owner == home_f, length)
    s_start = total(owner < home_f, length)
    t_place = jnp.where(step < t_count, t_start + step, -1.0)
    s_place = jnp.where(step < s_count, s_start + step, -1.0)
    t_place_ref[...] = t_place.astype(jnp.int32)
    s_place_ref[...] = s_place.astype(jnp.int32)


def arrange(group, core, lengths, owner, teacher_rows, student_rows, count):
    pad = student_rows.shape[1]
    width = -(-(teacher_rows.shape[2] + student_rows.shape[2]) // 128) * 128
    return pl.pallas_call(
        arrange_kernel,
        out_shape=[
            jax.ShapeDtypeStruct((count, pad, width), BF16),
            jax.ShapeDtypeStruct((1, count * pad), jnp.int32),
            jax.ShapeDtypeStruct((1, count * pad), jnp.int32),
            jax.ShapeDtypeStruct((3,), jnp.int32),
        ],
        in_specs=[SMEM] * 4 + [VMEM] * 4,
        out_specs=[VMEM, VMEM, VMEM, SMEM],
    )(
        group,
        core,
        lengths,
        owner,
        lengths.reshape(1, -1),
        owner.reshape(1, -1),
        teacher_rows,
        student_rows,
    )


def pack_kernel(t_width, rows_ref, t_place_ref, s_place_ref, out_ref):
    count, half, _ = out_ref.shape
    slots = rows_ref.shape[0]
    width = out_ref.shape[2] // 2

    def packed(place_ref, first, stop):
        pick = (place_ref[...] == iota((2 * half, slots), 0)).astype(F32).astype(BF16)
        found = jnp.dot(pick, rows_ref[:, first:stop], preferred_element_type=F32)
        return found[:half], found[half:]

    main = (width - t_width) // 128 * 128
    t = packed(t_place_ref, 0, t_width)
    low, high = packed(s_place_ref, t_width, width)
    value = jnp.concatenate(
        [*t, low[:, :main], high[:, :main], low[:, main:], high[:, main:]], axis=1
    ).astype(BF16)
    for k in range(count):
        out_ref[k] = value


def pack(rows, t_place, s_place, lanes, t_width, width, count):
    return pl.pallas_call(
        functools.partial(pack_kernel, t_width),
        out_shape=jax.ShapeDtypeStruct((count, lanes // 2, 2 * width), BF16),
        in_specs=[VMEM] * 3,
        out_specs=VMEM,
        compiler_params=PARAMS,
    )(rows, t_place, s_place)


def in_parts(stats, lanes):
    row = iota((16, lanes), 0)
    table = jnp.zeros((16, lanes), F32)
    for k, value in enumerate(stats):
        for part in range(3):
            rounded = value.astype(BF16).astype(F32)
            table = jnp.where(row == 3 * k + part, rounded, table)
            value = value - rounded
    return table


def from_parts(table, lanes):
    rows = [table[k : k + 1, :lanes] for k in range(9)]
    return [rows[k] + rows[k + 1] + rows[k + 2] for k in (0, 3, 6)]


def merged(stats):
    lse, mean, t_lse = zip(*stats)
    high = functools.reduce(jnp.maximum, lse)
    t_high = functools.reduce(jnp.maximum, t_lse)
    scale = [jnp.exp(v - high) for v in lse]
    total = sum(scale[1:], scale[0])
    scale = [v / total for v in scale]
    middle = sum((a * v for a, v in zip(scale[1:], mean[1:])), scale[0] * mean[0])
    t_total = sum((jnp.exp(v - t_high) for v in t_lse[1:]), jnp.exp(t_lse[0] - t_high))
    shift = [v - middle for v in mean]
    return scale, shift, [high + jnp.log(total), middle, t_high + jnp.log(t_total)]


def soften(t, s, g_ref, stat_ref):
    lanes = g_ref.shape[1] // 2
    gap = s - t
    t_top = jnp.max(t, axis=0, keepdims=True)
    t_lse = t_top + jnp.log(jnp.sum(jnp.exp(t - t_top), axis=0, keepdims=True))
    s_top = jnp.max(s, axis=0, keepdims=True)
    p = jnp.exp(s - s_top)
    total = jnp.sum(p, axis=0, keepdims=True)
    p = p / total
    mean = jnp.sum(p * gap, axis=0, keepdims=True)
    g_ref[:, :lanes] = (p * (gap - mean)).astype(BF16)
    g_ref[:, lanes:] = p.astype(BF16)
    table = in_parts([s_top + jnp.log(total), mean, t_lse], lanes)
    stat_ref[...] = jnp.concatenate([table, table], axis=1).astype(BF16)


def product(rows_ref, t_head_ref, s_head_ref, t, s):
    t_size, s_size = t_head_ref.shape[1], s_head_ref.shape[1]
    main = s_size // 128 * 128

    def rows(k, first, size):
        low = rows_ref[k, :, first : first + size]
        high = rows_ref[k, :, first + size : first + 2 * size]
        return jnp.concatenate([low, high], axis=0)

    count = rows_ref.shape[0]
    batch = 4
    for start in range(0, count, batch):
        ids = range(start, start + batch)
        t += jnp.dot(
            jnp.concatenate([rows(k, 0, t_size) for k in ids], axis=1),
            jnp.concatenate([t_head_ref[k] for k in ids], axis=0),
            preferred_element_type=F32,
        )
        s += jnp.dot(
            jnp.concatenate(
                [rows(k, 2 * t_size, main) for k in ids]
                + [rows(k, 2 * (t_size + main), s_size - main) for k in ids],
                axis=1,
            ),
            jnp.concatenate(
                [s_head_ref[k, :main] for k in ids] + [s_head_ref[k, main:] for k in ids],
                axis=0,
            ),
            preferred_element_type=F32,
        )
    return t, s


def first_kernel(
    info_ref, own_ref, t_head_ref, s_head_ref, t_ref, s_ref,
    s_own_ref, t_other_ref, s_other_ref, t_own_ref, sems,
):
    core = info_ref[1]
    copies = [
        pltpu.make_async_copy(head.at[:, c], to, sems.at[k])
        for k, (head, c, to) in enumerate(
            (
                (t_head_ref, core, t_own_ref),
                (s_head_ref, core, s_own_ref),
                (t_head_ref, 1 - core, t_other_ref),
                (s_head_ref, 1 - core, s_other_ref),
            )
        )
    ]
    for copy in copies:
        copy.start()
    copies[0].wait()
    copies[1].wait()
    zero = jnp.zeros(t_ref.shape, F32)
    t, s = product(own_ref, t_own_ref, s_own_ref, zero, zero)
    t_ref[...] = t
    s_ref[...] = s
    copies[2].wait()
    copies[3].wait()


def first(info, own, t_head, s_head):
    count, half_rows, width = own.shape
    vocab = t_head.shape[1]
    t_head = t_head.reshape(count, 2, -1, vocab)
    s_head = s_head.reshape(count, 2, -1, vocab)
    logit = jax.ShapeDtypeStruct((2 * half_rows, vocab), F32)
    t_part = (count, *t_head.shape[2:])
    s_part = (count, *s_head.shape[2:])
    return pl.pallas_call(
        first_kernel,
        out_shape=[
            logit,
            logit,
            jax.ShapeDtypeStruct(s_part, BF16),
            jax.ShapeDtypeStruct(t_part, BF16),
            jax.ShapeDtypeStruct(s_part, BF16),
        ],
        in_specs=[SMEM, VMEM] + [pl.BlockSpec(memory_space=pl.ANY)] * 2,
        out_specs=[VMEM] * 5,
        scratch_shapes=[pltpu.VMEM(t_part, BF16), pltpu.SemaphoreType.DMA((4,))],
        compiler_params=PARAMS,
        cost_estimate=pl.CostEstimate(
            flops=2 * own.size * vocab, bytes_accessed=4 * (t_head.size + s_head.size), transcendentals=0
        ),
    )(info, own, t_head, s_head)


def second_kernel(
    other_ref, t_ref, s_ref, s_own_ref, t_other_ref, s_other_ref, keep_ref, send_ref, g_ref, stat_ref
):
    t, s = product(other_ref, t_other_ref, s_other_ref, t_ref[...], s_ref[...])
    soften(t.T, s.T, g_ref, stat_ref)
    half = s_own_ref.shape[1]
    for k in range(keep_ref.shape[0]):
        for head_ref, out_ref in ((s_own_ref, keep_ref), (s_other_ref, send_ref)):
            out_ref[k, :half] = jnp.dot(
                head_ref[k], g_ref[...], preferred_element_type=F32
            ).astype(BF16)
            out_ref[k, half:] = stat_ref[...]


def second(other, t, s, s_own, t_other, s_other):
    lanes, vocab = t.shape
    count, half, _ = s_own.shape
    part = jax.ShapeDtypeStruct((count, half + 16, 2 * lanes), BF16)
    return pl.pallas_call(
        second_kernel,
        out_shape=[part, part],
        in_specs=[VMEM] * 6,
        out_specs=[VMEM] * 2,
        scratch_shapes=[
            pltpu.VMEM((vocab, 2 * lanes), BF16),
            pltpu.VMEM((16, 2 * lanes), BF16),
        ],
        compiler_params=PARAMS,
    )(other, t, s, s_own, t_other, s_other)


def pair_kernel(info_ref, keep_ref, came_ref, out_ref):
    lanes = out_ref.shape[2] // 2
    half = out_ref.shape[1] - 16
    low = info_ref[1] == 0
    kept = keep_ref[0, half:].astype(F32)
    come = came_ref[0, half:].astype(F32)
    first = jnp.where(low, kept, come)
    second = jnp.where(low, come, kept)
    scale, shift, stats = merged([from_parts(first, lanes), from_parts(second, lanes)])
    table = in_parts(stats, lanes)
    table = jnp.concatenate([table, table], axis=1).astype(BF16)
    own, other = (jnp.where(low, scale[0], scale[1]), jnp.where(low, scale[1], scale[0]))
    own_shift, other_shift = (
        own * jnp.where(low, shift[0], shift[1]),
        other * jnp.where(low, shift[1], shift[0]),
    )
    for k in range(out_ref.shape[0]):
        a = own * keep_ref[k, :half, :lanes].astype(F32)
        a += other * came_ref[k, :half, :lanes].astype(F32)
        b_own = keep_ref[k, :half, lanes:].astype(F32)
        b_other = came_ref[k, :half, lanes:].astype(F32)
        a += own_shift * b_own + other_shift * b_other
        out_ref[k, :half, :lanes] = a.astype(BF16)
        out_ref[k, :half, lanes:] = (own * b_own + other * b_other).astype(BF16)
        out_ref[k, half:] = table


def pair(info, keep, came):
    return pl.pallas_call(
        pair_kernel,
        out_shape=jax.ShapeDtypeStruct(keep.shape, BF16),
        in_specs=[SMEM, VMEM, VMEM],
        out_specs=VMEM,
        compiler_params=PARAMS,
    )(info, keep, came)


def spread_kernel(part_ref, place_ref, out_ref):
    lanes = part_ref.shape[2] // 2
    half = part_ref.shape[1] - 16
    count = part_ref.shape[0]
    groups, rows, width = out_ref.shape
    scale, shift, stats = merged(
        [from_parts(part_ref[k, half:].astype(F32), lanes) for k in range(count)]
    )
    a = jnp.zeros((half, lanes), F32)
    b = jnp.zeros((half, lanes), F32)
    for k in range(count):
        b_one = part_ref[k, :half, lanes:].astype(F32)
        a += scale[k] * part_ref[k, :half, :lanes].astype(F32) + (scale[k] * shift[k]) * b_one
        b += scale[k] * b_one
    rest = jnp.zeros((width - half - 16, lanes), F32)
    table = jnp.concatenate([in_parts(stats, lanes), rest], axis=0)
    slots = place_ref.shape[1]
    pick = (place_ref[...] == iota((lanes, slots), 0)).astype(F32).T.astype(BF16)

    def found(value):
        value = jnp.concatenate([value, table], axis=0).astype(BF16)
        value = lax.dot_general(
            pick, value, (((1,), (1,)), ((), ())), preferred_element_type=F32
        )
        return value.reshape(groups, rows // 2, width)

    out_ref[...] = jnp.concatenate([found(a), found(b)], axis=1).astype(BF16)


def spread(parts, place, pad):
    groups = place.shape[1] // pad
    width = -(-parts.shape[1] // 128) * 128
    return pl.pallas_call(
        spread_kernel,
        out_shape=jax.ShapeDtypeStruct((groups, 2 * pad, width), BF16),
        in_specs=[VMEM, VMEM],
        out_specs=VMEM,
        compiler_params=PARAMS,
    )(parts, place)


def finish_kernel(info_ref, part_ref, grad_ref, kl_ref):
    _, pad, width = grad_ref.shape
    parts = [part_ref[k].astype(F32) for k in range(part_ref.shape[0])]
    stats = []
    for part in parts:
        column = [part[:pad, width + k : width + k + 1] for k in range(9)]
        stats.append([column[k] + column[k + 1] + column[k + 2] for k in (0, 3, 6)])
    scale, shift, (lse, mean, t_lse) = merged(stats)
    grad = jnp.zeros((pad, width), F32)
    for part, a, b in zip(parts, scale, shift):
        grad += a * (part[:pad, :width] + b * part[pad:, :width])
    grad_ref[0] = grad.astype(BF16)
    kl = jnp.where(iota((pad, 1), 0) < info_ref[2], mean - lse + t_lse, 0.0)
    square = iota((pad, pad), 0) == iota((pad, pad), 1)
    kl_ref[...] = jnp.sum(jnp.where(square, kl, 0.0), axis=0, keepdims=True)


def finish(info, parts, width):
    pad = parts.shape[1] // 2
    return pl.pallas_call(
        finish_kernel,
        out_shape=[
            jax.ShapeDtypeStruct((1, pad, width), BF16),
            jax.ShapeDtypeStruct((1, pad), F32),
        ],
        in_specs=[SMEM, VMEM],
        out_specs=[VMEM, VMEM],
    )(info, parts)


def swap(value):
    return lax.ppermute(value, "c", ((0, 1), (1, 0)))


def some_rows(lanes, pad, t_width, width, operands):
    info, rows, t_place, s_place, teacher_head, student_head = operands
    ring = lax.axis_size("y")
    own = exchange(pack(rows, t_place, s_place, lanes, t_width, width, ring), "y")
    other = swap(own)
    t, s, *heads = first(info, own, teacher_head, student_head)
    keep, send = second(other, t, s, *heads)
    both = pair(info, keep, swap(send))
    return exchange(spread(exchange(both, "y"), s_place, pad), GRP)


def per_device(teacher_rows, student_rows, teacher_head, student_head, lengths, owner):
    groups = lax.axis_size(GRP)
    pad = student_rows.shape[1]
    t_width, s_width = teacher_rows.shape[2], student_rows.shape[2]
    group = lax.axis_index(GRP).astype(jnp.int32).reshape(1)
    core = lax.axis_index("c").astype(jnp.int32).reshape(1)
    mine, t_place, s_place, info = arrange(
        group, core, lengths, owner, teacher_rows, student_rows, groups
    )
    rows = exchange(mine, GRP).reshape(groups * pad, mine.shape[2])
    operands = (info, rows, t_place, s_place, teacher_head, student_head)
    branches = [functools.partial(some_rows, c, pad, t_width, t_width + s_width) for c in CAPACITIES]
    grad, divergence = finish(info, lax.switch(info[0], branches, operands), s_width)
    return divergence, grad


def solution(mesh):
    torus = Mesh(mesh.devices.reshape(4, 8, 8, 2), ("x", "z", "y", "c"))
    return jax.shard_map(
        per_device,
        mesh=torus,
        in_specs=(
            P(GRP, None, VOCAB),
            P(GRP, None, VOCAB),
            P(None, (*GRP, *VOCAB)),
            P(None, (*GRP, *VOCAB)),
            P(),
            P(),
        ),
        out_specs=(P(GRP, None), P(GRP, None, VOCAB)),
        check_vma=False,
    )
```

```python
import functools

import jax
import jax.numpy as jnp
from jax import lax
from jax.experimental import pallas as pl
from jax.experimental.pallas import tpu as pltpu
from jax.sharding import Mesh
from jax.sharding import PartitionSpec as P

GRP = ("x", "z")
Y = ("yh", "yl")
VOCAB = ("yh", "yl", "c")
NEAR = ("x", "yl")
REST = ("yh", "x", "z")
CAPACITIES = (128, 256)
F32 = jnp.float32
BF16 = jnp.bfloat16
VMEM = pl.BlockSpec(memory_space=pltpu.VMEM)
SMEM = pl.BlockSpec(memory_space=pltpu.SMEM)
PARAMS = pltpu.CompilerParams(vmem_limit_bytes=20 * 1024 * 1024)


def iota(shape, dim):
    return lax.broadcasted_iota(jnp.int32, shape, dim)


def exchange(pieces, axes):
    return lax.all_to_all(pieces, axes, 0, 0, tiled=True)


def arrange_kernel(
    group_ref, core_ref, lengths_ref, owner_ref, length_row_ref, owner_row_ref, teacher_ref, student_ref,
    out_ref, t_place_ref, s_place_ref, info_ref,
):
    count, pad, _ = out_ref.shape
    width = teacher_ref.shape[2]
    rest = out_ref.shape[2] - width - student_ref.shape[2]
    group = group_ref[0]
    share = lengths_ref.shape[0] // count
    first = lengths_ref[share * group]
    upper = teacher_ref[0].astype(F32)
    lower = pltpu.roll(teacher_ref[1].astype(F32), first, 0)
    chosen = jnp.where(iota(upper.shape, 0) < first, upper, lower).astype(BF16)
    for k in range(count):
        out_ref[k, :, :width] = chosen
        out_ref[k, :, width : width + student_ref.shape[2]] = student_ref[0]
        if rest:
            out_ref[k, :, -rest:] = jnp.zeros((pad, rest), BF16)

    live = jnp.int32(0)
    mine = jnp.int32(0)
    for k in range(lengths_ref.shape[0]):
        live += lengths_ref[k]
        mine += jnp.where(owner_ref[k] == group, lengths_ref[k], 0)
    which = jnp.int32(0)
    for c in CAPACITIES[:-1]:
        which += (live > c).astype(jnp.int32)
    info_ref[0] = which
    info_ref[1] = core_ref[0]
    info_ref[2] = mine

    slots = t_place_ref.shape[1]
    deep = length_row_ref.shape[1]

    def column(ref):
        one = jnp.broadcast_to(ref[...].astype(F32), (deep, deep)).T
        return jnp.broadcast_to(one[:, :1], (deep, slots))

    length, owner = column(length_row_ref), column(owner_row_ref)
    seq = iota((deep, slots), 0)
    home = (iota((deep, slots), 1) // pad)
    zero = jnp.zeros((deep, slots), F32)

    def total(mask, value):
        return jnp.sum(jnp.where(mask, value, zero), axis=0, keepdims=True)

    home_f = home.astype(F32)
    step = (iota((1, slots), 1) % pad).astype(F32)
    t_count = total(seq // share == home, length)
    t_owner = total(seq == share * home, owner)
    t_start = total(owner < t_owner, length)
    s_count = total(owner == home_f, length)
    s_start = total(owner < home_f, length)
    t_place = jnp.where(step < t_count, t_start + step, -1.0)
    s_place = jnp.where(step < s_count, s_start + step, -1.0)
    t_place_ref[...] = t_place.astype(jnp.int32)
    s_place_ref[...] = s_place.astype(jnp.int32)


def arrange(group, core, lengths, owner, teacher_rows, student_rows, count):
    pad = student_rows.shape[1]
    width = -(-(teacher_rows.shape[2] + student_rows.shape[2]) // 128) * 128
    return pl.pallas_call(
        arrange_kernel,
        out_shape=[
            jax.ShapeDtypeStruct((count, pad, width), BF16),
            jax.ShapeDtypeStruct((1, count * pad), jnp.int32),
            jax.ShapeDtypeStruct((1, count * pad), jnp.int32),
            jax.ShapeDtypeStruct((3,), jnp.int32),
        ],
        in_specs=[SMEM] * 4 + [VMEM] * 4,
        out_specs=[VMEM, VMEM, VMEM, SMEM],
    )(
        group,
        core,
        lengths,
        owner,
        lengths.reshape(1, -1),
        owner.reshape(1, -1),
        teacher_rows,
        student_rows,
    )


def pack_kernel(t_width, rows_ref, t_place_ref, s_place_ref, out_ref):
    count, half, _ = out_ref.shape
    slots = rows_ref.shape[0]
    width = out_ref.shape[2] // 2

    def packed(place_ref, first, stop):
        pick = (place_ref[...] == iota((2 * half, slots), 0)).astype(F32).astype(BF16)
        found = jnp.dot(pick, rows_ref[:, first:stop], preferred_element_type=F32)
        return found[:half], found[half:]

    main = (width - t_width) // 128 * 128
    t = packed(t_place_ref, 0, t_width)
    low, high = packed(s_place_ref, t_width, width)
    value = jnp.concatenate(
        [*t, low[:, :main], high[:, :main], low[:, main:], high[:, main:]], axis=1
    ).astype(BF16)
    for k in range(count):
        out_ref[k] = value


def pack(rows, t_place, s_place, lanes, t_width, width, count):
    return pl.pallas_call(
        functools.partial(pack_kernel, t_width),
        out_shape=jax.ShapeDtypeStruct((count, lanes // 2, 2 * width), BF16),
        in_specs=[VMEM] * 3,
        out_specs=VMEM,
        compiler_params=PARAMS,
    )(rows, t_place, s_place)


def in_parts(stats, lanes):
    row = iota((16, lanes), 0)
    table = jnp.zeros((16, lanes), F32)
    for k, value in enumerate(stats):
        for part in range(3):
            rounded = value.astype(BF16).astype(F32)
            table = jnp.where(row == 3 * k + part, rounded, table)
            value = value - rounded
    return table


def from_parts(table, lanes):
    rows = [table[k : k + 1, :lanes] for k in range(9)]
    return [rows[k] + rows[k + 1] + rows[k + 2] for k in (0, 3, 6)]


def merged(stats):
    lse, mean, t_lse = zip(*stats)
    high = functools.reduce(jnp.maximum, lse)
    t_high = functools.reduce(jnp.maximum, t_lse)
    scale = [jnp.exp(v - high) for v in lse]
    total = sum(scale[1:], scale[0])
    scale = [v / total for v in scale]
    middle = sum((a * v for a, v in zip(scale[1:], mean[1:])), scale[0] * mean[0])
    t_total = sum((jnp.exp(v - t_high) for v in t_lse[1:]), jnp.exp(t_lse[0] - t_high))
    shift = [v - middle for v in mean]
    return scale, shift, [high + jnp.log(total), middle, t_high + jnp.log(t_total)]


def soften(t, s, g_ref, stat_ref):
    lanes = g_ref.shape[1] // 2
    gap = s - t
    t_top = jnp.max(t, axis=0, keepdims=True)
    t_lse = t_top + jnp.log(jnp.sum(jnp.exp(t - t_top), axis=0, keepdims=True))
    s_top = jnp.max(s, axis=0, keepdims=True)
    p = jnp.exp(s - s_top)
    total = jnp.sum(p, axis=0, keepdims=True)
    p = p / total
    mean = jnp.sum(p * gap, axis=0, keepdims=True)
    g_ref[:, :lanes] = (p * (gap - mean)).astype(BF16)
    g_ref[:, lanes:] = p.astype(BF16)
    table = in_parts([s_top + jnp.log(total), mean, t_lse], lanes)
    stat_ref[...] = jnp.concatenate([table, table], axis=1).astype(BF16)


def product(rows_ref, t_head_ref, s_head_ref, t, s):
    t_size, s_size = t_head_ref.shape[1], s_head_ref.shape[1]
    main = s_size // 128 * 128

    def rows(k, first, size):
        low = rows_ref[k, :, first : first + size]
        high = rows_ref[k, :, first + size : first + 2 * size]
        return jnp.concatenate([low, high], axis=0)

    count = rows_ref.shape[0]
    batch = 4
    for start in range(0, count, batch):
        ids = range(start, start + batch)
        t += jnp.dot(
            jnp.concatenate([rows(k, 0, t_size) for k in ids], axis=1),
            jnp.concatenate([t_head_ref[k] for k in ids], axis=0),
            preferred_element_type=F32,
        )
        s += jnp.dot(
            jnp.concatenate(
                [rows(k, 2 * t_size, main) for k in ids]
                + [rows(k, 2 * (t_size + main), s_size - main) for k in ids],
                axis=1,
            ),
            jnp.concatenate(
                [s_head_ref[k, :main] for k in ids] + [s_head_ref[k, main:] for k in ids],
                axis=0,
            ),
            preferred_element_type=F32,
        )
    return t, s


def first_kernel(
    info_ref, own_ref, t_head_ref, s_head_ref, t_ref, s_ref,
    s_own_ref, t_other_ref, s_other_ref, t_own_ref, sems,
):
    core = info_ref[1]
    copies = [
        pltpu.make_async_copy(head.at[:, c], to, sems.at[k])
        for k, (head, c, to) in enumerate(
            (
                (t_head_ref, core, t_own_ref),
                (s_head_ref, core, s_own_ref),
                (t_head_ref, 1 - core, t_other_ref),
                (s_head_ref, 1 - core, s_other_ref),
            )
        )
    ]
    for copy in copies:
        copy.start()
    copies[0].wait()
    copies[1].wait()
    zero = jnp.zeros(t_ref.shape, F32)
    t, s = product(own_ref, t_own_ref, s_own_ref, zero, zero)
    t_ref[...] = t
    s_ref[...] = s
    copies[2].wait()
    copies[3].wait()


def first(info, own, t_head, s_head):
    count, half_rows, width = own.shape
    vocab = t_head.shape[1]
    t_head = t_head.reshape(count, 2, -1, vocab)
    s_head = s_head.reshape(count, 2, -1, vocab)
    logit = jax.ShapeDtypeStruct((2 * half_rows, vocab), F32)
    t_part = (count, *t_head.shape[2:])
    s_part = (count, *s_head.shape[2:])
    return pl.pallas_call(
        first_kernel,
        out_shape=[
            logit,
            logit,
            jax.ShapeDtypeStruct(s_part, BF16),
            jax.ShapeDtypeStruct(t_part, BF16),
            jax.ShapeDtypeStruct(s_part, BF16),
        ],
        in_specs=[SMEM, VMEM] + [pl.BlockSpec(memory_space=pl.ANY)] * 2,
        out_specs=[VMEM] * 5,
        scratch_shapes=[pltpu.VMEM(t_part, BF16), pltpu.SemaphoreType.DMA((4,))],
        compiler_params=PARAMS,
        cost_estimate=pl.CostEstimate(
            flops=2 * own.size * vocab, bytes_accessed=4 * (t_head.size + s_head.size), transcendentals=0
        ),
    )(info, own, t_head, s_head)


def second_kernel(
    other_ref, t_ref, s_ref, s_own_ref, t_other_ref, s_other_ref, keep_ref, send_ref, g_ref, stat_ref
):
    t, s = product(other_ref, t_other_ref, s_other_ref, t_ref[...], s_ref[...])
    soften(t.T, s.T, g_ref, stat_ref)
    half = s_own_ref.shape[1]
    for k in range(keep_ref.shape[0]):
        for head_ref, out_ref in ((s_own_ref, keep_ref), (s_other_ref, send_ref)):
            out_ref[k, :half] = jnp.dot(
                head_ref[k], g_ref[...], preferred_element_type=F32
            ).astype(BF16)
            out_ref[k, half:] = stat_ref[...]


def second(other, t, s, s_own, t_other, s_other):
    lanes, vocab = t.shape
    count, half, _ = s_own.shape
    part = jax.ShapeDtypeStruct((count, half + 16, 2 * lanes), BF16)
    return pl.pallas_call(
        second_kernel,
        out_shape=[part, part],
        in_specs=[VMEM] * 6,
        out_specs=[VMEM] * 2,
        scratch_shapes=[
            pltpu.VMEM((vocab, 2 * lanes), BF16),
            pltpu.VMEM((16, 2 * lanes), BF16),
        ],
        compiler_params=PARAMS,
    )(other, t, s, s_own, t_other, s_other)


def pair_kernel(parts, info_ref, keep_ref, came_ref, out_ref):
    lanes = out_ref.shape[2] // 2
    half = keep_ref.shape[1] - 16
    low = info_ref[1] == 0
    kept = keep_ref[0, half:].astype(F32)
    come = came_ref[0, half:].astype(F32)
    first = jnp.where(low, kept, come)
    second = jnp.where(low, come, kept)
    scale, shift, stats = merged([from_parts(first, lanes), from_parts(second, lanes)])
    table = in_parts(stats, lanes)
    table = jnp.concatenate([table, table], axis=1).astype(BF16)
    own, other = (jnp.where(low, scale[0], scale[1]), jnp.where(low, scale[1], scale[0]))
    own_shift, other_shift = (
        own * jnp.where(low, shift[0], shift[1]),
        other * jnp.where(low, shift[1], shift[0]),
    )
    per = half // parts
    near = out_ref.shape[0] // parts
    last = out_ref.shape[1] - 16
    for k in range(keep_ref.shape[0]):
        a = own * keep_ref[k, :half, :lanes].astype(F32)
        a += other * came_ref[k, :half, :lanes].astype(F32)
        b_own = keep_ref[k, :half, lanes:].astype(F32)
        b_other = came_ref[k, :half, lanes:].astype(F32)
        a += own_shift * b_own + other_shift * b_other
        both = jnp.concatenate([a, own * b_own + other * b_other], axis=1).astype(BF16)
        first = k // near * per
        for q in range(parts):
            piece = both[q * per : (q + 1) * per]
            out_ref[q * near + k % near, first : first + per] = piece
    for k in range(out_ref.shape[0]):
        out_ref[k, last:] = table


def pair(info, keep, came, parts, near):
    ring, deep, width = keep.shape
    deep = (deep - 16) // parts * (ring // near) + 16
    return pl.pallas_call(
        functools.partial(pair_kernel, parts),
        out_shape=jax.ShapeDtypeStruct((parts * near, deep, width), BF16),
        in_specs=[SMEM, VMEM, VMEM],
        out_specs=VMEM,
        compiler_params=PARAMS,
    )(info, keep, came)


def spread_kernel(part_ref, place_ref, out_ref):
    lanes = part_ref.shape[2] // 2
    half = part_ref.shape[1] - 16
    count = part_ref.shape[0]
    slots = place_ref.shape[1]
    pad = out_ref.shape[1] // 2
    width = out_ref.shape[2]
    groups = slots // pad
    far = out_ref.shape[0] // groups
    per = half // far
    scale, shift, stats = merged(
        [from_parts(part_ref[k, half:].astype(F32), lanes) for k in range(count)]
    )
    a = jnp.zeros((half, lanes), F32)
    b = jnp.zeros((half, lanes), F32)
    for k in range(count):
        b_one = part_ref[k, :half, lanes:].astype(F32)
        a += scale[k] * part_ref[k, :half, :lanes].astype(F32) + (scale[k] * shift[k]) * b_one
        b += scale[k] * b_one
    rest = jnp.zeros((width - per - 16, lanes), F32)
    table = jnp.concatenate([in_parts(stats, lanes), rest], axis=0)
    pick = (place_ref[...] == iota((lanes, slots), 0)).astype(F32).T.astype(BF16)

    def found(value):
        pieces = []
        for k in range(far):
            pieces += [value[k * per : (k + 1) * per], table]
        return lax.dot_general(
            pick,
            jnp.concatenate(pieces, axis=0).astype(BF16),
            (((1,), (1,)), ((), ())),
            preferred_element_type=F32,
        )

    a, b = found(a), found(b)
    for k in range(far):
        both = [v[:, k * width : (k + 1) * width].reshape(groups, pad, width) for v in (a, b)]
        out_ref[k * groups : (k + 1) * groups] = jnp.concatenate(both, axis=1).astype(BF16)


def spread(parts, place, pad, far):
    groups = place.shape[1] // pad
    per = (parts.shape[1] - 16) // far
    width = -(-(per + 16) // 128) * 128
    return pl.pallas_call(
        spread_kernel,
        out_shape=jax.ShapeDtypeStruct((far * groups, 2 * pad, width), BF16),
        in_specs=[VMEM, VMEM],
        out_specs=VMEM,
        compiler_params=PARAMS,
    )(parts, place)


def finish_kernel(far, near, info_ref, part_ref, grad_ref, kl_ref):
    _, pad, width = grad_ref.shape
    per = width // near
    groups = part_ref.shape[0] // far
    share = groups // near

    def source(q):
        return [f * groups + q * share + k for f in range(far) for k in range(share)]

    stats = []
    for k in source(0):
        part = part_ref[k].astype(F32)[:pad]
        column = [part[:, per + j : per + j + 1] for j in range(9)]
        stats.append([column[j] + column[j + 1] + column[j + 2] for j in (0, 3, 6)])
    scale, shift, (lse, mean, t_lse) = merged(stats)
    pieces = []
    for q in range(near):
        grad = jnp.zeros((pad, part_ref.shape[2]), F32)
        for k, a, b in zip(source(q), scale, shift):
            part = part_ref[k].astype(F32)
            grad += a * (part[:pad] + b * part[pad:])
        pieces.append(grad[:, :per])
    grad_ref[0] = jnp.concatenate(pieces, axis=1).astype(BF16)
    kl = jnp.where(iota((pad, 1), 0) < info_ref[2], mean - lse + t_lse, 0.0)
    square = iota((pad, pad), 0) == iota((pad, pad), 1)
    kl_ref[...] = jnp.sum(jnp.where(square, kl, 0.0), axis=0, keepdims=True)


def finish(info, parts, width, far, near):
    pad = parts.shape[1] // 2
    return pl.pallas_call(
        functools.partial(finish_kernel, far, near),
        out_shape=[
            jax.ShapeDtypeStruct((1, pad, width), BF16),
            jax.ShapeDtypeStruct((1, pad), F32),
        ],
        in_specs=[SMEM, VMEM],
        out_specs=[VMEM, VMEM],
    )(info, parts)


def swap(value):
    return lax.ppermute(value, "c", ((0, 1), (1, 0)))


def some_rows(lanes, pad, t_width, width, operands):
    info, rows, t_place, s_place, teacher_head, student_head = operands
    own = exchange(pack(rows, t_place, s_place, lanes, t_width, width, lax.axis_size(Y)), Y)
    other = swap(own)
    t, s, *heads = first(info, own, teacher_head, student_head)
    keep, send = second(other, t, s, *heads)
    both = pair(info, keep, swap(send), lax.axis_size("x"), lax.axis_size("yl"))
    return exchange(spread(exchange(both, NEAR), s_place, pad, lax.axis_size("yh")), REST)


def per_device(teacher_rows, student_rows, teacher_head, student_head, lengths, owner):
    groups = lax.axis_size(GRP)
    pad = student_rows.shape[1]
    t_width, s_width = teacher_rows.shape[2], student_rows.shape[2]
    group = lax.axis_index(GRP).astype(jnp.int32).reshape(1)
    core = lax.axis_index("c").astype(jnp.int32).reshape(1)
    mine, t_place, s_place, info = arrange(
        group, core, lengths, owner, teacher_rows, student_rows, groups
    )
    rows = exchange(mine, GRP).reshape(groups * pad, mine.shape[2])
    operands = (info, rows, t_place, s_place, teacher_head, student_head)
    branches = [functools.partial(some_rows, c, pad, t_width, t_width + s_width) for c in CAPACITIES]
    parts = lax.switch(info[0], branches, operands)
    grad, divergence = finish(info, parts, s_width, lax.axis_size("yh"), lax.axis_size("x"))
    return divergence, grad


def solution(mesh):
    torus = Mesh(mesh.devices.reshape(4, 8, 4, 2, 2), ("x", "z", "yh", "yl", "c"))
    return jax.shard_map(
        per_device,
        mesh=torus,
        in_specs=(
            P(GRP, None, VOCAB),
            P(GRP, None, VOCAB),
            P(None, (*GRP, *VOCAB)),
            P(None, (*GRP, *VOCAB)),
            P(),
            P(),
        ),
        out_specs=(P(GRP, None), P(GRP, None, VOCAB)),
        check_vma=False,
    )
```

```python
import functools

import jax
import jax.numpy as jnp
from jax import lax
from jax.experimental import pallas as pl
from jax.experimental.pallas import tpu as pltpu
from jax.sharding import Mesh
from jax.sharding import PartitionSpec as P

GRP = ("x", "z")
Y = ("yh", "yl")
VOCAB = ("yh", "yl", "c")
NEAR = ("x", "yl")
REST = ("yh", "x", "z")
CAPACITIES = ((128, 128), (160, 192), (256, 256))
F32 = jnp.float32
BF16 = jnp.bfloat16
VMEM = pl.BlockSpec(memory_space=pltpu.VMEM)
SMEM = pl.BlockSpec(memory_space=pltpu.SMEM)
PARAMS = pltpu.CompilerParams(vmem_limit_bytes=20 * 1024 * 1024)


def iota(shape, dim):
    return lax.broadcasted_iota(jnp.int32, shape, dim)


def exchange(pieces, axes):
    return lax.all_to_all(pieces, axes, 0, 0, tiled=True)


def arrange_kernel(group_ref, lengths_ref, teacher_ref, student_ref, out_ref):
    count, pad, _ = out_ref.shape
    width = teacher_ref.shape[2]
    rest = out_ref.shape[2] - width - student_ref.shape[2]
    share = lengths_ref.shape[0] // count
    first = lengths_ref[share * group_ref[0]]
    upper = teacher_ref[0].astype(F32)
    lower = pltpu.roll(teacher_ref[1].astype(F32), first, 0)
    chosen = jnp.where(iota(upper.shape, 0) < first, upper, lower).astype(BF16)
    for k in range(count):
        out_ref[k, :, :width] = chosen
        out_ref[k, :, width : width + student_ref.shape[2]] = student_ref[0]
        if rest:
            out_ref[k, :, -rest:] = jnp.zeros((pad, rest), BF16)


def arrange(group, lengths, teacher_rows, student_rows, count):
    pad = student_rows.shape[1]
    width = -(-(teacher_rows.shape[2] + student_rows.shape[2]) // 128) * 128
    return pl.pallas_call(
        arrange_kernel,
        out_shape=jax.ShapeDtypeStruct((count, pad, width), BF16),
        in_specs=[SMEM] * 2 + [VMEM] * 2,
        out_specs=VMEM,
    )(group, lengths, teacher_rows, student_rows)


def routing_kernel(
    pad, group_ref, core_ref, lengths_ref, owner_ref, length_row_ref, owner_row_ref,
    t_place_ref, s_place_ref, info_ref,
):
    group = group_ref[0]
    live = jnp.int32(0)
    mine = jnp.int32(0)
    for k in range(lengths_ref.shape[0]):
        live += lengths_ref[k]
        mine += jnp.where(owner_ref[k] == group, lengths_ref[k], 0)
    which = jnp.int32(0)
    for c, _ in CAPACITIES[:-1]:
        which += (live > c).astype(jnp.int32)
    info_ref[0] = which
    info_ref[1] = core_ref[0]
    info_ref[2] = mine

    slots = t_place_ref.shape[1]
    deep = length_row_ref.shape[1]
    share = deep * pad // slots

    def column(ref):
        one = jnp.broadcast_to(ref[...].astype(F32), (deep, deep)).T
        return jnp.broadcast_to(one[:, :1], (deep, slots))

    length, owner = column(length_row_ref), column(owner_row_ref)
    seq = iota((deep, slots), 0)
    home = iota((deep, slots), 1) // pad
    zero = jnp.zeros((deep, slots), F32)

    def total(mask, value):
        return jnp.sum(jnp.where(mask, value, zero), axis=0, keepdims=True)

    home_f = home.astype(F32)
    step = (iota((1, slots), 1) % pad).astype(F32)
    t_count = total(seq // share == home, length)
    t_owner = total(seq == share * home, owner)
    t_start = total(owner < t_owner, length)
    s_count = total(owner == home_f, length)
    s_start = total(owner < home_f, length)
    t_place = jnp.where(step < t_count, t_start + step, -1.0)
    s_place = jnp.where(step < s_count, s_start + step, -1.0)
    t_place_ref[...] = t_place.astype(jnp.int32)
    s_place_ref[...] = s_place.astype(jnp.int32)


def routing(group, core, lengths, owner, slots, pad):
    return pl.pallas_call(
        functools.partial(routing_kernel, pad),
        out_shape=[
            jax.ShapeDtypeStruct((1, slots), jnp.int32),
            jax.ShapeDtypeStruct((1, slots), jnp.int32),
            jax.ShapeDtypeStruct((3,), jnp.int32),
        ],
        in_specs=[SMEM] * 4 + [VMEM] * 2,
        out_specs=[VMEM, VMEM, SMEM],
        cost_estimate=pl.CostEstimate(flops=10**6, bytes_accessed=10**6, transcendentals=0),
    )(group, core, lengths, owner, lengths.reshape(1, -1), owner.reshape(1, -1))


def pack_kernel(t_width, rows_ref, t_place_ref, s_place_ref, out_ref):
    count, half, _ = out_ref.shape
    slots = rows_ref.shape[0]
    width = out_ref.shape[2] // 2

    def packed(place_ref, first, stop):
        pick = (place_ref[...] == iota((2 * half, slots), 0)).astype(F32).astype(BF16)
        found = jnp.dot(pick, rows_ref[:, first:stop], preferred_element_type=F32)
        return found[:half], found[half:]

    main = (width - t_width) // 128 * 128
    t = packed(t_place_ref, 0, t_width)
    low, high = packed(s_place_ref, t_width, width)
    value = jnp.concatenate(
        [*t, low[:, :main], high[:, :main], low[:, main:], high[:, main:]], axis=1
    ).astype(BF16)
    for k in range(count):
        out_ref[k] = value


def pack(rows, t_place, s_place, lanes, t_width, width, count):
    return pl.pallas_call(
        functools.partial(pack_kernel, t_width),
        out_shape=jax.ShapeDtypeStruct((count, lanes // 2, 2 * width), BF16),
        in_specs=[VMEM] * 3,
        out_specs=VMEM,
        compiler_params=PARAMS,
    )(rows, t_place, s_place)


def in_parts(stats, lanes):
    row = iota((16, lanes), 0)
    table = jnp.zeros((16, lanes), F32)
    for k, value in enumerate(stats):
        for part in range(3):
            rounded = value.astype(BF16).astype(F32)
            table = jnp.where(row == 3 * k + part, rounded, table)
            value = value - rounded
    return table


def from_parts(table, lanes):
    rows = [table[k : k + 1, :lanes] for k in range(9)]
    return [rows[k] + rows[k + 1] + rows[k + 2] for k in (0, 3, 6)]


def merged(stats):
    lse, mean, t_lse = zip(*stats)
    high = functools.reduce(jnp.maximum, lse)
    t_high = functools.reduce(jnp.maximum, t_lse)
    scale = [jnp.exp(v - high) for v in lse]
    total = sum(scale[1:], scale[0])
    scale = [v / total for v in scale]
    middle = sum((a * v for a, v in zip(scale[1:], mean[1:])), scale[0] * mean[0])
    t_total = sum((jnp.exp(v - t_high) for v in t_lse[1:]), jnp.exp(t_lse[0] - t_high))
    shift = [v - middle for v in mean]
    return scale, shift, [high + jnp.log(total), middle, t_high + jnp.log(t_total)]


def soften(t, s, g_ref, stat_ref):
    lanes = g_ref.shape[1] // 2
    gap = s - t
    t_top = jnp.max(t, axis=0, keepdims=True)
    t_lse = t_top + jnp.log(jnp.sum(jnp.exp(t - t_top), axis=0, keepdims=True))
    s_top = jnp.max(s, axis=0, keepdims=True)
    p = jnp.exp(s - s_top)
    total = jnp.sum(p, axis=0, keepdims=True)
    p = p / total
    mean = jnp.sum(p * gap, axis=0, keepdims=True)
    g_ref[...] = jnp.concatenate([p * (gap - mean), p], axis=1).astype(BF16)
    table = in_parts([s_top + jnp.log(total), mean, t_lse], lanes)
    stat_ref[...] = jnp.concatenate([table, table], axis=1).astype(BF16)


def product(rows_ref, t_head_ref, s_head_ref, t, s):
    t_size, s_size = t_head_ref.shape[1], s_head_ref.shape[1]
    main = s_size // 128 * 128

    def rows(k, first, size):
        low = rows_ref[k, :, first : first + size]
        high = rows_ref[k, :, first + size : first + 2 * size]
        return jnp.concatenate([low, high], axis=0)

    count = rows_ref.shape[0]
    batch = 4
    for start in range(0, count, batch):
        ids = range(start, start + batch)
        t += jnp.dot(
            jnp.concatenate([rows(k, 0, t_size) for k in ids], axis=1),
            jnp.concatenate([t_head_ref[k] for k in ids], axis=0),
            preferred_element_type=F32,
        )
        s += jnp.dot(
            jnp.concatenate(
                [rows(k, 2 * t_size, main) for k in ids]
                + [rows(k, 2 * (t_size + main), s_size - main) for k in ids],
                axis=1,
            ),
            jnp.concatenate(
                [s_head_ref[k, :main] for k in ids] + [s_head_ref[k, main:] for k in ids],
                axis=0,
            ),
            preferred_element_type=F32,
        )
    return t, s


def first_kernel(
    info_ref, own_ref, t_head_ref, s_head_ref, t_ref, s_ref,
    s_own_ref, t_other_ref, s_other_ref, t_own_ref, sems,
):
    core = info_ref[1]
    copies = [
        pltpu.make_async_copy(head.at[:, c], to, sems.at[k])
        for k, (head, c, to) in enumerate(
            (
                (t_head_ref, core, t_own_ref),
                (s_head_ref, core, s_own_ref),
                (t_head_ref, 1 - core, t_other_ref),
                (s_head_ref, 1 - core, s_other_ref),
            )
        )
    ]
    for copy in copies:
        copy.start()
    copies[0].wait()
    copies[1].wait()
    zero = jnp.zeros(t_ref.shape, F32)
    t, s = product(own_ref, t_own_ref, s_own_ref, zero, zero)
    t_ref[...] = t
    s_ref[...] = s
    copies[2].wait()
    copies[3].wait()


def first(info, own, t_head, s_head):
    count, half_rows, width = own.shape
    vocab = t_head.shape[1]
    t_head = t_head.reshape(count, 2, -1, vocab)
    s_head = s_head.reshape(count, 2, -1, vocab)
    logit = jax.ShapeDtypeStruct((2 * half_rows, vocab), F32)
    t_part = (count, *t_head.shape[2:])
    s_part = (count, *s_head.shape[2:])
    return pl.pallas_call(
        first_kernel,
        out_shape=[
            logit,
            logit,
            jax.ShapeDtypeStruct(s_part, BF16),
            jax.ShapeDtypeStruct(t_part, BF16),
            jax.ShapeDtypeStruct(s_part, BF16),
        ],
        in_specs=[SMEM, VMEM] + [pl.BlockSpec(memory_space=pl.ANY)] * 2,
        out_specs=[VMEM] * 5,
        scratch_shapes=[pltpu.VMEM(t_part, BF16), pltpu.SemaphoreType.DMA((4,))],
        compiler_params=PARAMS,
        cost_estimate=pl.CostEstimate(
            flops=2 * own.size * vocab, bytes_accessed=4 * (t_head.size + s_head.size), transcendentals=0
        ),
    )(info, own, t_head, s_head)


def second_kernel(
    other_ref, t_ref, s_ref, s_own_ref, t_other_ref, s_other_ref, keep_ref, send_ref, g_ref, stat_ref
):
    t, s = product(other_ref, t_other_ref, s_other_ref, t_ref[...], s_ref[...])
    count, lanes = t.shape[0], g_ref.shape[1] // 2

    def turned(value):
        rest = -count % 128
        if rest:
            value = jnp.concatenate([value, jnp.zeros((rest, value.shape[1]), F32)], axis=0)
        return value.T[:, :lanes]

    soften(turned(t), turned(s), g_ref, stat_ref)
    half = s_own_ref.shape[1]
    for k in range(keep_ref.shape[0]):
        for head_ref, out_ref in ((s_own_ref, keep_ref), (s_other_ref, send_ref)):
            out_ref[k, :half] = jnp.dot(
                head_ref[k], g_ref[...], preferred_element_type=F32
            ).astype(BF16)
            out_ref[k, half:] = stat_ref[...]


def second(other, t, s, s_own, t_other, s_other, lanes):
    vocab = t.shape[1]
    count, half, _ = s_own.shape
    part = jax.ShapeDtypeStruct((count, half + 16, 2 * lanes), BF16)
    return pl.pallas_call(
        second_kernel,
        out_shape=[part, part],
        in_specs=[VMEM] * 6,
        out_specs=[VMEM] * 2,
        scratch_shapes=[
            pltpu.VMEM((vocab, 2 * lanes), BF16),
            pltpu.VMEM((16, 2 * lanes), BF16),
        ],
        compiler_params=PARAMS,
    )(other, t, s, s_own, t_other, s_other)


def pair_kernel(parts, info_ref, keep_ref, came_ref, out_ref):
    lanes = out_ref.shape[2] // 2
    half = keep_ref.shape[1] - 16
    low = info_ref[1] == 0
    kept = keep_ref[0, half:].astype(F32)
    come = came_ref[0, half:].astype(F32)
    first = jnp.where(low, kept, come)
    second = jnp.where(low, come, kept)
    scale, shift, stats = merged([from_parts(first, lanes), from_parts(second, lanes)])
    table = in_parts(stats, lanes)
    table = jnp.concatenate([table, table], axis=1).astype(BF16)
    own, other = (jnp.where(low, scale[0], scale[1]), jnp.where(low, scale[1], scale[0]))
    own_shift, other_shift = (
        own * jnp.where(low, shift[0], shift[1]),
        other * jnp.where(low, shift[1], shift[0]),
    )
    per = half // parts
    near = out_ref.shape[0] // parts
    last = out_ref.shape[1] - 16
    for k in range(keep_ref.shape[0]):
        kept, come = keep_ref[k, :half].astype(F32), came_ref[k, :half].astype(F32)
        a = own * kept[:, :lanes] + other * come[:, :lanes]
        b_own, b_other = kept[:, lanes:], come[:, lanes:]
        a += own_shift * b_own + other_shift * b_other
        both = jnp.concatenate([a, own * b_own + other * b_other], axis=1).astype(BF16)
        first = k // near * per
        for q in range(parts):
            piece = both[q * per : (q + 1) * per]
            out_ref[q * near + k % near, first : first + per] = piece
    for k in range(out_ref.shape[0]):
        out_ref[k, last:] = table


def pair(info, keep, came, parts, near):
    ring, deep, width = keep.shape
    deep = (deep - 16) // parts * (ring // near) + 16
    return pl.pallas_call(
        functools.partial(pair_kernel, parts),
        out_shape=jax.ShapeDtypeStruct((parts * near, deep, width), BF16),
        in_specs=[SMEM, VMEM, VMEM],
        out_specs=VMEM,
        compiler_params=PARAMS,
    )(info, keep, came)


def spread_kernel(part_ref, place_ref, out_ref):
    lanes = part_ref.shape[2] // 2
    half = part_ref.shape[1] - 16
    count = part_ref.shape[0]
    slots = place_ref.shape[1]
    pad = out_ref.shape[1] // 2
    width = out_ref.shape[2]
    groups = slots // pad
    far = out_ref.shape[0] // groups
    per = half // far
    scale, shift, stats = merged(
        [from_parts(part_ref[k, half:].astype(F32), lanes) for k in range(count)]
    )
    a = jnp.zeros((half, lanes), F32)
    b = jnp.zeros((half, lanes), F32)
    for k in range(count):
        one = part_ref[k, :half].astype(F32)
        b_one = one[:, lanes:]
        a += scale[k] * one[:, :lanes] + (scale[k] * shift[k]) * b_one
        b += scale[k] * b_one
    rest = jnp.zeros((width - per - 16, lanes), F32)
    table = jnp.concatenate([in_parts(stats, lanes), rest], axis=0)
    tall = -(-lanes // 128) * 128
    pick = (place_ref[...] == iota((tall, slots), 0)).astype(F32).T[:, :lanes].astype(BF16)

    def found(value):
        pieces = []
        for k in range(far):
            pieces += [value[k * per : (k + 1) * per], table]
        return lax.dot_general(
            pick,
            jnp.concatenate(pieces, axis=0).astype(BF16),
            (((1,), (1,)), ((), ())),
            preferred_element_type=F32,
        )

    a, b = found(a), found(b)
    for k in range(far):
        both = [v[:, k * width : (k + 1) * width].reshape(groups, pad, width) for v in (a, b)]
        out_ref[k * groups : (k + 1) * groups] = jnp.concatenate(both, axis=1).astype(BF16)


def spread(parts, place, pad, far):
    groups = place.shape[1] // pad
    per = (parts.shape[1] - 16) // far
    width = -(-(per + 16) // 128) * 128
    return pl.pallas_call(
        spread_kernel,
        out_shape=jax.ShapeDtypeStruct((far * groups, 2 * pad, width), BF16),
        in_specs=[VMEM, VMEM],
        out_specs=VMEM,
        compiler_params=PARAMS,
    )(parts, place)


def finish_kernel(far, near, info_ref, part_ref, grad_ref, kl_ref):
    _, pad, width = grad_ref.shape
    per = width // near
    groups = part_ref.shape[0] // far
    share = groups // near

    def source(q):
        return [f * groups + q * share + k for f in range(far) for k in range(share)]

    wide = part_ref.shape[2]

    def moved(value, by):
        return pltpu.roll(value, by % wide, 1)

    tables = []
    for k in source(0):
        part = part_ref[k].astype(F32)[:pad]
        tables.append(part + moved(part, -1) + moved(part, -2))
    high = functools.reduce(jnp.maximum, tables)
    weight = [jnp.exp(v - high) for v in tables]
    total = functools.reduce(jnp.add, weight)
    weight = [w / total for w in weight]
    mean = functools.reduce(jnp.add, [moved(w, 3) * v for w, v in zip(weight, tables)])
    scale = [w[:, per : per + 1] for w in weight]
    shift = [(v - mean)[:, per + 3 : per + 4] for v in tables]
    lse = high + jnp.log(total)
    lse, t_lse, mean = lse[:, per : per + 1], lse[:, per + 6 : per + 7], mean[:, per + 3 : per + 4]
    pieces = []
    for q in range(near):
        grad = jnp.zeros((pad, part_ref.shape[2]), F32)
        for k, a, b in zip(source(q), scale, shift):
            part = part_ref[k].astype(F32)
            grad += a * (part[:pad] + b * part[pad:])
        pieces.append(grad[:, :per])
    grad_ref[0] = jnp.concatenate(pieces, axis=1).astype(BF16)
    kl = jnp.where(iota((pad, 1), 0) < info_ref[2], mean - lse + t_lse, 0.0)
    square = iota((pad, pad), 0) == iota((pad, pad), 1)
    kl_ref[...] = jnp.sum(jnp.where(square, kl, 0.0), axis=0, keepdims=True)


def finish(info, parts, width, far, near):
    pad = parts.shape[1] // 2
    return pl.pallas_call(
        functools.partial(finish_kernel, far, near),
        out_shape=[
            jax.ShapeDtypeStruct((1, pad, width), BF16),
            jax.ShapeDtypeStruct((1, pad), F32),
        ],
        in_specs=[SMEM, VMEM],
        out_specs=[VMEM, VMEM],
    )(info, parts)


def swap(value):
    return lax.ppermute(value, "c", ((0, 1), (1, 0)))


def some_rows(count, lanes, pad, t_width, width, operands):
    info, rows, t_place, s_place, teacher_head, student_head = operands
    own = exchange(pack(rows, t_place, s_place, count, t_width, width, lax.axis_size(Y)), Y)
    other = swap(own)
    t, s, *heads = first(info, own, teacher_head, student_head)
    keep, send = second(other, t, s, *heads, lanes)
    both = pair(info, keep, swap(send), lax.axis_size("x"), lax.axis_size("yl"))
    return exchange(spread(exchange(both, NEAR), s_place, pad, lax.axis_size("yh")), REST)


def per_device(teacher_rows, student_rows, teacher_head, student_head, lengths, owner):
    groups = lax.axis_size(GRP)
    pad = student_rows.shape[1]
    t_width, s_width = teacher_rows.shape[2], student_rows.shape[2]
    group = lax.axis_index(GRP).astype(jnp.int32).reshape(1)
    core = lax.axis_index("c").astype(jnp.int32).reshape(1)
    mine = arrange(group, lengths, teacher_rows, student_rows, groups)
    t_place, s_place, info = routing(group, core, lengths, owner, groups * pad, pad)
    rows = exchange(mine, GRP).reshape(groups * pad, mine.shape[2])
    operands = (info, rows, t_place, s_place, teacher_head, student_head)
    branches = [functools.partial(some_rows, *c, pad, t_width, t_width + s_width) for c in CAPACITIES]
    parts = lax.switch(info[0], branches, operands)
    grad, divergence = finish(info, parts, s_width, lax.axis_size("yh"), lax.axis_size("x"))
    return divergence, grad


def solution(mesh):
    torus = Mesh(mesh.devices.reshape(4, 8, 4, 2, 2), ("x", "z", "yh", "yl", "c"))
    return jax.shard_map(
        per_device,
        mesh=torus,
        in_specs=(
            P(GRP, None, VOCAB),
            P(GRP, None, VOCAB),
            P(None, (*GRP, *VOCAB)),
            P(None, (*GRP, *VOCAB)),
            P(),
            P(),
        ),
        out_specs=(P(GRP, None), P(GRP, None, VOCAB)),
        check_vma=False,
    )
```

```python
import functools

import jax
import jax.numpy as jnp
from jax import lax
from jax.experimental import pallas as pl
from jax.experimental.pallas import tpu as pltpu
from jax.sharding import Mesh
from jax.sharding import PartitionSpec as P

GRP = ("x", "z")
VOCAB = ("y", "c")
CAPACITIES = ((128, 128), (160, 192), (256, 256))
F32 = jnp.float32
BF16 = jnp.bfloat16
VMEM = pl.BlockSpec(memory_space=pltpu.VMEM)
SMEM = pl.BlockSpec(memory_space=pltpu.SMEM)
PARAMS = pltpu.CompilerParams(vmem_limit_bytes=20 * 1024 * 1024)


def iota(shape, dim):
    return lax.broadcasted_iota(jnp.int32, shape, dim)


def exchange(pieces, axes):
    return lax.all_to_all(pieces, axes, 0, 0, tiled=True)


def arrange_kernel(group_ref, lengths_ref, teacher_ref, student_ref, out_ref):
    count, pad, _ = out_ref.shape
    width = teacher_ref.shape[2]
    rest = out_ref.shape[2] - width - student_ref.shape[2]
    share = lengths_ref.shape[0] // count
    first = lengths_ref[share * group_ref[0]]
    upper = teacher_ref[0].astype(F32)
    lower = pltpu.roll(teacher_ref[1].astype(F32), first, 0)
    chosen = jnp.where(iota(upper.shape, 0) < first, upper, lower).astype(BF16)
    for k in range(count):
        out_ref[k, :, :width] = chosen
        out_ref[k, :, width : width + student_ref.shape[2]] = student_ref[0]
        if rest:
            out_ref[k, :, -rest:] = jnp.zeros((pad, rest), BF16)


def arrange(group, lengths, teacher_rows, student_rows, count):
    pad = student_rows.shape[1]
    width = -(-(teacher_rows.shape[2] + student_rows.shape[2]) // 128) * 128
    return pl.pallas_call(
        arrange_kernel,
        out_shape=jax.ShapeDtypeStruct((count, pad, width), BF16),
        in_specs=[SMEM] * 2 + [VMEM] * 2,
        out_specs=VMEM,
    )(group, lengths, teacher_rows, student_rows)


def routing_kernel(
    pad, group_ref, core_ref, lengths_ref, owner_ref, length_row_ref, owner_row_ref,
    t_place_ref, s_place_ref, info_ref,
):
    group = group_ref[0]
    live = jnp.int32(0)
    mine = jnp.int32(0)
    for k in range(lengths_ref.shape[0]):
        live += lengths_ref[k]
        mine += jnp.where(owner_ref[k] == group, lengths_ref[k], 0)
    which = jnp.int32(0)
    for c, _ in CAPACITIES[:-1]:
        which += (live > c).astype(jnp.int32)
    info_ref[0] = which
    info_ref[1] = core_ref[0]
    info_ref[2] = mine

    slots = t_place_ref.shape[1]
    deep = length_row_ref.shape[1]
    share = deep * pad // slots

    def column(ref):
        one = jnp.broadcast_to(ref[...].astype(F32), (deep, deep)).T
        return jnp.broadcast_to(one[:, :1], (deep, slots))

    length, owner = column(length_row_ref), column(owner_row_ref)
    seq = iota((deep, slots), 0)
    home = iota((deep, slots), 1) // pad
    zero = jnp.zeros((deep, slots), F32)

    def total(mask, value):
        return jnp.sum(jnp.where(mask, value, zero), axis=0, keepdims=True)

    home_f = home.astype(F32)
    step = (iota((1, slots), 1) % pad).astype(F32)
    t_count = total(seq // share == home, length)
    t_owner = total(seq == share * home, owner)
    t_start = total(owner < t_owner, length)
    s_count = total(owner == home_f, length)
    s_start = total(owner < home_f, length)
    t_place = jnp.where(step < t_count, t_start + step, -1.0)
    s_place = jnp.where(step < s_count, s_start + step, -1.0)
    t_place_ref[...] = t_place.astype(jnp.int32)
    s_place_ref[...] = s_place.astype(jnp.int32)


def routing(group, core, lengths, owner, slots, pad):
    return pl.pallas_call(
        functools.partial(routing_kernel, pad),
        out_shape=[
            jax.ShapeDtypeStruct((1, slots), jnp.int32),
            jax.ShapeDtypeStruct((1, slots), jnp.int32),
            jax.ShapeDtypeStruct((3,), jnp.int32),
        ],
        in_specs=[SMEM] * 4 + [VMEM] * 2,
        out_specs=[VMEM, VMEM, SMEM],
        cost_estimate=pl.CostEstimate(flops=10**6, bytes_accessed=10**6, transcendentals=0),
    )(group, core, lengths, owner, lengths.reshape(1, -1), owner.reshape(1, -1))


def pack_kernel(t_width, rows_ref, t_place_ref, s_place_ref, out_ref):
    count, half, _ = out_ref.shape
    slots = rows_ref.shape[0]
    width = out_ref.shape[2] // 2

    def packed(place_ref, first, stop):
        pick = (place_ref[...] == iota((2 * half, slots), 0)).astype(F32).astype(BF16)
        found = jnp.dot(pick, rows_ref[:, first:stop], preferred_element_type=F32)
        return found[:half], found[half:]

    main = (width - t_width) // 128 * 128
    t = packed(t_place_ref, 0, t_width)
    low, high = packed(s_place_ref, t_width, width)
    value = jnp.concatenate(
        [*t, low[:, :main], high[:, :main], low[:, main:], high[:, main:]], axis=1
    ).astype(BF16)
    for k in range(count):
        out_ref[k] = value


def pack(rows, t_place, s_place, lanes, t_width, width, count):
    return pl.pallas_call(
        functools.partial(pack_kernel, t_width),
        out_shape=jax.ShapeDtypeStruct((count, lanes // 2, 2 * width), BF16),
        in_specs=[VMEM] * 3,
        out_specs=VMEM,
        compiler_params=PARAMS,
    )(rows, t_place, s_place)


def in_parts(stats, lanes):
    row = iota((16, lanes), 0)
    table = jnp.zeros((16, lanes), F32)
    for k, value in enumerate(stats):
        for part in range(3):
            rounded = value.astype(BF16).astype(F32)
            table = jnp.where(row == 3 * k + part, rounded, table)
            value = value - rounded
    return table


def from_parts(table, lanes):
    rows = [table[k : k + 1, :lanes] for k in range(9)]
    return [rows[k] + rows[k + 1] + rows[k + 2] for k in (0, 3, 6)]


def merged(stats):
    lse, mean, t_lse = zip(*stats)
    high = functools.reduce(jnp.maximum, lse)
    t_high = functools.reduce(jnp.maximum, t_lse)
    scale = [jnp.exp(v - high) for v in lse]
    total = sum(scale[1:], scale[0])
    scale = [v / total for v in scale]
    middle = sum((a * v for a, v in zip(scale[1:], mean[1:])), scale[0] * mean[0])
    t_total = sum((jnp.exp(v - t_high) for v in t_lse[1:]), jnp.exp(t_lse[0] - t_high))
    shift = [v - middle for v in mean]
    return scale, shift, [high + jnp.log(total), middle, t_high + jnp.log(t_total)]


def soften(t, s, g_ref, stat_ref):
    lanes = g_ref.shape[1] // 2
    gap = s - t
    t_top = jnp.max(t, axis=0, keepdims=True)
    t_lse = t_top + jnp.log(jnp.sum(jnp.exp(t - t_top), axis=0, keepdims=True))
    s_top = jnp.max(s, axis=0, keepdims=True)
    p = jnp.exp(s - s_top)
    total = jnp.sum(p, axis=0, keepdims=True)
    p = p / total
    mean = jnp.sum(p * gap, axis=0, keepdims=True)
    g_ref[...] = jnp.concatenate([p * (gap - mean), p], axis=1).astype(BF16)
    table = in_parts([s_top + jnp.log(total), mean, t_lse], lanes)
    stat_ref[...] = jnp.concatenate([table, table], axis=1).astype(BF16)


def product(rows_ref, t_head_ref, s_head_ref, t, s):
    t_size, s_size = t_head_ref.shape[1], s_head_ref.shape[1]
    main = s_size // 128 * 128

    def rows(k, first, size):
        low = rows_ref[k, :, first : first + size]
        high = rows_ref[k, :, first + size : first + 2 * size]
        return jnp.concatenate([low, high], axis=0)

    count = rows_ref.shape[0]
    batch = 4
    for start in range(0, count, batch):
        ids = range(start, start + batch)
        t += jnp.dot(
            jnp.concatenate([rows(k, 0, t_size) for k in ids], axis=1),
            jnp.concatenate([t_head_ref[k] for k in ids], axis=0),
            preferred_element_type=F32,
        )
        s += jnp.dot(
            jnp.concatenate(
                [rows(k, 2 * t_size, main) for k in ids]
                + [rows(k, 2 * (t_size + main), s_size - main) for k in ids],
                axis=1,
            ),
            jnp.concatenate(
                [s_head_ref[k, :main] for k in ids] + [s_head_ref[k, main:] for k in ids],
                axis=0,
            ),
            preferred_element_type=F32,
        )
    return t, s


def first_kernel(
    info_ref, own_ref, t_head_ref, s_head_ref, t_ref, s_ref,
    s_own_ref, t_other_ref, s_other_ref, t_own_ref, sems,
):
    core = info_ref[1]
    copies = [
        pltpu.make_async_copy(head.at[:, c], to, sems.at[k])
        for k, (head, c, to) in enumerate(
            (
                (t_head_ref, core, t_own_ref),
                (s_head_ref, core, s_own_ref),
                (t_head_ref, 1 - core, t_other_ref),
                (s_head_ref, 1 - core, s_other_ref),
            )
        )
    ]
    for copy in copies:
        copy.start()
    copies[0].wait()
    copies[1].wait()
    zero = jnp.zeros(t_ref.shape, F32)
    t, s = product(own_ref, t_own_ref, s_own_ref, zero, zero)
    t_ref[...] = t
    s_ref[...] = s
    copies[2].wait()
    copies[3].wait()


def first(info, own, t_head, s_head):
    count, half_rows, width = own.shape
    vocab = t_head.shape[1]
    t_head = t_head.reshape(count, 2, -1, vocab)
    s_head = s_head.reshape(count, 2, -1, vocab)
    logit = jax.ShapeDtypeStruct((2 * half_rows, vocab), F32)
    t_part = (count, *t_head.shape[2:])
    s_part = (count, *s_head.shape[2:])
    return pl.pallas_call(
        first_kernel,
        out_shape=[
            logit,
            logit,
            jax.ShapeDtypeStruct(s_part, BF16),
            jax.ShapeDtypeStruct(t_part, BF16),
            jax.ShapeDtypeStruct(s_part, BF16),
        ],
        in_specs=[SMEM, VMEM] + [pl.BlockSpec(memory_space=pl.ANY)] * 2,
        out_specs=[VMEM] * 5,
        scratch_shapes=[pltpu.VMEM(t_part, BF16), pltpu.SemaphoreType.DMA((4,))],
        compiler_params=PARAMS,
        cost_estimate=pl.CostEstimate(
            flops=2 * own.size * vocab, bytes_accessed=4 * (t_head.size + s_head.size), transcendentals=0
        ),
    )(info, own, t_head, s_head)


def second_kernel(
    other_ref, t_ref, s_ref, s_own_ref, t_other_ref, s_other_ref, keep_ref, send_ref, g_ref, stat_ref
):
    t, s = product(other_ref, t_other_ref, s_other_ref, t_ref[...], s_ref[...])
    count, lanes = t.shape[0], g_ref.shape[1] // 2

    def turned(value):
        rest = -count % 128
        if rest:
            value = jnp.concatenate([value, jnp.zeros((rest, value.shape[1]), F32)], axis=0)
        return value.T[:, :lanes]

    soften(turned(t), turned(s), g_ref, stat_ref)
    half = s_own_ref.shape[1]
    for k in range(keep_ref.shape[0]):
        for head_ref, out_ref in ((s_own_ref, keep_ref), (s_other_ref, send_ref)):
            out_ref[k, :half] = jnp.dot(
                head_ref[k], g_ref[...], preferred_element_type=F32
            ).astype(BF16)
            out_ref[k, half:] = stat_ref[...]


def second(other, t, s, s_own, t_other, s_other, lanes):
    vocab = t.shape[1]
    count, half, _ = s_own.shape
    part = jax.ShapeDtypeStruct((count, half + 16, 2 * lanes), BF16)
    return pl.pallas_call(
        second_kernel,
        out_shape=[part, part],
        in_specs=[VMEM] * 6,
        out_specs=[VMEM] * 2,
        scratch_shapes=[
            pltpu.VMEM((vocab, 2 * lanes), BF16),
            pltpu.VMEM((16, 2 * lanes), BF16),
        ],
        compiler_params=PARAMS,
    )(other, t, s, s_own, t_other, s_other)


def pair_kernel(parts, info_ref, keep_ref, came_ref, out_ref):
    lanes = out_ref.shape[2] // 2
    half = keep_ref.shape[1] - 16
    low = info_ref[1] == 0
    kept = keep_ref[0, half:].astype(F32)
    come = came_ref[0, half:].astype(F32)
    first = jnp.where(low, kept, come)
    second = jnp.where(low, come, kept)
    scale, shift, stats = merged([from_parts(first, lanes), from_parts(second, lanes)])
    table = in_parts(stats, lanes)
    table = jnp.concatenate([table, table], axis=1).astype(BF16)
    own, other = (jnp.where(low, scale[0], scale[1]), jnp.where(low, scale[1], scale[0]))
    own_shift, other_shift = (
        own * jnp.where(low, shift[0], shift[1]),
        other * jnp.where(low, shift[1], shift[0]),
    )
    per = half // parts
    last = out_ref.shape[1] - 16
    for k in range(keep_ref.shape[0]):
        kept, come = keep_ref[k, :half].astype(F32), came_ref[k, :half].astype(F32)
        a = own * kept[:, :lanes] + other * come[:, :lanes]
        b_own, b_other = kept[:, lanes:], come[:, lanes:]
        a += own_shift * b_own + other_shift * b_other
        both = jnp.concatenate([a, own * b_own + other * b_other], axis=1).astype(BF16)
        for q in range(parts):
            out_ref[q, k * per : (k + 1) * per] = both[q * per : (q + 1) * per]
    for k in range(out_ref.shape[0]):
        out_ref[k, last:] = table


def pair(info, keep, came, parts):
    ring, deep, width = keep.shape
    deep = (deep - 16) // parts * ring + 16
    return pl.pallas_call(
        functools.partial(pair_kernel, parts),
        out_shape=jax.ShapeDtypeStruct((parts, deep, width), BF16),
        in_specs=[SMEM, VMEM, VMEM],
        out_specs=VMEM,
        compiler_params=PARAMS,
    )(info, keep, came)


def gathered(part_ref, lanes, half):
    count = part_ref.shape[0]
    scale, shift, stats = merged(
        [from_parts(part_ref[k, half:].astype(F32), lanes) for k in range(count)]
    )
    shift = [a * b for a, b in zip(scale, shift)]

    def piece(first, size):
        a = jnp.zeros((size, lanes), F32)
        b = jnp.zeros((size, lanes), F32)
        for k in range(count):
            one = part_ref[k, first : first + size].astype(F32)
            a += scale[k] * one[:, :lanes] + shift[k] * one[:, lanes:]
            b += scale[k] * one[:, lanes:]
        return a, b

    return piece, in_parts(stats, lanes)


def fold_kernel(part_ref, out_ref):
    lanes = part_ref.shape[2] // 2
    per = out_ref.shape[1] - 16
    piece, table = gathered(part_ref, lanes, part_ref.shape[1] - 16)
    table = jnp.concatenate([table, table], axis=1).astype(BF16)
    for k in range(out_ref.shape[0]):
        out_ref[k, :per] = jnp.concatenate(piece(k * per, per), axis=1).astype(BF16)
        out_ref[k, per:] = table


def fold(parts, count):
    _, deep, width = parts.shape
    return pl.pallas_call(
        fold_kernel,
        out_shape=jax.ShapeDtypeStruct((count, (deep - 16) // count + 16, width), BF16),
        in_specs=[VMEM],
        out_specs=VMEM,
        compiler_params=PARAMS,
    )(parts)


def spread_kernel(part_ref, place_ref, out_ref):
    lanes = part_ref.shape[2] // 2
    half = part_ref.shape[1] - 16
    groups, rows, width = out_ref.shape
    slots = place_ref.shape[1]
    piece, table = gathered(part_ref, lanes, half)
    rest = jnp.zeros((width - half - 16, lanes), F32)
    tall = -(-lanes // 128) * 128
    pick = (place_ref[...] == iota((tall, slots), 0)).astype(F32).T[:, :lanes].astype(BF16)

    def found(value):
        value = lax.dot_general(
            pick,
            jnp.concatenate([value, table, rest], axis=0).astype(BF16),
            (((1,), (1,)), ((), ())),
            preferred_element_type=F32,
        )
        return value.reshape(groups, rows // 2, width)

    both = [found(value) for value in piece(0, half)]
    out_ref[...] = jnp.concatenate(both, axis=1).astype(BF16)


def spread(parts, place, pad):
    width = -(-parts.shape[1] // 128) * 128
    return pl.pallas_call(
        spread_kernel,
        out_shape=jax.ShapeDtypeStruct((place.shape[1] // pad, 2 * pad, width), BF16),
        in_specs=[VMEM, VMEM],
        out_specs=VMEM,
        compiler_params=PARAMS,
    )(parts, place)


def finish_kernel(near, info_ref, part_ref, grad_ref, kl_ref):
    _, pad, width = grad_ref.shape
    per = width // near
    share = part_ref.shape[0] // near

    def source(q):
        return range(q * share, (q + 1) * share)

    wide = part_ref.shape[2]

    def moved(value, by):
        return pltpu.roll(value, by % wide, 1)

    tables = []
    for k in source(0):
        part = part_ref[k].astype(F32)[:pad]
        tables.append(part + moved(part, -1) + moved(part, -2))
    high = functools.reduce(jnp.maximum, tables)
    weight = [jnp.exp(v - high) for v in tables]
    total = functools.reduce(jnp.add, weight)
    weight = [w / total for w in weight]
    mean = functools.reduce(jnp.add, [moved(w, 3) * v for w, v in zip(weight, tables)])
    scale = [w[:, per : per + 1] for w in weight]
    shift = [(v - mean)[:, per + 3 : per + 4] for v in tables]
    lse = high + jnp.log(total)
    lse, t_lse, mean = lse[:, per : per + 1], lse[:, per + 6 : per + 7], mean[:, per + 3 : per + 4]
    pieces = []
    for q in range(near):
        grad = jnp.zeros((pad, part_ref.shape[2]), F32)
        for k, a, b in zip(source(q), scale, shift):
            part = part_ref[k].astype(F32)
            grad += a * (part[:pad] + b * part[pad:])
        pieces.append(grad[:, :per])
    grad_ref[0] = jnp.concatenate(pieces, axis=1).astype(BF16)
    kl = jnp.where(iota((pad, 1), 0) < info_ref[2], mean - lse + t_lse, 0.0)
    square = iota((pad, pad), 0) == iota((pad, pad), 1)
    kl_ref[...] = jnp.sum(jnp.where(square, kl, 0.0), axis=0, keepdims=True)


def finish(info, parts, width, near):
    pad = parts.shape[1] // 2
    return pl.pallas_call(
        functools.partial(finish_kernel, near),
        out_shape=[
            jax.ShapeDtypeStruct((1, pad, width), BF16),
            jax.ShapeDtypeStruct((1, pad), F32),
        ],
        in_specs=[SMEM, VMEM],
        out_specs=[VMEM, VMEM],
    )(info, parts)


def swap(value):
    return lax.ppermute(value, "c", ((0, 1), (1, 0)))


def some_rows(count, lanes, pad, t_width, width, operands):
    info, rows, t_place, s_place, teacher_head, student_head = operands
    own = exchange(pack(rows, t_place, s_place, count, t_width, width, lax.axis_size("y")), "y")
    other = swap(own)
    t, s, *heads = first(info, own, teacher_head, student_head)
    keep, send = second(other, t, s, *heads, lanes)
    both = exchange(pair(info, keep, swap(send), lax.axis_size("x")), "x")
    both = exchange(fold(both, lax.axis_size("y")), "y")
    return exchange(spread(both, s_place, pad), GRP)


def per_device(teacher_rows, student_rows, teacher_head, student_head, lengths, owner):
    groups = lax.axis_size(GRP)
    pad = student_rows.shape[1]
    t_width, s_width = teacher_rows.shape[2], student_rows.shape[2]
    group = lax.axis_index(GRP).astype(jnp.int32).reshape(1)
    core = lax.axis_index("c").astype(jnp.int32).reshape(1)
    mine = arrange(group, lengths, teacher_rows, student_rows, groups)
    t_place, s_place, info = routing(group, core, lengths, owner, groups * pad, pad)
    rows = exchange(mine, GRP).reshape(groups * pad, mine.shape[2])
    operands = (info, rows, t_place, s_place, teacher_head, student_head)
    branches = [functools.partial(some_rows, *c, pad, t_width, t_width + s_width) for c in CAPACITIES]
    parts = lax.switch(info[0], branches, operands)
    grad, divergence = finish(info, parts, s_width, lax.axis_size("x"))
    return divergence, grad


def solution(mesh):
    torus = Mesh(mesh.devices.reshape(4, 8, 8, 2), ("x", "z", "y", "c"))
    return jax.shard_map(
        per_device,
        mesh=torus,
        in_specs=(
            P(GRP, None, VOCAB),
            P(GRP, None, VOCAB),
            P(None, (*GRP, *VOCAB)),
            P(None, (*GRP, *VOCAB)),
            P(),
            P(),
        ),
        out_specs=(P(GRP, None), P(GRP, None, VOCAB)),
        check_vma=False,
    )
```

```python
import functools

import jax
import jax.numpy as jnp
from jax import lax
from jax.experimental import pallas as pl
from jax.experimental.pallas import tpu as pltpu
from jax.sharding import Mesh
from jax.sharding import PartitionSpec as P

GRP = ("x", "z")
Y = ("yh", "yl")
VOCAB = ("yh", "yl", "c")
NEAR = ("x", "yl")
REST = ("yh", "x", "z")
CAPACITIES = ((128, 128), (160, 192), (256, 256))
F32 = jnp.float32
BF16 = jnp.bfloat16
VMEM = pl.BlockSpec(memory_space=pltpu.VMEM)
SMEM = pl.BlockSpec(memory_space=pltpu.SMEM)
PARAMS = pltpu.CompilerParams(vmem_limit_bytes=20 * 1024 * 1024)


def iota(shape, dim):
    return lax.broadcasted_iota(jnp.int32, shape, dim)


def exchange(pieces, axes):
    return lax.all_to_all(pieces, axes, 0, 0, tiled=True)


def arrange_kernel(group_ref, lengths_ref, teacher_ref, student_ref, out_ref):
    count, pad, _ = out_ref.shape
    width = teacher_ref.shape[2]
    rest = out_ref.shape[2] - width - student_ref.shape[2]
    share = lengths_ref.shape[0] // count
    first = lengths_ref[share * group_ref[0]]
    upper = teacher_ref[0].astype(F32)
    lower = pltpu.roll(teacher_ref[1].astype(F32), first, 0)
    chosen = jnp.where(iota(upper.shape, 0) < first, upper, lower).astype(BF16)
    for k in range(count):
        out_ref[k, :, :width] = chosen
        out_ref[k, :, width : width + student_ref.shape[2]] = student_ref[0]
        if rest:
            out_ref[k, :, -rest:] = jnp.zeros((pad, rest), BF16)


def arrange(group, lengths, teacher_rows, student_rows, count):
    pad = student_rows.shape[1]
    width = -(-(teacher_rows.shape[2] + student_rows.shape[2]) // 128) * 128
    return pl.pallas_call(
        arrange_kernel,
        out_shape=jax.ShapeDtypeStruct((count, pad, width), BF16),
        in_specs=[SMEM] * 2 + [VMEM] * 2,
        out_specs=VMEM,
    )(group, lengths, teacher_rows, student_rows)


def routing_kernel(
    pad, group_ref, core_ref, lengths_ref, owner_ref, length_row_ref, owner_row_ref,
    t_place_ref, s_place_ref, info_ref,
):
    group = group_ref[0]
    live = jnp.int32(0)
    mine = jnp.int32(0)
    for k in range(lengths_ref.shape[0]):
        live += lengths_ref[k]
        mine += jnp.where(owner_ref[k] == group, lengths_ref[k], 0)
    which = jnp.int32(0)
    for c, _ in CAPACITIES[:-1]:
        which += (live > c).astype(jnp.int32)
    info_ref[0] = which
    info_ref[1] = core_ref[0]
    info_ref[2] = mine

    slots = t_place_ref.shape[1]
    deep = length_row_ref.shape[1]
    share = deep * pad // slots

    def column(ref):
        one = jnp.broadcast_to(ref[...].astype(F32), (deep, deep)).T
        return jnp.broadcast_to(one[:, :1], (deep, slots))

    length, owner = column(length_row_ref), column(owner_row_ref)
    seq = iota((deep, slots), 0)
    home = iota((deep, slots), 1) // pad
    zero = jnp.zeros((deep, slots), F32)

    def total(mask, value):
        return jnp.sum(jnp.where(mask, value, zero), axis=0, keepdims=True)

    home_f = home.astype(F32)
    step = (iota((1, slots), 1) % pad).astype(F32)
    t_count = total(seq // share == home, length)
    t_owner = total(seq == share * home, owner)
    t_start = total(owner < t_owner, length)
    s_count = total(owner == home_f, length)
    s_start = total(owner < home_f, length)
    t_place = jnp.where(step < t_count, t_start + step, -1.0)
    s_place = jnp.where(step < s_count, s_start + step, -1.0)
    t_place_ref[...] = t_place.astype(jnp.int32)
    s_place_ref[...] = s_place.astype(jnp.int32)


def routing(group, core, lengths, owner, slots, pad):
    return pl.pallas_call(
        functools.partial(routing_kernel, pad),
        out_shape=[
            jax.ShapeDtypeStruct((1, slots), jnp.int32),
            jax.ShapeDtypeStruct((1, slots), jnp.int32),
            jax.ShapeDtypeStruct((3,), jnp.int32),
        ],
        in_specs=[SMEM] * 4 + [VMEM] * 2,
        out_specs=[VMEM, VMEM, SMEM],
        cost_estimate=pl.CostEstimate(flops=10**6, bytes_accessed=10**6, transcendentals=0),
    )(group, core, lengths, owner, lengths.reshape(1, -1), owner.reshape(1, -1))


def pack_kernel(t_width, rows_ref, t_place_ref, s_place_ref, out_ref):
    count, half, _ = out_ref.shape
    slots = rows_ref.shape[0]
    width = out_ref.shape[2] // 2

    def packed(place_ref, first, stop):
        pick = (place_ref[...] == iota((2 * half, slots), 0)).astype(F32).astype(BF16)
        found = jnp.dot(pick, rows_ref[:, first:stop], preferred_element_type=F32)
        return found[:half], found[half:]

    main = (width - t_width) // 128 * 128
    t = packed(t_place_ref, 0, t_width)
    low, high = packed(s_place_ref, t_width, width)
    value = jnp.concatenate(
        [*t, low[:, :main], high[:, :main], low[:, main:], high[:, main:]], axis=1
    ).astype(BF16)
    for k in range(count):
        out_ref[k] = value


def pack(rows, t_place, s_place, lanes, t_width, width, count):
    return pl.pallas_call(
        functools.partial(pack_kernel, t_width),
        out_shape=jax.ShapeDtypeStruct((count, lanes // 2, 2 * width), BF16),
        in_specs=[VMEM] * 3,
        out_specs=VMEM,
        compiler_params=PARAMS,
    )(rows, t_place, s_place)


def in_parts(stats, lanes):
    row = iota((16, lanes), 0)
    table = jnp.zeros((16, lanes), F32)
    for k, value in enumerate(stats):
        for part in range(3):
            rounded = value.astype(BF16).astype(F32)
            table = jnp.where(row == 3 * k + part, rounded, table)
            value = value - rounded
    return table


def from_parts(table, lanes):
    rows = [table[k : k + 1, :lanes] for k in range(9)]
    return [rows[k] + rows[k + 1] + rows[k + 2] for k in (0, 3, 6)]


def merged(stats):
    lse, mean, t_lse = zip(*stats)
    high = functools.reduce(jnp.maximum, lse)
    t_high = functools.reduce(jnp.maximum, t_lse)
    scale = [jnp.exp(v - high) for v in lse]
    total = sum(scale[1:], scale[0])
    scale = [v / total for v in scale]
    middle = sum((a * v for a, v in zip(scale[1:], mean[1:])), scale[0] * mean[0])
    t_total = sum((jnp.exp(v - t_high) for v in t_lse[1:]), jnp.exp(t_lse[0] - t_high))
    shift = [v - middle for v in mean]
    return scale, shift, [high + jnp.log(total), middle, t_high + jnp.log(t_total)]


def soften(t, s, g_ref, stat_ref):
    lanes = g_ref.shape[1] // 2
    gap = s - t
    t_top = jnp.max(t, axis=0, keepdims=True)
    t_lse = t_top + jnp.log(jnp.sum(jnp.exp(t - t_top), axis=0, keepdims=True))
    s_top = jnp.max(s, axis=0, keepdims=True)
    p = jnp.exp(s - s_top)
    total = jnp.sum(p, axis=0, keepdims=True)
    p = p / total
    mean = jnp.sum(p * gap, axis=0, keepdims=True)
    g_ref[...] = jnp.concatenate([p * (gap - mean), p], axis=1).astype(BF16)
    table = in_parts([s_top + jnp.log(total), mean, t_lse], lanes)
    stat_ref[...] = jnp.concatenate([table, table], axis=1).astype(BF16)


def product(rows_ref, t_head_ref, s_head_ref, t, s):
    t_size, s_size = t_head_ref.shape[1], s_head_ref.shape[1]
    main = s_size // 128 * 128

    def rows(k, first, size):
        low = rows_ref[k, :, first : first + size]
        high = rows_ref[k, :, first + size : first + 2 * size]
        return jnp.concatenate([low, high], axis=0)

    count = rows_ref.shape[0]
    batch = 4
    for start in range(0, count, batch):
        ids = range(start, start + batch)
        t += jnp.dot(
            jnp.concatenate([rows(k, 0, t_size) for k in ids], axis=1),
            jnp.concatenate([t_head_ref[k] for k in ids], axis=0),
            preferred_element_type=F32,
        )
        s += jnp.dot(
            jnp.concatenate(
                [rows(k, 2 * t_size, main) for k in ids]
                + [rows(k, 2 * (t_size + main), s_size - main) for k in ids],
                axis=1,
            ),
            jnp.concatenate(
                [s_head_ref[k, :main] for k in ids] + [s_head_ref[k, main:] for k in ids],
                axis=0,
            ),
            preferred_element_type=F32,
        )
    return t, s


def first_kernel(
    info_ref, own_ref, t_head_ref, s_head_ref, t_ref, s_ref,
    s_own_ref, t_other_ref, s_other_ref, t_own_ref, sems,
):
    core = info_ref[1]
    copies = [
        pltpu.make_async_copy(head.at[:, c], to, sems.at[k])
        for k, (head, c, to) in enumerate(
            (
                (t_head_ref, core, t_own_ref),
                (s_head_ref, core, s_own_ref),
                (t_head_ref, 1 - core, t_other_ref),
                (s_head_ref, 1 - core, s_other_ref),
            )
        )
    ]
    for copy in copies:
        copy.start()
    copies[0].wait()
    copies[1].wait()
    zero = jnp.zeros(t_ref.shape, F32)
    t, s = product(own_ref, t_own_ref, s_own_ref, zero, zero)
    t_ref[...] = t
    s_ref[...] = s
    copies[2].wait()
    copies[3].wait()


def first(info, own, t_head, s_head):
    count, half_rows, width = own.shape
    vocab = t_head.shape[1]
    t_head = t_head.reshape(count, 2, -1, vocab)
    s_head = s_head.reshape(count, 2, -1, vocab)
    logit = jax.ShapeDtypeStruct((2 * half_rows, vocab), F32)
    t_part = (count, *t_head.shape[2:])
    s_part = (count, *s_head.shape[2:])
    return pl.pallas_call(
        first_kernel,
        out_shape=[
            logit,
            logit,
            jax.ShapeDtypeStruct(s_part, BF16),
            jax.ShapeDtypeStruct(t_part, BF16),
            jax.ShapeDtypeStruct(s_part, BF16),
        ],
        in_specs=[SMEM, VMEM] + [pl.BlockSpec(memory_space=pl.ANY)] * 2,
        out_specs=[VMEM] * 5,
        scratch_shapes=[pltpu.VMEM(t_part, BF16), pltpu.SemaphoreType.DMA((4,))],
        compiler_params=PARAMS,
        cost_estimate=pl.CostEstimate(
            flops=2 * own.size * vocab, bytes_accessed=4 * (t_head.size + s_head.size), transcendentals=0
        ),
    )(info, own, t_head, s_head)


def second_kernel(other_ref, t_ref, s_ref, t_other_ref, s_other_ref, out_ref):
    t, s = product(other_ref, t_other_ref, s_other_ref, t_ref[...], s_ref[...])
    count, lanes = t.shape[0], out_ref.shape[1] // 2

    def turned(value):
        rest = -count % 128
        if rest:
            value = jnp.concatenate([value, jnp.zeros((rest, value.shape[1]), F32)], axis=0)
        return value.T[:, :lanes]

    vocab = t.shape[1]
    soften(turned(t), turned(s), out_ref.at[:vocab], out_ref.at[vocab:])


def second(other, t, s, t_other, s_other, lanes):
    return pl.pallas_call(
        second_kernel,
        out_shape=jax.ShapeDtypeStruct((t.shape[1] + 16, 2 * lanes), BF16),
        in_specs=[VMEM] * 5,
        out_specs=VMEM,
        compiler_params=PARAMS,
    )(other, t, s, t_other, s_other)


def third_kernel(parts, info_ref, own_ref, came_ref, s_own_ref, cross_ref, out_ref):
    lanes = own_ref.shape[1] // 2
    vocab = own_ref.shape[0] - 16
    core = info_ref[1]
    low = core == 0
    own = own_ref[...].astype(F32)
    came = came_ref[...].astype(F32)
    first = jnp.where(low, own[vocab:], came[vocab:])
    second = jnp.where(low, came[vocab:], own[vocab:])
    scale, shift, stats = merged([from_parts(first, lanes), from_parts(second, lanes)])

    def scaled(value, k):
        a = jnp.where(low, scale[k], scale[1 - k])
        d = a * jnp.where(low, shift[k], shift[1 - k])
        top, plain = value[:vocab, :lanes], value[:vocab, lanes:]
        return jnp.concatenate([a * top + d * plain, a * plain], axis=1).astype(BF16)

    g = jnp.concatenate([scaled(own, 0), scaled(came, 1)], axis=0)
    ring, half, _ = s_own_ref.shape
    per = half // parts
    near = out_ref.shape[0] // parts
    last = out_ref.shape[1] - 16
    for k in range(ring):
        head = jnp.concatenate([s_own_ref[k], cross_ref[k, core]], axis=1)
        both = jnp.dot(head, g, preferred_element_type=F32).astype(BF16)
        start = k // near * per
        for q in range(parts):
            piece = both[q * per : (q + 1) * per]
            out_ref[q * near + k % near, start : start + per] = piece
    table = in_parts(stats, lanes)
    table = jnp.concatenate([table, table], axis=1).astype(BF16)
    for k in range(out_ref.shape[0]):
        out_ref[k, last:] = table


def third(info, own, came, s_own, cross, parts, near):
    ring, half, _ = s_own.shape
    deep = half // parts * (ring // near) + 16
    return pl.pallas_call(
        functools.partial(third_kernel, parts),
        out_shape=jax.ShapeDtypeStruct((parts * near, deep, own.shape[1]), BF16),
        in_specs=[SMEM] + [VMEM] * 4,
        out_specs=VMEM,
        compiler_params=PARAMS,
    )(info, own, came, s_own, cross.reshape(ring, 2, half, -1))


def spread_kernel(part_ref, place_ref, out_ref):
    lanes = part_ref.shape[2] // 2
    half = part_ref.shape[1] - 16
    count = part_ref.shape[0]
    slots = place_ref.shape[1]
    pad = out_ref.shape[1] // 2
    width = out_ref.shape[2]
    groups = slots // pad
    far = out_ref.shape[0] // groups
    per = half // far
    scale, shift, stats = merged(
        [from_parts(part_ref[k, half:].astype(F32), lanes) for k in range(count)]
    )
    a = jnp.zeros((half, lanes), F32)
    b = jnp.zeros((half, lanes), F32)
    for k in range(count):
        one = part_ref[k, :half].astype(F32)
        b_one = one[:, lanes:]
        a += scale[k] * one[:, :lanes] + (scale[k] * shift[k]) * b_one
        b += scale[k] * b_one
    rest = jnp.zeros((width - per - 16, lanes), F32)
    table = jnp.concatenate([in_parts(stats, lanes), rest], axis=0)
    tall = -(-lanes // 128) * 128
    pick = (place_ref[...] == iota((tall, slots), 0)).astype(F32).T[:, :lanes].astype(BF16)

    def found(value):
        pieces = []
        for k in range(far):
            pieces += [value[k * per : (k + 1) * per], table]
        return lax.dot_general(
            pick,
            jnp.concatenate(pieces, axis=0).astype(BF16),
            (((1,), (1,)), ((), ())),
            preferred_element_type=F32,
        )

    a, b = found(a), found(b)
    for k in range(far):
        both = [v[:, k * width : (k + 1) * width].reshape(groups, pad, width) for v in (a, b)]
        out_ref[k * groups : (k + 1) * groups] = jnp.concatenate(both, axis=1).astype(BF16)


def spread(parts, place, pad, far):
    groups = place.shape[1] // pad
    per = (parts.shape[1] - 16) // far
    width = -(-(per + 16) // 128) * 128
    return pl.pallas_call(
        spread_kernel,
        out_shape=jax.ShapeDtypeStruct((far * groups, 2 * pad, width), BF16),
        in_specs=[VMEM, VMEM],
        out_specs=VMEM,
        compiler_params=PARAMS,
    )(parts, place)


def finish_kernel(far, near, info_ref, part_ref, grad_ref, kl_ref):
    _, pad, width = grad_ref.shape
    per = width // near
    groups = part_ref.shape[0] // far
    share = groups // near

    def source(q):
        return [f * groups + q * share + k for f in range(far) for k in range(share)]

    wide = part_ref.shape[2]

    def moved(value, by):
        return pltpu.roll(value, by % wide, 1)

    tables = []
    for k in source(0):
        part = part_ref[k].astype(F32)[:pad]
        tables.append(part + moved(part, -1) + moved(part, -2))
    high = functools.reduce(jnp.maximum, tables)
    weight = [jnp.exp(v - high) for v in tables]
    total = functools.reduce(jnp.add, weight)
    weight = [w / total for w in weight]
    mean = functools.reduce(jnp.add, [moved(w, 3) * v for w, v in zip(weight, tables)])
    scale = [w[:, per : per + 1] for w in weight]
    shift = [(v - mean)[:, per + 3 : per + 4] for v in tables]
    lse = high + jnp.log(total)
    lse, t_lse, mean = lse[:, per : per + 1], lse[:, per + 6 : per + 7], mean[:, per + 3 : per + 4]
    pieces = []
    for q in range(near):
        grad = jnp.zeros((pad, part_ref.shape[2]), F32)
        for k, a, b in zip(source(q), scale, shift):
            part = part_ref[k].astype(F32)
            grad += a * (part[:pad] + b * part[pad:])
        pieces.append(grad[:, :per])
    grad_ref[0] = jnp.concatenate(pieces, axis=1).astype(BF16)
    kl = jnp.where(iota((pad, 1), 0) < info_ref[2], mean - lse + t_lse, 0.0)
    square = iota((pad, pad), 0) == iota((pad, pad), 1)
    kl_ref[...] = jnp.sum(jnp.where(square, kl, 0.0), axis=0, keepdims=True)


def finish(info, parts, width, far, near):
    pad = parts.shape[1] // 2
    return pl.pallas_call(
        functools.partial(finish_kernel, far, near),
        out_shape=[
            jax.ShapeDtypeStruct((1, pad, width), BF16),
            jax.ShapeDtypeStruct((1, pad), F32),
        ],
        in_specs=[SMEM, VMEM],
        out_specs=[VMEM, VMEM],
    )(info, parts)


def swap(value):
    return lax.ppermute(value, "c", ((0, 1), (1, 0)))


def some_rows(count, lanes, pad, t_width, width, operands):
    info, rows, t_place, s_place, teacher_head, student_head, cross = operands
    own = exchange(pack(rows, t_place, s_place, count, t_width, width, lax.axis_size(Y)), Y)
    other = swap(own)
    t, s, s_own, t_other, s_other = first(info, own, teacher_head, student_head)
    g = second(other, t, s, t_other, s_other, lanes)
    both = third(info, g, swap(g), s_own, cross, lax.axis_size("x"), lax.axis_size("yl"))
    return exchange(spread(exchange(both, NEAR), s_place, pad, lax.axis_size("yh")), REST)


def per_device(teacher_rows, student_rows, teacher_head, student_head, lengths, owner):
    groups = lax.axis_size(GRP)
    pad = student_rows.shape[1]
    t_width, s_width = teacher_rows.shape[2], student_rows.shape[2]
    group = lax.axis_index(GRP).astype(jnp.int32).reshape(1)
    core = lax.axis_index("c").astype(jnp.int32).reshape(1)
    mine = arrange(group, lengths, teacher_rows, student_rows, groups)
    t_place, s_place, info = routing(group, core, lengths, owner, groups * pad, pad)
    mine, outgoing = lax.optimization_barrier((mine, student_head))
    cross = swap(outgoing)
    rows = exchange(mine, GRP).reshape(groups * pad, mine.shape[2])
    operands = (info, rows, t_place, s_place, teacher_head, student_head, cross)
    branches = [functools.partial(some_rows, *c, pad, t_width, t_width + s_width) for c in CAPACITIES]
    parts = lax.switch(info[0], branches, operands)
    grad, divergence = finish(info, parts, s_width, lax.axis_size("yh"), lax.axis_size("x"))
    return divergence, grad


def solution(mesh):
    torus = Mesh(mesh.devices.reshape(4, 8, 4, 2, 2), ("x", "z", "yh", "yl", "c"))
    return jax.shard_map(
        per_device,
        mesh=torus,
        in_specs=(
            P(GRP, None, VOCAB),
            P(GRP, None, VOCAB),
            P(None, (*GRP, *VOCAB)),
            P(None, (*GRP, *VOCAB)),
            P(),
            P(),
        ),
        out_specs=(P(GRP, None), P(GRP, None, VOCAB)),
        check_vma=False,
    )
```

```python
import functools

import jax
import jax.numpy as jnp
from jax import lax
from jax.experimental import pallas as pl
from jax.experimental.pallas import tpu as pltpu
from jax.sharding import Mesh
from jax.sharding import PartitionSpec as P

GRP = ("x", "z")
Y = ("yh", "yl")
VOCAB = ("yh", "yl", "c")
NEAR = ("x", "yl")
REST = ("yh", "x", "z")
CAPACITIES = ((128, 128), (160, 192), (256, 256))
F32 = jnp.float32
BF16 = jnp.bfloat16
VMEM = pl.BlockSpec(memory_space=pltpu.VMEM)
SMEM = pl.BlockSpec(memory_space=pltpu.SMEM)
PARAMS = pltpu.CompilerParams(vmem_limit_bytes=20 * 1024 * 1024)


def iota(shape, dim):
    return lax.broadcasted_iota(jnp.int32, shape, dim)


def exchange(pieces, axes):
    return lax.all_to_all(pieces, axes, 0, 0, tiled=True)


def arrange_kernel(group_ref, lengths_ref, teacher_ref, student_ref, out_ref):
    count, pad, _ = out_ref.shape
    width = teacher_ref.shape[2]
    rest = out_ref.shape[2] - width - student_ref.shape[2]
    share = lengths_ref.shape[0] // count
    first = lengths_ref[share * group_ref[0]]
    upper = teacher_ref[0].astype(F32)
    lower = pltpu.roll(teacher_ref[1].astype(F32), first, 0)
    chosen = jnp.where(iota(upper.shape, 0) < first, upper, lower).astype(BF16)
    for k in range(count):
        out_ref[k, :, :width] = chosen
        out_ref[k, :, width : width + student_ref.shape[2]] = student_ref[0]
        if rest:
            out_ref[k, :, -rest:] = jnp.zeros((pad, rest), BF16)


def arrange(group, lengths, teacher_rows, student_rows, count):
    pad = student_rows.shape[1]
    width = -(-(teacher_rows.shape[2] + student_rows.shape[2]) // 128) * 128
    return pl.pallas_call(
        arrange_kernel,
        out_shape=jax.ShapeDtypeStruct((count, pad, width), BF16),
        in_specs=[SMEM] * 2 + [VMEM] * 2,
        out_specs=VMEM,
    )(group, lengths, teacher_rows, student_rows)


def routing_kernel(
    pad, group_ref, core_ref, lengths_ref, owner_ref, length_row_ref, owner_row_ref,
    t_place_ref, s_place_ref, info_ref,
):
    group = group_ref[0]
    live = jnp.int32(0)
    mine = jnp.int32(0)
    for k in range(lengths_ref.shape[0]):
        live += lengths_ref[k]
        mine += jnp.where(owner_ref[k] == group, lengths_ref[k], 0)
    which = jnp.int32(0)
    for c, _ in CAPACITIES[:-1]:
        which += (live > c).astype(jnp.int32)
    info_ref[0] = which
    info_ref[1] = core_ref[0]
    info_ref[2] = mine

    slots = t_place_ref.shape[1]
    deep = length_row_ref.shape[1]
    share = deep * pad // slots

    def column(ref):
        one = jnp.broadcast_to(ref[...].astype(F32), (deep, deep)).T
        return jnp.broadcast_to(one[:, :1], (deep, slots))

    length, owner = column(length_row_ref), column(owner_row_ref)
    seq = iota((deep, slots), 0)
    home = iota((deep, slots), 1) // pad
    zero = jnp.zeros((deep, slots), F32)

    def total(mask, value):
        return jnp.sum(jnp.where(mask, value, zero), axis=0, keepdims=True)

    home_f = home.astype(F32)
    step = (iota((1, slots), 1) % pad).astype(F32)
    t_count = total(seq // share == home, length)
    t_owner = total(seq == share * home, owner)
    t_start = total(owner < t_owner, length)
    s_count = total(owner == home_f, length)
    s_start = total(owner < home_f, length)
    t_place = jnp.where(step < t_count, t_start + step, -1.0)
    s_place = jnp.where(step < s_count, s_start + step, -1.0)
    t_place_ref[...] = t_place.astype(jnp.int32)
    s_place_ref[...] = s_place.astype(jnp.int32)


def routing(group, core, lengths, owner, slots, pad):
    return pl.pallas_call(
        functools.partial(routing_kernel, pad),
        out_shape=[
            jax.ShapeDtypeStruct((1, slots), jnp.int32),
            jax.ShapeDtypeStruct((1, slots), jnp.int32),
            jax.ShapeDtypeStruct((3,), jnp.int32),
        ],
        in_specs=[SMEM] * 4 + [VMEM] * 2,
        out_specs=[VMEM, VMEM, SMEM],
        cost_estimate=pl.CostEstimate(flops=10**6, bytes_accessed=10**6, transcendentals=0),
    )(group, core, lengths, owner, lengths.reshape(1, -1), owner.reshape(1, -1))


def pack_kernel(t_width, rows_ref, t_place_ref, s_place_ref, out_ref):
    count, half, _ = out_ref.shape
    slots = rows_ref.shape[0]
    width = out_ref.shape[2] // 2

    def packed(place_ref, first, stop):
        pick = (place_ref[...] == iota((2 * half, slots), 0)).astype(F32).astype(BF16)
        found = jnp.dot(pick, rows_ref[:, first:stop], preferred_element_type=F32)
        return found[:half], found[half:]

    main = (width - t_width) // 128 * 128
    t = packed(t_place_ref, 0, t_width)
    low, high = packed(s_place_ref, t_width, width)
    value = jnp.concatenate(
        [*t, low[:, :main], high[:, :main], low[:, main:], high[:, main:]], axis=1
    ).astype(BF16)
    for k in range(count):
        out_ref[k] = value


def pack(rows, t_place, s_place, lanes, t_width, width, count):
    return pl.pallas_call(
        functools.partial(pack_kernel, t_width),
        out_shape=jax.ShapeDtypeStruct((count, lanes // 2, 2 * width), BF16),
        in_specs=[VMEM] * 3,
        out_specs=VMEM,
        compiler_params=PARAMS,
    )(rows, t_place, s_place)


def in_parts(stats, lanes):
    row = iota((16, lanes), 0)
    table = jnp.zeros((16, lanes), F32)
    for k, value in enumerate(stats):
        for part in range(3):
            rounded = value.astype(BF16).astype(F32)
            table = jnp.where(row == 3 * k + part, rounded, table)
            value = value - rounded
    return table


def from_parts(table, lanes):
    rows = [table[k : k + 1, :lanes] for k in range(9)]
    return [rows[k] + rows[k + 1] + rows[k + 2] for k in (0, 3, 6)]


def merged(stats):
    lse, mean, t_lse = zip(*stats)
    high = functools.reduce(jnp.maximum, lse)
    t_high = functools.reduce(jnp.maximum, t_lse)
    scale = [jnp.exp(v - high) for v in lse]
    total = sum(scale[1:], scale[0])
    scale = [v / total for v in scale]
    middle = sum((a * v for a, v in zip(scale[1:], mean[1:])), scale[0] * mean[0])
    t_total = sum((jnp.exp(v - t_high) for v in t_lse[1:]), jnp.exp(t_lse[0] - t_high))
    shift = [v - middle for v in mean]
    return scale, shift, [high + jnp.log(total), middle, t_high + jnp.log(t_total)]


def soften(t, s, g_ref, stat_ref):
    lanes = g_ref.shape[1] // 2
    gap = s - t
    t_top = jnp.max(t, axis=0, keepdims=True)
    t_lse = t_top + jnp.log(jnp.sum(jnp.exp(t - t_top), axis=0, keepdims=True))
    s_top = jnp.max(s, axis=0, keepdims=True)
    p = jnp.exp(s - s_top)
    total = jnp.sum(p, axis=0, keepdims=True)
    p = p / total
    mean = jnp.sum(p * gap, axis=0, keepdims=True)
    g_ref[...] = jnp.concatenate([p * (gap - mean), p], axis=1).astype(BF16)
    table = in_parts([s_top + jnp.log(total), mean, t_lse], lanes)
    stat_ref[...] = jnp.concatenate([table, table], axis=1).astype(BF16)


def product(rows_ref, t_head_ref, s_head_ref, t, s):
    t_size, s_size = t_head_ref.shape[1], s_head_ref.shape[1]
    main = s_size // 128 * 128

    def rows(k, first, size):
        low = rows_ref[k, :, first : first + size]
        high = rows_ref[k, :, first + size : first + 2 * size]
        return jnp.concatenate([low, high], axis=0)

    count = rows_ref.shape[0]
    batch = 4
    for start in range(0, count, batch):
        ids = range(start, start + batch)
        t += jnp.dot(
            jnp.concatenate([rows(k, 0, t_size) for k in ids], axis=1),
            jnp.concatenate([t_head_ref[k] for k in ids], axis=0),
            preferred_element_type=F32,
        )
        s += jnp.dot(
            jnp.concatenate(
                [rows(k, 2 * t_size, main) for k in ids]
                + [rows(k, 2 * (t_size + main), s_size - main) for k in ids],
                axis=1,
            ),
            jnp.concatenate(
                [s_head_ref[k, :main] for k in ids] + [s_head_ref[k, main:] for k in ids],
                axis=0,
            ),
            preferred_element_type=F32,
        )
    return t, s


def first_kernel(
    info_ref, own_ref, t_head_ref, s_head_ref, t_ref, s_ref,
    s_own_ref, t_other_ref, s_other_ref, t_own_ref, sems,
):
    core = info_ref[1]
    copies = [
        pltpu.make_async_copy(head.at[:, c], to, sems.at[k])
        for k, (head, c, to) in enumerate(
            (
                (t_head_ref, core, t_own_ref),
                (s_head_ref, core, s_own_ref),
                (t_head_ref, 1 - core, t_other_ref),
                (s_head_ref, 1 - core, s_other_ref),
            )
        )
    ]
    for copy in copies:
        copy.start()
    copies[0].wait()
    copies[1].wait()
    zero = jnp.zeros(t_ref.shape, F32)
    t, s = product(own_ref, t_own_ref, s_own_ref, zero, zero)
    t_ref[...] = t
    s_ref[...] = s
    copies[2].wait()
    copies[3].wait()


def first(info, own, t_head, s_head):
    count, half_rows, width = own.shape
    vocab = t_head.shape[1]
    t_head = t_head.reshape(count, 2, -1, vocab)
    s_head = s_head.reshape(count, 2, -1, vocab)
    logit = jax.ShapeDtypeStruct((2 * half_rows, vocab), F32)
    t_part = (count, *t_head.shape[2:])
    s_part = (count, *s_head.shape[2:])
    return pl.pallas_call(
        first_kernel,
        out_shape=[
            logit,
            logit,
            jax.ShapeDtypeStruct(s_part, BF16),
            jax.ShapeDtypeStruct(t_part, BF16),
            jax.ShapeDtypeStruct(s_part, BF16),
        ],
        in_specs=[SMEM, VMEM] + [pl.BlockSpec(memory_space=pl.ANY)] * 2,
        out_specs=[VMEM] * 5,
        scratch_shapes=[pltpu.VMEM(t_part, BF16), pltpu.SemaphoreType.DMA((4,))],
        compiler_params=PARAMS,
        cost_estimate=pl.CostEstimate(
            flops=2 * own.size * vocab, bytes_accessed=4 * (t_head.size + s_head.size), transcendentals=0
        ),
    )(info, own, t_head, s_head)


def second_kernel(other_ref, t_ref, s_ref, t_other_ref, s_other_ref, out_ref):
    t, s = product(other_ref, t_other_ref, s_other_ref, t_ref[...], s_ref[...])
    count, lanes = t.shape[0], out_ref.shape[1] // 2

    def turned(value):
        rest = -count % 128
        if rest:
            value = jnp.concatenate([value, jnp.zeros((rest, value.shape[1]), F32)], axis=0)
        return value.T[:, :lanes]

    vocab = t.shape[1]
    soften(turned(t), turned(s), out_ref.at[:vocab], out_ref.at[vocab:])


def second(other, t, s, t_other, s_other, lanes):
    return pl.pallas_call(
        second_kernel,
        out_shape=jax.ShapeDtypeStruct((t.shape[1] + 16, 2 * lanes), BF16),
        in_specs=[VMEM] * 5,
        out_specs=VMEM,
        compiler_params=PARAMS,
    )(other, t, s, t_other, s_other)


def third_kernel(parts, info_ref, own_ref, came_ref, s_own_ref, cross_ref, out_ref):
    lanes = own_ref.shape[1] // 2
    vocab = own_ref.shape[0] - 16
    core = info_ref[1]
    low = core == 0
    own = own_ref[...].astype(F32)
    came = came_ref[...].astype(F32)
    first = jnp.where(low, own[vocab:], came[vocab:])
    second = jnp.where(low, came[vocab:], own[vocab:])
    scale, shift, stats = merged([from_parts(first, lanes), from_parts(second, lanes)])

    def scaled(value, k):
        a = jnp.where(low, scale[k], scale[1 - k])
        d = a * jnp.where(low, shift[k], shift[1 - k])
        top, plain = value[:vocab, :lanes], value[:vocab, lanes:]
        return jnp.concatenate([a * top + d * plain, a * plain], axis=1).astype(BF16)

    g = jnp.concatenate([scaled(own, 0), scaled(came, 1)], axis=0)
    ring, half, _ = s_own_ref.shape
    per = half // parts
    near = out_ref.shape[0] // parts
    last = out_ref.shape[1] - 16
    for k in range(ring):
        head = jnp.concatenate([s_own_ref[k], cross_ref[k, core]], axis=1)
        both = jnp.dot(head, g, preferred_element_type=F32).astype(BF16)
        start = k // near * per
        for q in range(parts):
            piece = both[q * per : (q + 1) * per]
            out_ref[q * near + k % near, start : start + per] = piece
    table = in_parts(stats, lanes)
    table = jnp.concatenate([table, table], axis=1).astype(BF16)
    for k in range(out_ref.shape[0]):
        out_ref[k, last:] = table


def third(info, own, came, s_own, cross, parts, near):
    ring, half, _ = s_own.shape
    deep = half // parts * (ring // near) + 16
    return pl.pallas_call(
        functools.partial(third_kernel, parts),
        out_shape=jax.ShapeDtypeStruct((parts * near, deep, own.shape[1]), BF16),
        in_specs=[SMEM] + [VMEM] * 4,
        out_specs=VMEM,
        compiler_params=PARAMS,
    )(info, own, came, s_own, cross.reshape(ring, 2, half, -1))


def spread_kernel(part_ref, place_ref, out_ref):
    lanes = part_ref.shape[2] // 2
    half = part_ref.shape[1] - 16
    count = part_ref.shape[0]
    slots = place_ref.shape[1]
    pad = out_ref.shape[1] // 2
    width = out_ref.shape[2]
    groups = slots // pad
    far = out_ref.shape[0] // groups
    per = half // far
    scale, shift, stats = merged(
        [from_parts(part_ref[k, half:].astype(F32), lanes) for k in range(count)]
    )
    a = jnp.zeros((half, lanes), F32)
    b = jnp.zeros((half, lanes), F32)
    for k in range(count):
        one = part_ref[k, :half].astype(F32)
        b_one = one[:, lanes:]
        a += scale[k] * one[:, :lanes] + (scale[k] * shift[k]) * b_one
        b += scale[k] * b_one
    rest = jnp.zeros((width - per - 16, lanes), F32)
    table = jnp.concatenate([in_parts(stats, lanes), rest], axis=0)
    tall = -(-lanes // 128) * 128
    pick = (place_ref[...] == iota((tall, slots), 0)).astype(F32).T[:, :lanes].astype(BF16)

    def found(value):
        pieces = []
        for k in range(far):
            pieces += [value[k * per : (k + 1) * per], table]
        return lax.dot_general(
            pick,
            jnp.concatenate(pieces, axis=0).astype(BF16),
            (((1,), (1,)), ((), ())),
            preferred_element_type=F32,
        )

    a, b = found(a), found(b)
    for k in range(far):
        both = [v[:, k * width : (k + 1) * width].reshape(groups, pad, width) for v in (a, b)]
        out_ref[k * groups : (k + 1) * groups] = jnp.concatenate(both, axis=1).astype(BF16)


def spread(parts, place, pad, far):
    groups = place.shape[1] // pad
    per = (parts.shape[1] - 16) // far
    width = -(-(per + 16) // 128) * 128
    return pl.pallas_call(
        spread_kernel,
        out_shape=jax.ShapeDtypeStruct((far * groups, 2 * pad, width), BF16),
        in_specs=[VMEM, VMEM],
        out_specs=VMEM,
        compiler_params=PARAMS,
    )(parts, place)


def finish_kernel(far, near, info_ref, part_ref, grad_ref, kl_ref):
    _, pad, width = grad_ref.shape
    per = width // near
    groups = part_ref.shape[0] // far
    share = groups // near

    def source(q):
        return [f * groups + q * share + k for f in range(far) for k in range(share)]

    wide = part_ref.shape[2]

    def moved(value, by):
        return pltpu.roll(value, by % wide, 1)

    tables = []
    for k in source(0):
        part = part_ref[k].astype(F32)[:pad]
        tables.append(part + moved(part, -1) + moved(part, -2))
    high = functools.reduce(jnp.maximum, tables)
    weight = [jnp.exp(v - high) for v in tables]
    total = functools.reduce(jnp.add, weight)
    weight = [w / total for w in weight]
    mean = functools.reduce(jnp.add, [moved(w, 3) * v for w, v in zip(weight, tables)])
    scale = [w[:, per : per + 1] for w in weight]
    shift = [(v - mean)[:, per + 3 : per + 4] for v in tables]
    lse = high + jnp.log(total)
    lse, t_lse, mean = lse[:, per : per + 1], lse[:, per + 6 : per + 7], mean[:, per + 3 : per + 4]
    pieces = []
    for q in range(near):
        grad = jnp.zeros((pad, part_ref.shape[2]), F32)
        for k, a, b in zip(source(q), scale, shift):
            part = part_ref[k].astype(F32)
            grad += a * (part[:pad] + b * part[pad:])
        pieces.append(grad[:, :per])
    grad_ref[0] = jnp.concatenate(pieces, axis=1).astype(BF16)
    kl = jnp.where(iota((pad, 1), 0) < info_ref[2], mean - lse + t_lse, 0.0)
    square = iota((pad, pad), 0) == iota((pad, pad), 1)
    kl_ref[...] = jnp.sum(jnp.where(square, kl, 0.0), axis=0, keepdims=True)


def finish(info, parts, width, far, near):
    pad = parts.shape[1] // 2
    return pl.pallas_call(
        functools.partial(finish_kernel, far, near),
        out_shape=[
            jax.ShapeDtypeStruct((1, pad, width), BF16),
            jax.ShapeDtypeStruct((1, pad), F32),
        ],
        in_specs=[SMEM, VMEM],
        out_specs=[VMEM, VMEM],
    )(info, parts)


def swap(value):
    return lax.ppermute(value, "c", ((0, 1), (1, 0)))


def some_rows(count, lanes, pad, t_width, width, operands):
    info, rows, t_place, s_place, teacher_head, student_head, cross = operands
    own = exchange(pack(rows, t_place, s_place, count, t_width, width, lax.axis_size(Y)), Y)
    other = swap(own)
    t, s, s_own, t_other, s_other = first(info, own, teacher_head, student_head)
    g = second(other, t, s, t_other, s_other, lanes)
    both = third(info, g, swap(g), s_own, cross, lax.axis_size("x"), lax.axis_size("yl"))
    return exchange(spread(exchange(both, NEAR), s_place, pad, lax.axis_size("yh")), REST)


def per_device(teacher_rows, student_rows, teacher_head, student_head, lengths, owner):
    groups = lax.axis_size(GRP)
    pad = student_rows.shape[1]
    t_width, s_width = teacher_rows.shape[2], student_rows.shape[2]
    group = lax.axis_index(GRP).astype(jnp.int32).reshape(1)
    core = lax.axis_index("c").astype(jnp.int32).reshape(1)
    mine = arrange(group, lengths, teacher_rows, student_rows, groups)
    t_place, s_place, info = routing(group, core, lengths, owner, groups * pad, pad)
    cross = swap(student_head)
    rows = exchange(mine, GRP).reshape(groups * pad, mine.shape[2])
    operands = (info, rows, t_place, s_place, teacher_head, student_head, cross)
    branches = [functools.partial(some_rows, *c, pad, t_width, t_width + s_width) for c in CAPACITIES]
    parts = lax.switch(info[0], branches, operands)
    grad, divergence = finish(info, parts, s_width, lax.axis_size("yh"), lax.axis_size("x"))
    return divergence, grad


def solution(mesh):
    torus = Mesh(mesh.devices.reshape(4, 8, 4, 2, 2), ("x", "z", "yh", "yl", "c"))
    return jax.shard_map(
        per_device,
        mesh=torus,
        in_specs=(
            P(GRP, None, VOCAB),
            P(GRP, None, VOCAB),
            P(None, (*GRP, *VOCAB)),
            P(None, (*GRP, *VOCAB)),
            P(),
            P(),
        ),
        out_specs=(P(GRP, None), P(GRP, None, VOCAB)),
        check_vma=False,
    )
```
